32 devices in a mesh: fsdp: 8 (over y, x, core), tensor: 4 (over z).
Axes of the slice: x: 2, y: 2, z: 4, core: 2. Of those that a mesh axis runs over, the one named last changes fastest.
Arguments:
- pixels: bfloat16 [32768, 768], P(('fsdp', 'tensor')), may hold values from -6 to 6
- segment: int32 [32768], P('fsdp'), may hold values from -1 to 4, as said below
- band_group: int32 [32768], P(('fsdp', 'tensor')), may hold values from 0 to 3, as said below
- scaled_position: int32 [32768], P(('fsdp', 'tensor')), may hold values from 0 to 390, as said below
- patch_weight: bfloat16 [4, 768, 1024], P(None, None, ('fsdp', 'tensor')), may hold values from -0.21875 to 0.21875
- patch_bias: bfloat16 [4, 1024], P(None, ('fsdp', 'tensor')), may hold values from -3 to 3
- norm_gains: bfloat16 [2, 1024], P(None, ('fsdp', 'tensor')), may hold values from 0.5 to 1.5
- vector_biases: bfloat16 [4, 1024], P(None, ('fsdp', 'tensor')), may hold values from -2 to 2
- attention_weight: bfloat16 [3, 1024, 1024], P(None, 'fsdp', 'tensor'), may hold values from -0.1875 to 0.1875
- query_value_bias: bfloat16 [2, 1024], P(None, ('tensor', 'fsdp')), may hold values from -2 to 2
- merge_weight: bfloat16 [1024, 1024], P('tensor', 'fsdp'), may hold values from -0.5 to 0.5
- expand_weight: bfloat16 [1024, 4096], P('fsdp', 'tensor'), may hold values from -0.1875 to 0.1875
- expand_bias: bfloat16 [4096], P(('tensor', 'fsdp')), may hold values from -3 to 3
- contract_weight: bfloat16 [4096, 1024], P('tensor', 'fsdp'), may hold values from -0.09375 to 0.09375
- cotangent: bfloat16 [32768, 1024], P(('fsdp', 'tensor')), may hold values from -6 to 6
Outputs:
- block_output: float32 [32768, 1024], P(('fsdp', 'tensor'))
- pixel_grad: float32 [32768, 768], P(('fsdp', 'tensor'))
- patch_weight_grad: float32 [4, 768, 1024], P(None, None, ('fsdp', 'tensor'))
- patch_bias_grad: float32 [4, 1024], P(None, ('fsdp', 'tensor'))
- norm_gains_grad: float32 [2, 1024], P(None, ('fsdp', 'tensor'))
- vector_biases_grad: float32 [4, 1024], P(None, ('fsdp', 'tensor'))
- attention_weight_grad: float32 [3, 1024, 1024], P(None, 'fsdp', 'tensor')
- query_value_bias_grad: float32 [2, 1024], P(None, ('tensor', 'fsdp'))
- merge_weight_grad: float32 [1024, 1024], P('tensor', 'fsdp')
- expand_weight_grad: float32 [1024, 4096], P('fsdp', 'tensor')
- expand_bias_grad: float32 [4096], P(('tensor', 'fsdp'))
- contract_weight_grad: float32 [4096, 1024], P('tensor', 'fsdp')
The draws below stay inside these ranges and needn't reach their ends.
Inputs may be any that keep to these rules, and one draw needn't show every extreme that they name: `segment`: rows of 1024 consecutive slots each hold whole items numbered 0, 1, ... from the row's start: a 13-band item fills 3 * 196 slots, an RGB item 196; -1 marks the padding after the row's last item. `band_group`: 0 on RGB items and padding; a 13-band item's three runs of 196 slots carry the groups 1, 2 and 3, one each, in some order. `scaled_position`: within each aligned block of 196 slots of an item, the slot's place in the run times a scale of 1 or 2 that is fixed for the item; 0 on padding.
All inputs are finite; a program needn't handle non-finite values.
Results may differ from the reference program's by a relative error of at most 0.019.
Values may be sent and summed in bfloat16 or wider, within the bound.
No kernel may reach another device: no remote copies, remote signals or barrier semaphores. Data moves between devices by JAX's collectives and lax.ppermute only.
A program may use at most 512 MiB of HBM per device.

```python
import math
import jax
import jax.numpy as jnp
from jax import lax

D = 1024
HEADS = 16
HEAD_DIM = 64
FF = 4096
PIX = 768
GROUPS = 4
PATCHES = 196
SLOTS = 1024
TOKENS = 32768


COMPOSITIONS = [[3, 1, 1, 0, 0], [1, 3, 1, 0, 0], [1, 1, 3, 0, 0], [1, 1, 1, 1, 1], [3, 1, 0, 0, 0], [1, 3, 0, 0, 0], [1, 1, 1, 0, 0]]


def packing(key):
    key = jax.random.fold_in(key, 101)
    table = jnp.array(COMPOSITIONS, dtype=jnp.int32)
    row_total = TOKENS // SLOTS
    pick_key, turn_key, scale_key = jax.random.split(key, 3)
    picks = jax.random.randint(pick_key, (row_total,), 0, table.shape[0])
    picks = picks.at[0].set(3).at[1].set(0)
    units = table[picks]
    ends = jnp.cumsum(units, axis=1)
    starts = ends - units
    slot_ids = jnp.arange(SLOTS, dtype=jnp.int32)
    unit_ids = (slot_ids // PATCHES)[None, :, None]
    inside = ((unit_ids >= starts[:, None, :]) & (unit_ids < ends[:, None, :])).astype(jnp.int32)
    live = jnp.sum(inside, axis=2) > 0
    item_ids = jnp.sum(inside * jnp.arange(5, dtype=jnp.int32)[None, None, :], axis=2)
    turns = jax.random.randint(turn_key, (row_total, 5), 0, 3)
    scales = jax.random.randint(scale_key, (row_total, 5), 1, 3).at[0, 0].set(2)

    def per_slot(values):
        return jnp.sum(inside * values[:, None, :], axis=2)
    offset_units = unit_ids[:, :, 0] - per_slot(starts)
    spectral_ids = 1 + (offset_units + per_slot(turns)) % 3
    band_ids = jnp.where(per_slot(units) == 3, spectral_ids, 0)
    position = jnp.where(live, (slot_ids % PATCHES)[None, :] * per_slot(scales), 0)
    segment_ids = jnp.where(live, item_ids, -1)
    return (segment_ids.reshape(-1).astype(jnp.int32), band_ids.reshape(-1).astype(jnp.int32), position.reshape(-1).astype(jnp.int32))


def draw_segment(key, part):
    return packing(key)[0]


def draw_band_group(key, part):
    return packing(key)[1]


def draw_scaled_position(key, part):
    return packing(key)[2]


def levels(rng, shape, cuts, least, top_value):
    factor_of = 1.0
    for dim, shards_of in cuts:
        steps = jax.random.uniform(jax.random.fold_in(jax.random.fold_in(rng, 6), dim), (shards_of,), jnp.float32, least / len(cuts), top_value / len(cuts))
        factor_of = factor_of * jnp.repeat(jnp.exp(steps), shape[dim] // shards_of).reshape((-1,) + (1,) * (len(shape) - 1 - dim))
    return factor_of


def bell_draw(stream_key, extent, spread, limit, cuts=(), held_as=jnp.bfloat16):
    entries = jax.random.normal(stream_key, extent, jnp.float32) * spread
    if len(cuts) > 0:
        entries = levels(stream_key, extent, cuts, -0.22, 0.18) * entries
    return jnp.clip(entries, min=-limit, max=limit).astype(held_as)


def setup_inputs(seed: int = 0) -> dict:
    splits = jax.random.split(jax.random.key(seed), 16)
    pixels = bell_draw(splits[0], (TOKENS, PIX), 1.0, 6.0, ((0, 32),))
    segment = draw_segment(jax.random.fold_in(splits[15], 71), 0)
    band_group = draw_band_group(jax.random.fold_in(splits[15], 71), 0)
    scaled_position = draw_scaled_position(jax.random.fold_in(splits[15], 71), 0)
    patch_weight = bell_draw(splits[4], (GROUPS, PIX, D), PIX ** -0.5, 0.21875, ((2, 32),))
    patch_bias = bell_draw(splits[5], (GROUPS, D), 0.5, 3.0, ((1, 32),))
    norm_gains = jnp.clip(1.0 + 0.1 * jax.random.normal(splits[6], (2, D), jnp.float32), 0.5, 1.5).astype(jnp.bfloat16)
    vector_biases = bell_draw(splits[7], (4, D), 0.3, 2.0, ((1, 32),))
    attention_weight = bell_draw(splits[8], (3, D, D), D ** -0.5, 0.1875, ((1, 8), (2, 4)))
    query_value_bias = bell_draw(splits[9], (2, D), 0.3, 2.0, ((1, 32),))
    merge_weight = bell_draw(splits[10], (D, D), (D // 8) ** -0.5, 0.5, ((0, 4), (1, 8)))
    expand_weight = bell_draw(splits[11], (D, FF), D ** -0.5, 0.1875, ((0, 8), (1, 4)))
    expand_bias = bell_draw(splits[12], (FF,), 0.5, 3.0, ((0, 32),))
    contract_weight = bell_draw(splits[13], (FF, D), FF ** -0.5, 0.09375, ((0, 4), (1, 8)))
    cotangent = bell_draw(splits[14], (TOKENS, D), 1.0, 6.0, ((0, 32),))
    return dict(pixels=pixels, segment=segment, band_group=band_group, scaled_position=scaled_position, patch_weight=patch_weight, patch_bias=patch_bias, norm_gains=norm_gains, vector_biases=vector_biases, attention_weight=attention_weight, query_value_bias=query_value_bias, merge_weight=merge_weight, expand_weight=expand_weight, expand_bias=expand_bias, contract_weight=contract_weight, cotangent=cotangent)


@jax.custom_vjp
def low(v):
    return lax.optimization_barrier(v.astype(jnp.bfloat16)).astype(jnp.float32)

@jax.custom_vjp
def low_back(v):
    return v

def low_keep(v):
    return (low(v), None)

def low_pass(kept, grad):
    return (grad,)

def back_keep(v):
    return (v, None)

def back_low(kept, grad):
    return (low(grad),)
low.defvjp(low_keep, low_pass)
low_back.defvjp(back_keep, back_low)
HIGHEST_PRECISION = lax.Precision.HIGHEST
EPSILON = 1e-06

def matmul_high(left, right):
    return jnp.dot(left, right, precision=HIGHEST_PRECISION)

def positions(index, model_width):
    half_width = model_width // 2
    rates = jnp.exp(jnp.arange(half_width).astype(jnp.float32) * (-math.log(10000.0) / half_width))
    angles = index.astype(jnp.float32)[:, None] * rates[None, :]
    return jnp.concatenate([jnp.sin(angles), jnp.cos(angles)], axis=1)

def layer_norm(values, gain, shift):
    row_mean = lax.optimization_barrier(jnp.mean(values, axis=-1, keepdims=True))
    centred = values - row_mean
    variance = lax.optimization_barrier(jnp.mean(centred * centred, axis=-1, keepdims=True))
    return centred * lax.rsqrt(variance + EPSILON) * gain + shift

def block_forward(params, pixels_f, segment, band_group, scaled_position):
    patch_weight, patch_bias, norm_gains, vector_biases, attention_weight, query_value_bias, merge_weight, expand_weight, expand_bias, contract_weight = params
    onehot = (band_group[:, None] == jnp.arange(GROUPS)[None, :]).astype(jnp.float32)
    embedded = onehot[:, 0:1] * matmul_high(pixels_f, patch_weight[0])
    for group_id in range(1, GROUPS):
        embedded = embedded + onehot[:, group_id:group_id + 1] * matmul_high(pixels_f, patch_weight[group_id])
    stream_zero = low_back(embedded) + matmul_high(onehot, patch_bias) + positions(scaled_position, D)
    input_one = low(layer_norm(stream_zero, norm_gains[0], vector_biases[0]))
    query_rows = low(low_back(matmul_high(input_one, attention_weight[0]) + query_value_bias[0]))
    key_rows = low(low_back(matmul_high(input_one, attention_weight[1])))
    value_rows = low(low_back(matmul_high(input_one, attention_weight[2]) + query_value_bias[1]))
    row_count = input_one.shape[0] // SLOTS

    def split_heads(table):
        return table.reshape(row_count, SLOTS, HEADS, HEAD_DIM)
    scores = jnp.einsum('rqhe,rkhe->rhqk', split_heads(query_rows), split_heads(key_rows), precision=HIGHEST_PRECISION) * HEAD_DIM ** (-0.5)
    scores = low_back(scores)
    item_ids = segment.reshape(row_count, 1, SLOTS)
    same_item = item_ids[:, :, :, None] == item_ids[:, :, None, :]
    scores = jnp.where(same_item, scores, -1e+30)
    row_max = lax.optimization_barrier(jnp.max(scores, axis=-1, keepdims=True))
    shifted = jnp.exp(scores - row_max)
    probabilities = low(shifted / lax.optimization_barrier(jnp.sum(shifted, axis=-1, keepdims=True)))
    attended = jnp.einsum('rhqk,rkhe->rqhe', probabilities, split_heads(value_rows), precision=HIGHEST_PRECISION).reshape(-1, D)
    attended = low(low_back(attended))
    stream_one = stream_zero + low_back(matmul_high(attended, merge_weight)) + vector_biases[1]
    input_two = low(layer_norm(stream_one, norm_gains[1], vector_biases[2]))
    hidden_pre = low_back(matmul_high(input_two, expand_weight) + expand_bias)
    activated = low(jax.nn.gelu(hidden_pre, approximate=False))
    return stream_one + low_back(matmul_high(activated, contract_weight)) + vector_biases[3]

def reference(pixels, segment, band_group, scaled_position, patch_weight, patch_bias, norm_gains, vector_biases, attention_weight, query_value_bias, merge_weight, expand_weight, expand_bias, contract_weight, cotangent):
    params = tuple((array.astype(jnp.float32) for array in (patch_weight, patch_bias, norm_gains, vector_biases, attention_weight, query_value_bias, merge_weight, expand_weight, expand_bias, contract_weight)))
    pixels_f = pixels.astype(jnp.float32)
    row_total = pixels.shape[0] // SLOTS
    block_rows = math.gcd(row_total, 2)
    block_count = row_total // block_rows
    block_step = jax.checkpoint(block_forward)

    def forward(weights, pixel_values):

        def scan_step(running, inputs):
            return (running, block_step(weights, inputs[0], inputs[1], inputs[2], inputs[3]))
        inputs = (pixel_values.reshape(block_count, block_rows * SLOTS, -1), segment.reshape(block_count, -1), band_group.reshape(block_count, -1), scaled_position.reshape(block_count, -1))
        running, outputs = lax.scan(scan_step, jnp.zeros((), jnp.float32), inputs)
        return outputs.reshape(-1, D)
    block_output, pullback = jax.vjp(forward, params, pixels_f)
    weight_grads, pixel_grad = pullback(cotangent.astype(jnp.float32))
    return (block_output, pixel_grad) + tuple(weight_grads)
```

```python
import math
from functools import partial

import jax
import jax.numpy as jnp
from jax import lax
from jax.experimental import pallas as pl
from jax.experimental.pallas import tpu as pltpu
from jax.sharding import PartitionSpec as P

HEAD_DIM = 64
GROUPS = 4
LANES = 128
TILE = 256
EPSILON = 1e-06
VMEM = 56 * 1024 * 1024
F32 = jnp.float32
BF16 = jnp.bfloat16
NN = (((1,), (0,)), ((), ()))
NT = (((1,), (1,)), ((), ()))
TN = (((0,), (0,)), ((), ()))
ANY = pl.BlockSpec(memory_space=pl.ANY)


def dot(left, right, dims=NN):
    return lax.dot_general(left, right, dims, preferred_element_type=F32)


def merged(block):
    return block.reshape(-1, block.shape[-1])


def normalize(values):
    row_mean = jnp.mean(values, axis=-1, keepdims=True)
    centred = values - row_mean
    inv_scale = lax.rsqrt(jnp.mean(centred * centred, axis=-1, keepdims=True) + EPSILON)
    return (centred * inv_scale, inv_scale)


def normalize_back(grad_normed, normed, inv_scale):
    return inv_scale * (
        grad_normed
        - jnp.mean(grad_normed, axis=-1, keepdims=True)
        - normed * jnp.mean(grad_normed * normed, axis=-1, keepdims=True)
    )


def whole(shape):
    return pl.BlockSpec(shape, lambda *_: (0,) * len(shape))


def row_tile(shape):
    return pl.BlockSpec((TILE,) + shape[1:], lambda i, *_: (i,) + (0,) * (len(shape) - 1))


def call(kernel, grid, in_specs, out_specs, out_shape, args, scratch=(), flops=0, exps=0, scalars=(), after=()):
    count = len(args)

    def with_waits(*refs):
        head = refs[: len(scalars) + count]
        return kernel(*head, *refs[len(scalars) + count + len(after) :])

    moved = sum(a.size * a.dtype.itemsize for a in args) + sum(math.prod(s.shape) * s.dtype.itemsize for s in out_shape)
    return pl.pallas_call(
        with_waits,
        grid_spec=pltpu.PrefetchScalarGridSpec(
            num_scalar_prefetch=len(scalars),
            grid=grid,
            in_specs=list(in_specs) + [ANY] * len(after),
            out_specs=list(out_specs),
            scratch_shapes=list(scratch),
        ),
        out_shape=list(out_shape),
        compiler_params=pltpu.CompilerParams(vmem_limit_bytes=VMEM),
        cost_estimate=pl.CostEstimate(flops=int(flops), bytes_accessed=int(moved), transcendentals=int(exps)),
    )(*scalars, *args, *after)


def shaped(shape, dtype):
    return jax.ShapeDtypeStruct(shape, dtype)


def split_kernel(core, array, out, *, wide):
    half = out.shape[1] // 2
    for place in range(half // wide):
        even = array[:, 2 * place * wide : (2 * place + 1) * wide]
        odd = array[:, (2 * place + 1) * wide : (2 * place + 2) * wide]
        at = place * wide
        out[:, at : at + wide] = jnp.where(core[0] == 0, even, odd)
        out[:, half + at : half + at + wide] = jnp.where(core[0] == 0, odd, even)


def split_columns(core, array, wide):
    tile = row_tile(array.shape)
    return call(
        partial(split_kernel, wide=wide),
        (array.shape[0] // TILE,),
        [tile],
        [tile],
        [shaped(array.shape, array.dtype)],
        (array,),
        scalars=(core,),
    )[0]


def output_kernel(core, stream, one, two, bias, out, *, wide):
    half = out.shape[1] // 2
    total = stream[...] + one[...] + two[...] + bias[...]
    if wide % LANES:
        out[...] = total
        return
    for place in range(half // wide):
        at = place * wide
        own, other = total[:, at : at + wide], total[:, half + at : half + at + wide]
        out[:, 2 * at : 2 * at + wide] = jnp.where(core[0] == 0, own, other)
        out[:, 2 * at + wide : 2 * at + 2 * wide] = jnp.where(core[0] == 0, other, own)


def output_rows(core, stream, one, two, bias, wide, after=()):
    tile = row_tile(stream.shape)
    return call(
        partial(output_kernel, wide=wide),
        (stream.shape[0] // TILE,),
        [tile] * 3 + [whole(bias.shape)],
        [tile],
        [shaped(stream.shape, F32)],
        (stream, one, two, bias),
        scalars=(core,),
        after=after,
    )[0]


def finish_feed_kernel(low, high, expand, contract):
    part = low.shape[2]
    for at, ref in ((0, low), (part, high)):
        expand[:, at : at + part] = ref[0].astype(F32)
        contract[at : at + part, :] = ref[1].astype(F32).T


def finish_feed(low, high):
    _, wide, part = low.shape
    return call(
        finish_feed_kernel,
        (1,),
        [whole(low.shape)] * 2,
        [whole((wide, 2 * part)), whole((2 * part, wide))],
        [shaped((wide, 2 * part), F32), shaped((2 * part, wide), F32)],
        (low, high),
    )


def finish_attention_kernel(blocks, attention, merge_out):
    attention[...] = blocks[:3].astype(F32)
    merge_out[...] = blocks[3].astype(F32).T


def finish_attention(blocks):
    _, wide, columns = blocks.shape
    return call(
        finish_attention_kernel,
        (1,),
        [whole(blocks.shape)],
        [whole((3, wide, columns)), whole((columns, wide))],
        [shaped((3, wide, columns), F32), shaped((columns, wide), F32)],
        (blocks,),
    )


def group_rows(band, group, values):
    return jnp.where(band == group, values, jnp.zeros_like(values))


def embed_kernel(present, pix, band, table, bias, gain, shift, lo_own, lo_came, hi_own, hi_came, stream, normed, acc):
    tile = pl.program_id(0)
    half = acc.shape[1] // 2
    width = pix.shape[1]
    acc[...] = table[...]
    for group in range(GROUPS):

        @pl.when(present[tile * GROUPS + group] > 0)
        def _():
            rows = group_rows(band[...], group, pix[...])
            at = pl.ds((group % 2) * width, width)
            own, came = (lo_own, lo_came) if group < 2 else (hi_own, hi_came)
            acc[:, :half] += dot(rows, merged(own[:, :, at]), NT)
            acc[:, half:] += dot(rows, merged(came[:, :, at]), NT)

    total = acc[...]
    for group in range(GROUPS):
        total = total + jnp.where(band[...] == group, bias[group : group + 1, :], 0.0)
    stream[...] = total
    normed[...] = (normalize(total)[0] * gain[...] + shift[...]).astype(BF16)


def embed(present, pixels, band, table, bias, gain, shift, patches, after=()):
    rows, model = table.shape
    args = (pixels, band, table, bias, gain, shift) + patches
    specs = [row_tile(pixels.shape), row_tile(band.shape), row_tile(table.shape)] + [whole(a.shape) for a in args[3:]]
    return call(
        embed_kernel,
        (rows // TILE,),
        specs,
        [row_tile((rows, model))] * 2,
        [shaped((rows, model), F32), shaped((rows, model), BF16)],
        args,
        scratch=[pltpu.VMEM((TILE, model), F32)],
        flops=4 * rows * pixels.shape[1] * model,
        scalars=(present,),
        after=after,
    )


def project_kernel(x, qk_own, qk_came, vm_own, vm_came, bias, query, key, value):
    half = x.shape[1] // 2
    kept, other = x[:, :half], x[:, half:]

    def product(own, came, which):
        return dot(kept, merged(own[which])) + dot(other, merged(came[which]))

    query[...] = (product(qk_own, qk_came, 0) + bias[0:1, :]).astype(BF16)
    key[...] = product(qk_own, qk_came, 1).astype(BF16)
    value[...] = (product(vm_own, vm_came, 0) + bias[1:2, :]).astype(BF16)


def project(x, qk, vm, bias, after=()):
    rows, model = x.shape
    columns = min(256, model)
    weight = lambda a: pl.BlockSpec(a.shape[:-1] + (columns,), lambda i: (0, 0, 0, i))
    first = lambda a: pl.BlockSpec((1,) + a.shape[1:-1] + (columns,), lambda i: (0, 0, 0, i))
    return call(
        project_kernel,
        (model // columns,),
        [whole(x.shape)] + [weight(a) for a in qk] + [first(a) for a in vm] + [pl.BlockSpec((2, columns), lambda i: (0, i))],
        [pl.BlockSpec((rows, columns), lambda i: (0, i))] * 3,
        [shaped((rows, model), BF16)] * 3,
        (x,) + qk + vm + (bias,),
        flops=6 * rows * model * model,
        after=after,
    )


def head_mask(shape, head):
    lane = lax.broadcasted_iota(jnp.int32, shape, 1)
    return (lane < HEAD_DIM) if head == 0 else (lane >= HEAD_DIM)


def only_head(values, head):
    return jnp.where(head_mask(values.shape, head), values, jnp.zeros_like(values))


def attend_kernel(q_ref, k_ref, v_ref, seg_col_ref, seg_row_ref, out_ref, log_ref, bias_ref):
    pair = pl.program_id(0)
    rows = q_ref.shape[0]

    @pl.when(pair == 0)
    def _():
        bias_ref[...] = jnp.where(seg_col_ref[...] == seg_row_ref[...], 0.0, -1e30).astype(F32)
        log_ref[...] = jnp.zeros_like(log_ref)

    keys = k_ref[...]
    value_of = [only_head(v_ref[...], head) for head in range(2)]
    for start in range(0, rows, TILE):
        at = pl.ds(start, TILE)
        query = q_ref[at, :] * jnp.asarray(HEAD_DIM ** (-0.5), BF16)
        lane = lax.broadcasted_iota(jnp.int32, (TILE, LANES), 1)
        logs = log_ref[at, :]
        total = jnp.zeros((TILE, LANES), F32)
        for head in range(2):
            scores = dot(only_head(query, head), keys, NT) + bias_ref[at, :]
            top = jnp.max(scores, axis=1, keepdims=True)
            shifted = jnp.exp(scores - top)
            mass = jnp.sum(shifted, axis=1, keepdims=True)
            total = total + dot(shifted.astype(BF16), value_of[head]) * (1.0 / mass)
            logs = jnp.where(lane == 2 * pair + head, top + jnp.log(mass), logs)
        out_ref[at, :] = total.astype(BF16)
        log_ref[at, :] = logs


def attend(query, key, value, segment, after=()):
    rows, width = query.shape
    block = pl.BlockSpec((rows, LANES), lambda i: (0, i))
    return call(
        attend_kernel,
        (width // LANES,),
        [block, block, block, whole((rows, 1)), whole((1, rows))],
        [block, whole((rows, LANES))],
        [shaped((rows, width), BF16), shaped((rows, LANES), F32)],
        (query, key, value, segment[:, None], segment[None, :]),
        scratch=[pltpu.VMEM((rows, rows), F32)],
        flops=16 * rows * rows * width,
        exps=rows * rows * width // HEAD_DIM,
        after=after,
    )


def attend_back_kernel(
    q_ref, k_ref, v_ref, g_ref, seg_col_ref, seg_row_ref, log_ref, delta_ref, dq_ref, dk_ref, dv_ref, sum_ref, bias_ref, acc_ref, *, base
):
    pair = base + pl.program_id(0)
    rows = q_ref.shape[0]

    @pl.when(pl.program_id(0) == 0)
    def _():
        bias_ref[...] = jnp.where(seg_col_ref[...] == seg_row_ref[...], 0.0, -1e30).astype(F32)

    query = q_ref[...] * jnp.asarray(HEAD_DIM ** (-0.5), BF16)
    grads = g_ref[...]
    query_of = [only_head(query, head) for head in range(2)]
    grads_of = [only_head(grads, head) for head in range(2)]
    acc_ref[...] = jnp.zeros_like(acc_ref)
    value_sum = jnp.zeros((1, LANES), F32)
    for start in range(0, rows, TILE):
        at = pl.ds(start, TILE)
        keys = k_ref[at, :]
        values = v_ref[at, :]
        grad_key = jnp.zeros((TILE, LANES), F32)
        grad_value = jnp.zeros((TILE, LANES), F32)
        for head in range(2):
            key_h = only_head(keys, head)
            log_row = log_ref[pl.ds(2 * pair + head, 1), :]
            delta_row = delta_ref[pl.ds(2 * pair + head, 1), :]
            scores = dot(key_h, query, NT) + bias_ref[at, :]
            probs = jnp.exp(scores - log_row)
            grad_value = grad_value + dot(probs.astype(BF16), grads_of[head])
            grad_probs = dot(only_head(values, head), grads, NT)
            grad_scores = (probs * (grad_probs - delta_row)).astype(BF16)
            grad_key = grad_key + dot(grad_scores, query_of[head])
            acc_ref[...] += dot(key_h, grad_scores, TN)
        grad_value = grad_value.astype(BF16)
        dk_ref[at, :] = grad_key.astype(BF16)
        dv_ref[at, :] = grad_value
        value_sum = value_sum + jnp.sum(grad_value.astype(F32), axis=0, keepdims=True)
    grad_query = (acc_ref[...].T * HEAD_DIM ** (-0.5)).astype(BF16)
    dq_ref[...] = grad_query
    sum_ref[0:1, :] = jnp.sum(grad_query.astype(F32), axis=0, keepdims=True)
    sum_ref[1:2, :] = value_sum


def attend_back(query, key, value, grads, segment, log_rows, delta_rows, base, pairs, after=()):
    rows = query.shape[0]
    width = pairs * LANES
    taken = pl.BlockSpec((rows, LANES), lambda i: (0, base + i))
    given = pl.BlockSpec((rows, LANES), lambda i: (0, i))
    return call(
        partial(attend_back_kernel, base=base),
        (pairs,),
        [taken] * 4 + [whole((rows, 1)), whole((1, rows)), whole(log_rows.shape), whole(delta_rows.shape)],
        [given] * 3 + [pl.BlockSpec((2, LANES), lambda i: (0, i))],
        [shaped((rows, width), BF16)] * 3 + [shaped((2, width), F32)],
        (query, key, value, grads, segment[:, None], segment[None, :], log_rows, delta_rows),
        scratch=[pltpu.VMEM((rows, rows), F32), pltpu.VMEM((LANES, rows), F32)],
        flops=40 * rows * rows * width,
        exps=rows * rows * width // HEAD_DIM,
        after=after,
    )


def merge_kernel(attended, stream, bias, gain, shift, own, came, stream_one, normed):
    half = stream.shape[1] // 2
    stream_one[:, :half] = stream[:, :half] + dot(attended[...], merged(own[0]), NT)
    stream_one[:, half:] = stream[:, half:] + dot(attended[...], merged(came[0]), NT)
    total = stream_one[...] + bias[...]
    stream_one[...] = total
    normed[...] = (normalize(total)[0] * gain[...] + shift[...]).astype(BF16)


def second(array):
    return pl.BlockSpec((1,) + array.shape[1:], lambda *_: (1,) + (0,) * (array.ndim - 1))


def merge(attended, stream, bias, gain, shift, vm, after=()):
    rows, model = stream.shape
    return call(
        merge_kernel,
        (rows // TILE,),
        [row_tile(attended.shape), row_tile(stream.shape)] + [whole((1, model))] * 3 + [second(a) for a in vm],
        [row_tile((rows, model))] * 2,
        [shaped((rows, model), F32), shaped((rows, model), BF16)],
        (attended, stream, bias, gain, shift) + vm,
        flops=2 * rows * model * model,
        after=after,
    )


def gelu_parts(hidden):
    t = 1.0 / (1.0 + (0.3275911 * math.sqrt(0.5)) * jnp.abs(hidden))
    bell = jnp.exp(-0.5 * hidden * hidden)
    poly = t * (
        0.5 * 0.254829592
        + t * (-0.5 * 0.284496736 + t * (0.5 * 1.421413741 + t * (-0.5 * 1.453152027 + t * (0.5 * 1.061405429))))
    )
    tail = poly * bell
    below = jnp.where(hidden >= 0, 1.0 - tail, tail)
    return hidden * below, below + (hidden * (1.0 / math.sqrt(2.0 * math.pi))) * bell


def feed_kernel(
    core, x_ref, g_ref, e_own, e_other, c_own, c_other, b_ref, y_ref, d_ref, keep_ref, send_ref, db_ref, xt_ref, gt_ref, a_ref, h_ref
):
    step = pl.program_id(0)
    rows, model = x_ref.shape
    half = model // 2

    @pl.when(step == 0)
    def _():
        xt_ref[...] = x_ref[...].T
        gt_ref[...] = g_ref[...].T
        y_ref[...] = jnp.zeros_like(y_ref)
        d_ref[...] = jnp.zeros_like(d_ref)

    expand = (merged(e_own[...]), merged(e_other[...]))
    contract = (merged(c_own[...]), merged(c_other[...]))
    sums = jnp.zeros((1, h_ref.shape[1]), F32)
    for start in range(0, rows, TILE):
        at = pl.ds(start, TILE)
        hidden = dot(x_ref[at, :half], expand[0]) + dot(x_ref[at, half:], expand[1]) + b_ref[0]
        grad_active = dot(g_ref[at, :half], contract[0]) + dot(g_ref[at, half:], contract[1])
        active, slope = gelu_parts(hidden)
        active = active.astype(BF16)
        grad_hidden = (grad_active * slope).astype(BF16)
        a_ref[at, :] = active
        h_ref[at, :] = grad_hidden
        sums = sums + jnp.sum(grad_hidden.astype(F32), axis=0, keepdims=True)
        for side in range(2):
            cols = pl.ds(side * half, half)
            y_ref[at, cols] += dot(active, contract[side], NT)
            d_ref[at, cols] += dot(grad_hidden, expand[side], NT)
    db_ref[0] = sums
    for side, ref in ((0, keep_ref), (1, send_ref)):
        cols = pl.ds(side * half, half)
        shape = ref.shape[:1] + ref.shape[3:]
        ref[:, 0, 0] = dot(xt_ref[cols, :], h_ref[...]).astype(BF16).reshape(shape)
        ref[:, 0, 1] = dot(gt_ref[cols, :], a_ref[...]).astype(BF16).reshape(shape)


def feed(core, rows_two, cotangent, weights, bias, which, after=()):
    rows, model = rows_two.shape
    pairs, _, steps, _, wide, unit = weights.shape
    part = unit // 2
    block = (pairs, 1, 1, 1, wide, part)
    weight = lambda side, mat: pl.BlockSpec(
        block, lambda i, core: (0, core[0] if side == 0 else 1 - core[0], i, mat, 0, which)
    )
    grad = pl.BlockSpec((pairs, 1, 2, wide, part), lambda i, core: (0, i, 0, 0, 0))
    return call(
        feed_kernel,
        (steps,),
        [whole((rows, model))] * 2
        + [weight(0, 0), weight(1, 0), weight(0, 1), weight(1, 1)]
        + [pl.BlockSpec((1, 1, part), lambda i, core: (i, 0, 0))],
        [whole((rows, model))] * 2 + [grad, grad, pl.BlockSpec((1, 1, part), lambda i, core: (i, 0, 0))],
        [shaped((rows, model), F32)] * 2
        + [shaped((pairs, steps, 2, wide, part), BF16)] * 2
        + [shaped((steps, 1, part), F32)],
        (rows_two, cotangent, weights, weights, weights, weights, bias),
        scratch=[
            pltpu.VMEM((model, rows), BF16),
            pltpu.VMEM((model, rows), BF16),
            pltpu.VMEM((rows, part), BF16),
            pltpu.VMEM((rows, part), BF16),
        ],
        flops=12 * rows * model * part * steps,
        exps=rows * part * steps,
        scalars=(core,),
        after=after,
    )


def merge_back_kernel(
    d_one, d_two, top, stream_one, attended, gain, own, came, heads, grad_stream, grad_branch, grad_attended, delta, sums
):
    half = top.shape[1] // 2
    grad_two = d_one[...] + d_two[...]
    normed, scale = normalize(stream_one[...])
    cotangent = top[...].astype(F32)
    total = cotangent + normalize_back(grad_two * gain[...], normed, scale)
    grad_stream[...] = total
    low = total.astype(BF16)
    grad_branch[...] = low
    grads = (dot(low[:, :half], merged(own[0])) + dot(low[:, half:], merged(came[0]))).astype(BF16)
    grad_attended[...] = grads
    both = grads.astype(F32) * attended[...].astype(F32)
    delta[...] = lax.dot_general(heads[...], both, NT, precision=lax.Precision.HIGHEST, preferred_element_type=F32)

    @pl.when(pl.program_id(0) == 0)
    def _():
        sums[...] = jnp.zeros_like(sums)

    for row, part in enumerate((grad_two * normed, grad_two, total, cotangent)):
        sums[row : row + 1, :] += jnp.sum(part, axis=0, keepdims=True)


def merge_back(d_one, d_two, top, stream_one, attended, gain, vm, heads, after=()):
    rows, model = stream_one.shape
    tile = row_tile((rows, model))
    return call(
        merge_back_kernel,
        (rows // TILE,),
        [tile] * 5 + [whole((1, model))] + [second(a) for a in vm] + [whole(heads.shape)],
        [tile] * 3 + [pl.BlockSpec((heads.shape[0], TILE), lambda i: (0, i)), whole((8, model))],
        [
            shaped((rows, model), F32),
            shaped((rows, model), BF16),
            shaped((rows, model), BF16),
            shaped((heads.shape[0], rows), F32),
            shaped((8, model), F32),
        ],
        (d_one, d_two, top, stream_one, attended, gain) + vm + (heads,),
        flops=2 * rows * model * model,
        after=after,
    )


def attention_grads_kernel(x, branch, query, key, value, attended, keep, send, xt, bt):
    half = xt.shape[0] // 2

    @pl.when(pl.program_id(0) == 0)
    def _():
        xt[...] = x[...].T
        bt[...] = branch[...].T

    pairs, blocks, _, wide, columns = keep.shape
    for side, ref in ((0, keep), (1, send)):
        at = pl.ds(side * half, half)
        for place, (left, right) in enumerate(((xt, query), (xt, key), (xt, value), (bt, attended))):
            grad = dot(left[at, :], right[...]).astype(BF16)
            for block in range(blocks):
                part = grad[:, block * columns : (block + 1) * columns]
                ref[:, block, place] = part.reshape(pairs, wide, columns)


def attention_grads(x, branch, query, key, value, attended, pairs, steps, base, columns, after=()):
    rows, model = x.shape
    wide = model // (2 * pairs)
    blocks = max(1, LANES // columns)
    column = pl.BlockSpec((rows, blocks * columns), lambda i: (0, i))
    shifted = pl.BlockSpec((rows, blocks * columns), lambda i: (0, base // blocks + i))
    grad = pl.BlockSpec((pairs, blocks, 4, wide, columns), lambda i: (0, i, 0, 0, 0))
    return call(
        attention_grads_kernel,
        (steps // blocks,),
        [whole(x.shape)] * 2 + [column] * 3 + [shifted],
        [grad] * 2,
        [shaped((pairs, steps, 4, wide, columns), BF16)] * 2,
        (x, branch, query, key, value, attended),
        scratch=[pltpu.VMEM((model, rows), BF16)] * 2,
        flops=8 * rows * model * columns * steps,
        after=after,
    )


def project_back_kernel(
    query, key, value, grad_stream, stream, band, gain, qk_own, qk_came, vm_own, vm_came, grad_embed, sums, acc
):
    half = stream.shape[1] // 2
    for side, (qk, vm) in enumerate(((qk_own, vm_own), (qk_came, vm_came))):
        acc[:, side * half : (side + 1) * half] = (
            dot(query[...], merged(qk[0]), NT) + dot(key[...], merged(qk[1]), NT) + dot(value[...], merged(vm[0]), NT)
        )
    grad_one = acc[...]
    normed, scale = normalize(stream[...])
    total = grad_stream[...] + normalize_back(grad_one * gain[...], normed, scale)
    grad_embed[...] = total.astype(BF16)

    @pl.when(pl.program_id(0) == 0)
    def _():
        sums[...] = jnp.zeros_like(sums)

    parts = [group_rows(band[...], group, total) for group in range(GROUPS)] + [grad_one * normed, grad_one]
    for row, part in enumerate(parts):
        sums[row : row + 1, :] += jnp.sum(part, axis=0, keepdims=True)


def project_back(query, key, value, grad_stream, stream, band, gain, qk, vm, after=()):
    rows, model = stream.shape
    tile = row_tile((rows, model))
    first = lambda a: pl.BlockSpec((1,) + a.shape[1:], lambda i: (0, 0, 0, 0))
    return call(
        project_back_kernel,
        (rows // TILE,),
        [tile] * 5 + [row_tile(band.shape), whole((1, model))] + [whole(a.shape) for a in qk] + [first(a) for a in vm],
        [tile, whole((8, model))],
        [shaped((rows, model), BF16), shaped((8, model), F32)],
        (query, key, value, grad_stream, stream, band, gain) + qk + vm,
        scratch=[pltpu.VMEM((TILE, model), F32)],
        flops=6 * rows * model * model,
        after=after,
    )


def patch_grads_kernel(present, grads, pix, band, keep, send, gt, acc, *, base):
    group = base + pl.program_id(0)
    half = gt.shape[0] // 2

    @pl.when(pl.program_id(0) == 0)
    def _():
        gt[...] = grads[...].T

    acc[...] = jnp.zeros_like(acc)
    for tile in range(pix.shape[0] // TILE):

        @pl.when(present[tile * GROUPS + group] > 0)
        def _():
            at = pl.ds(tile * TILE, TILE)
            acc[...] += dot(gt[:, at], group_rows(band[at, :], group, pix[at, :]))

    keep[...] = acc[:half, :].astype(BF16)
    send[...] = acc[half:, :].astype(BF16)


def patch_grads(present, grads, pixels, band, base, after=()):
    rows, model = grads.shape
    width = pixels.shape[1]
    count = GROUPS // 2
    given = pl.BlockSpec((model // 2, width), lambda i, present: (0, i))
    return call(
        partial(patch_grads_kernel, base=base),
        (count,),
        [whole(grads.shape), whole(pixels.shape), whole(band.shape)],
        [given] * 2,
        [shaped((model // 2, count * width), BF16)] * 2,
        (grads, pixels, band),
        scratch=[pltpu.VMEM((model, rows), BF16), pltpu.VMEM((model, width), F32)],
        flops=2 * rows * width * model,
        scalars=(present,),
        after=after,
    )


def pixel_grads_kernel(present, grads, band, lo_own, lo_came, hi_own, hi_came, out):
    tile = pl.program_id(0)
    half = grads.shape[1] // 2
    width = out.shape[1]
    out[...] = jnp.zeros_like(out)
    for group in range(GROUPS):

        @pl.when(present[tile * GROUPS + group] > 0)
        def _():
            at = pl.ds((group % 2) * width, width)
            own, came = (lo_own, lo_came) if group < 2 else (hi_own, hi_came)
            spread = dot(grads[:, :half], merged(own[:, :, at])) + dot(grads[:, half:], merged(came[:, :, at]))
            out[...] = jnp.where(band[...] == group, spread, out[...])


def pixel_grads(present, grads, band, patches, width, after=()):
    rows, model = grads.shape
    return call(
        pixel_grads_kernel,
        (rows // TILE,),
        [row_tile(grads.shape), row_tile(band.shape)] + [whole(a.shape) for a in patches],
        [row_tile((rows, width))],
        [shaped((rows, width), F32)],
        (grads, band) + patches,
        flops=4 * rows * width * model,
        scalars=(present,),
        after=after,
    )[0]


def make_body(fsdp, tensor):
    pairs = fsdp // 2
    t_bits = list(range(tensor.bit_length() - 1))
    f_bits = list(range(1, fsdp.bit_length() - 1))
    up, down = f_bits, f_bits[::-1]

    def swap(array, axis, bit):
        size = fsdp if axis == "fsdp" else tensor
        return lax.ppermute(array, axis, [(i, i ^ (1 << bit)) for i in range(size)])

    def body(
        pixels,
        segment,
        band_group,
        scaled_position,
        patch_weight,
        patch_bias,
        norm_gains,
        vector_biases,
        attention_weight,
        query_value_bias,
        merge_weight,
        expand_weight,
        expand_bias,
        contract_weight,
        cotangent,
    ):
        index = {"fsdp": lax.axis_index("fsdp"), "tensor": lax.axis_index("tensor")}
        core = index["fsdp"] & 1
        rows, pix = pixels.shape
        model = cotangent.shape[1]
        thin = patch_bias.shape[1]
        wide = model // fsdp
        unit = expand_weight.shape[1]
        half_unit = unit // 2
        segment = lax.dynamic_slice_in_dim(segment, index["tensor"] * rows, rows)

        def grow(array, axis, bit, dim):
            came = swap(array, axis, bit)
            mine = ((index[axis] >> bit) & 1) == 1
            return jnp.where(
                mine, jnp.concatenate([came, array], axis=dim), jnp.concatenate([array, came], axis=dim)
            )

        def spread(array, order):
            lead = array.shape[:-2]
            array = array.reshape(lead + (1,) * len(f_bits) + array.shape[-2:])
            for bit in order:
                array = grow(array, "fsdp", bit, len(lead) + len(f_bits) - bit)
            array = array.reshape(lead + (pairs,) + array.shape[-2:])
            return array, swap(array, "fsdp", 0)

        def first_swap(send):
            return swap(send, "fsdp", 0)

        def next_swap(keep, came, bit):
            dim = len(f_bits) - bit
            mine = (index["fsdp"] >> bit) & 1
            take = lambda array, at: lax.dynamic_slice_in_dim(array, at, 1, axis=dim)
            both = lambda at: (take(keep, at).astype(F32) + take(came, at).astype(F32)).astype(keep.dtype)
            return both(mine), swap(both(1 - mine), "fsdp", bit)

        def unfold(array):
            return array.reshape((2,) * len(f_bits) + array.shape[1:])

        def last_sum(keep, came):
            rest = keep.shape[len(f_bits) :]
            return (keep.astype(F32) + came.astype(F32)).astype(keep.dtype).reshape(rest)

        def over_tensor(blocks):
            return lax.psum_scatter(blocks, "tensor", scatter_dimension=0, tiled=False)

        def to_split(array):
            parts = array.reshape(array.shape[0], pairs, 2, wide)
            even, odd = (parts[:, :, i].reshape(array.shape[0], -1) for i in range(2))
            return jnp.where(core == 0, jnp.concatenate([even, odd], axis=1), jnp.concatenate([odd, even], axis=1))

        def from_split(array):
            parts = array.reshape(array.shape[0], 2, pairs, wide)
            mine, other = parts[:, 0], parts[:, 1]
            parts = jnp.where(core == 0, jnp.stack([mine, other], axis=2), jnp.stack([other, mine], axis=2))
            return parts.reshape(array.shape)

        tie = lambda array, *others: lax.optimization_barrier((array,) + others)[0]
        core_at = core[None].astype(jnp.int32)
        aligned = wide % LANES == 0

        both = jnp.stack([expand_weight, contract_weight.T])
        feed_weights = lax.all_gather(both, ("fsdp", "tensor"), axis=0, tiled=False)
        feed_weights = feed_weights.reshape(pairs, 2, tensor, 2, wide, unit)

        patch = patch_weight.reshape(-1, thin).T
        for bit in t_bits:
            patch = grow(patch, "tensor", bit, 0)
        columns = (GROUPS // 2) * pix
        patch_lo = spread(patch[:, :columns], up)
        patch_hi = spread(patch[:, columns:], down)
        patches = patch_lo + patch_hi

        small = jnp.concatenate(
            [patch_bias.reshape(-1), norm_gains.reshape(-1), vector_biases.reshape(-1), query_value_bias.reshape(-1), expand_bias]
        )[None, :]
        small = tie(small, patch)
        for bit in t_bits:
            small = grow(small, "tensor", bit, 0)
        for bit in range(len(f_bits) + 1):
            small = grow(small, "fsdp", bit, 0)
        n_vec = GROUPS + 2 + 4
        cut = n_vec * thin
        small = small.astype(F32)
        vectors = small[:, :cut].reshape(fsdp * tensor, n_vec, thin).transpose(1, 0, 2).reshape(n_vec, model)
        vectors = to_split(vectors)
        patch_bias_rows = vectors[:GROUPS]
        gains = [vectors[GROUPS + i : GROUPS + i + 1] for i in range(2)]
        biases = [vectors[GROUPS + 2 + i : GROUPS + 3 + i] for i in range(4)]
        by_hidden = small[:, cut:].reshape(fsdp, tensor, -1).transpose(1, 0, 2)
        qv_rows = by_hidden[:, :, : 2 * thin].reshape(fsdp * tensor, 2, thin).transpose(1, 0, 2).reshape(2, model)
        unit_bias = by_hidden[:, :, 2 * thin :].reshape(tensor, 2, 1, half_unit)

        attention = jnp.concatenate([attention_weight, merge_weight.T[None]], axis=0)
        attention = tie(attention, patch)
        for bit in t_bits:
            attention = grow(attention, "tensor", bit, 2)
        qk = spread(attention[:2], up)
        vm = spread(attention[2:], down)

        band = band_group[:, None]
        present = jnp.any(band_group.reshape(-1, TILE, 1) == jnp.arange(GROUPS), axis=1).astype(jnp.int32).reshape(-1)
        half_width = model // 2
        column = jnp.arange(model)
        place = column % half_width
        natural = (2 * (place // wide) + (core ^ (column // half_width))) * wide + place % wide
        rates = jnp.exp((natural % half_width).astype(F32) * (-math.log(10000.0) / half_width))
        angles = scaled_position.astype(F32)[:, None] * rates[None, :]
        quarter = model // 4
        table = jnp.concatenate(
            [
                f(angles[:, i * quarter : (i + 1) * quarter])
                for i, f in enumerate((jnp.sin, jnp.cos, jnp.sin, jnp.cos))
            ],
            axis=1,
        )
        top = split_columns(core_at, cotangent, wide) if aligned else to_split(cotangent)
        stream_zero, input_one = embed(present, pixels, band, table, patch_bias_rows, gains[0], biases[0], patches)

        query, key, value = project(input_one, qk, vm, qv_rows)
        attended, logs = attend(query, key, value, segment)
        stream_one, input_two = merge(attended, stream_zero, biases[1], gains[1], biases[2], vm)

        y_low, d_low, keep_low, send_low, units_low = feed(core_at, input_two, top, feed_weights, unit_bias[:, 0], 0)
        came_low = first_swap(send_low)
        y_high, d_high, keep_high, send_high, units_high = feed(core_at, input_two, top, feed_weights, unit_bias[:, 1], 1)
        unit_grads = [units_low, units_high]

        heads = model // HEAD_DIM
        head_rows = (jnp.arange(heads)[:, None] == jnp.arange(model)[None, :] // HEAD_DIM).astype(F32)
        came_high = first_swap(send_high)
        grad_stream_one, grad_branch, grad_attended, delta, sums_two = merge_back(
            d_low, d_high, top, stream_one, attended, gains[1], vm, head_rows, after=(came_low,)
        )
        log_rows = logs[:, :heads].T
        all_pairs = model // LANES
        calls = 4
        each = all_pairs // calls
        back = lambda i, after: attend_back(
            query, key, value, grad_attended, segment, log_rows, delta, i * each, each, after=after
        )
        half_columns = 2 * each * LANES
        per_call = tensor // 2

        def grads_of(two, base, after):
            q, k, v = (jnp.concatenate([p[i] for p in two], axis=1) for i in range(3))
            return (q, k, v), attention_grads(
                input_one, grad_branch, q, k, v, attended, pairs, per_call, base, half_columns // per_call, after=after
            )

        keep_low, came_low = next_swap(unfold(keep_low), unfold(came_low), down[0])
        first = back(0, (came_high,))
        keep_high, came_high = next_swap(unfold(keep_high), unfold(came_high), up[0])
        second_part = back(1, ())
        left, (keep_left, send_left) = grads_of((first, second_part), 0, (came_low,))
        came_left = first_swap(send_left)
        if len(f_bits) > 1:
            keep_low, came_low = next_swap(keep_low, came_low, down[1])
        third = back(2, ())
        fourth = back(3, (came_high, came_left))
        keep_left, came_left = next_swap(unfold(keep_left), unfold(came_left), up[0])
        if len(f_bits) > 1:
            keep_high, came_high = next_swap(keep_high, came_high, up[1])
        right, (keep_right, send_right) = grads_of((third, fourth), per_call, (came_low,))
        came_right = first_swap(send_right)
        for bit in down[2:]:
            keep_low, came_low = next_swap(keep_low, came_low, bit)
        for bit in up[2:]:
            keep_high, came_high = next_swap(keep_high, came_high, bit)
        feed_low = over_tensor(last_sum(keep_low, came_low))
        feed_high = over_tensor(last_sum(keep_high, came_high))
        expand_out, contract_out = finish_feed(feed_low, feed_high)
        grad_query, grad_key, grad_value = (jnp.concatenate([a, b], axis=1) for a, b in zip(left, right))
        grad_qv = jnp.concatenate([p[3] for p in (first, second_part, third, fourth)], axis=1)
        grad_embed, sums_one = project_back(
            grad_query, grad_key, grad_value, grad_stream_one, stream_zero, band, gains[0], qk, vm, after=(came_right, came_high)
        )
        for bit in up[1:]:
            keep_left, came_left = next_swap(keep_left, came_left, bit)
        keep_right, came_right = unfold(keep_right), unfold(came_right)
        for bit in down:
            keep_right, came_right = next_swap(keep_right, came_right, bit)
        grad_attention = over_tensor(
            jnp.concatenate([last_sum(keep_left, came_left), last_sum(keep_right, came_right)], axis=0)
        )
        attention_out, merge_out = finish_attention(grad_attention)

        patch_parts = []
        for base, order in ((0, up), (GROUPS // 2, down)):
            keep, send = patch_grads(present, grad_embed, pixels, band, base)
            shape = (pairs, tensor, thin, columns)
            keep, came = unfold(keep.reshape(shape)), unfold(first_swap(send.reshape(shape)))
            for bit in order:
                keep, came = next_swap(keep, came, bit)
            patch_parts.append(last_sum(keep, came))
        grad_patch = over_tensor(jnp.concatenate(patch_parts, axis=2)).astype(F32).T.reshape(GROUPS, pix, thin)
        pixel_grad = pixel_grads(present, grad_embed, band, patches, pix)
        block_output = output_rows(core_at, stream_one, y_low, y_high, biases[3], wide)
        if not aligned:
            block_output = from_split(block_output)

        vector_grads = from_split(
            jnp.concatenate(
                [sums_one[:GROUPS], sums_one[GROUPS : GROUPS + 1], sums_two[0:1], sums_one[GROUPS + 1 : GROUPS + 2]]
                + [sums_two[2:3], sums_two[1:2], sums_two[3:4]],
                axis=0,
            )
        )
        vector_grads = vector_grads.reshape(n_vec, fsdp * tensor, thin).transpose(1, 0, 2).reshape(fsdp, tensor, cut)
        hidden_grads = jnp.concatenate(
            [
                grad_qv.reshape(2, tensor, fsdp, thin).transpose(2, 1, 0, 3).reshape(fsdp, tensor, 2 * thin),
                jnp.stack(unit_grads, axis=1).reshape(tensor, fsdp, unit // fsdp).transpose(1, 0, 2),
            ],
            axis=2,
        )
        small_grads = jnp.concatenate([vector_grads, hidden_grads], axis=2).reshape(fsdp * tensor, -1)
        for axis, bits in (("fsdp", list(range(len(f_bits) + 1))[::-1]), ("tensor", t_bits[::-1])):
            for bit in bits:
                half = small_grads.shape[0] // 2
                mine = (index[axis] >> bit) & 1
                sent = lax.dynamic_slice_in_dim(small_grads, (1 - mine) * half, half)
                small_grads = lax.dynamic_slice_in_dim(small_grads, mine * half, half) + swap(sent, axis, bit)
        small_grads = small_grads[0]
        mine = small_grads[:cut].reshape(n_vec, thin)
        return (
            block_output,
            pixel_grad,
            grad_patch,
            mine[:GROUPS],
            mine[GROUPS : GROUPS + 2],
            mine[GROUPS + 2 :],
            attention_out,
            small_grads[cut : cut + 2 * thin].reshape(2, thin),
            merge_out,
            expand_out,
            small_grads[cut + 2 * thin :],
            contract_out,
        )

    return body


def solution(mesh):
    every = ("fsdp", "tensor")
    args = (
        P(every, None),
        P("fsdp"),
        P(every),
        P(every),
        P(None, None, every),
        P(None, every),
        P(None, every),
        P(None, every),
        P(None, "fsdp", "tensor"),
        P(None, ("tensor", "fsdp")),
        P("tensor", "fsdp"),
        P("fsdp", "tensor"),
        P(("tensor", "fsdp")),
        P("tensor", "fsdp"),
        P(every, None),
    )
    outs = (P(every, None), P(every, None)) + args[4:14]
    body = make_body(mesh.shape["fsdp"], mesh.shape["tensor"])
    return jax.shard_map(body, mesh=mesh, in_specs=args, out_specs=outs, check_vma=False)
```

```python
import math
from functools import partial

import jax
import jax.numpy as jnp
from jax import lax
from jax.experimental import pallas as pl
from jax.experimental.pallas import tpu as pltpu
from jax.sharding import PartitionSpec as P

HEAD_DIM = 64
GROUPS = 4
LANES = 128
TILE = 256
EPSILON = 1e-06
VMEM = 56 * 1024 * 1024
F32 = jnp.float32
BF16 = jnp.bfloat16
NN = (((1,), (0,)), ((), ()))
NT = (((1,), (1,)), ((), ()))
TN = (((0,), (0,)), ((), ()))
ANY = pl.BlockSpec(memory_space=pl.ANY)


def dot(left, right, dims=NN):
    return lax.dot_general(left, right, dims, preferred_element_type=F32)


def merged(block):
    return block.reshape(-1, block.shape[-1])


def joined(refs, *mats):
    blocks = [merged(ref[:, t, mat]) for ref in refs for t in range(ref.shape[1]) for mat in mats]
    return jnp.concatenate(blocks, axis=1)


def qkv_joined(refs, mat):
    blocks = [merged(ref[:, t, ref.shape[2] - 3 + mat]) for ref in refs for t in range(ref.shape[1])]
    return jnp.concatenate(blocks, axis=1)


def beside(refs):
    return jnp.concatenate([ref[...] for ref in refs], axis=1)


def normalize(values):
    row_mean = jnp.mean(values, axis=-1, keepdims=True)
    centred = values - row_mean
    inv_scale = lax.rsqrt(jnp.mean(centred * centred, axis=-1, keepdims=True) + EPSILON)
    return (centred * inv_scale, inv_scale)


def normalize_back(grad_normed, normed, inv_scale):
    return inv_scale * (
        grad_normed
        - jnp.mean(grad_normed, axis=-1, keepdims=True)
        - normed * jnp.mean(grad_normed * normed, axis=-1, keepdims=True)
    )


def whole(shape):
    return pl.BlockSpec(shape, lambda *_: (0,) * len(shape))


def row_tile(shape):
    return pl.BlockSpec((TILE,) + shape[1:], lambda i, *_: (i,) + (0,) * (len(shape) - 1))


def call(kernel, grid, in_specs, out_specs, out_shape, args, scratch=(), flops=0, exps=0, scalars=(), after=(), filled=()):
    count = len(args)
    after = tuple(after) + tuple(array for _, array in filled)
    first = len(scalars) + len(args) + len(after) - len(filled)

    def with_waits(*refs):
        head = refs[: len(scalars) + count]
        return kernel(*head, *refs[len(scalars) + count + len(after) :])

    moved = sum(a.size * a.dtype.itemsize for a in args) + sum(math.prod(s.shape) * s.dtype.itemsize for s in out_shape)
    return pl.pallas_call(
        with_waits,
        grid_spec=pltpu.PrefetchScalarGridSpec(
            num_scalar_prefetch=len(scalars),
            grid=grid,
            in_specs=list(in_specs) + [ANY] * len(after),
            out_specs=list(out_specs),
            scratch_shapes=list(scratch),
        ),
        out_shape=list(out_shape),
        input_output_aliases={first + i: out for i, (out, _) in enumerate(filled)},
        compiler_params=pltpu.CompilerParams(vmem_limit_bytes=VMEM),
        cost_estimate=pl.CostEstimate(flops=int(flops), bytes_accessed=int(moved), transcendentals=int(exps)),
    )(*scalars, *args, *after)


def shaped(shape, dtype):
    return jax.ShapeDtypeStruct(shape, dtype)


def split_kernel(core, array, out, turned, *, wide):
    half = out.shape[1] // 2
    for place in range(half // wide):
        even = array[:, 2 * place * wide : (2 * place + 1) * wide]
        odd = array[:, (2 * place + 1) * wide : (2 * place + 2) * wide]
        at = place * wide
        out[:, at : at + wide] = jnp.where(core[0] == 0, even, odd)
        out[:, half + at : half + at + wide] = jnp.where(core[0] == 0, odd, even)
    turned[...] = out[...].T


def turned_tile(shape):
    return pl.BlockSpec((shape[1], TILE), lambda i, *_: (0, i))


def split_columns(core, array, wide):
    tile = row_tile(array.shape)
    return call(
        partial(split_kernel, wide=wide),
        (array.shape[0] // TILE,),
        [tile],
        [tile, turned_tile(array.shape)],
        [shaped(array.shape, array.dtype), shaped(array.shape[::-1], array.dtype)],
        (array,),
        scalars=(core,),
    )


def shares_kernel(expand, contract, e_low, c_low, high):
    part = e_low.shape[1]
    e_low[...] = expand[:, :part]
    c_low[...] = contract[:part, :].T
    high[0] = expand[:, part:]
    high[1] = contract[part:, :].T


def shares(expand, contract, after=()):
    wide, unit = expand.shape
    half = (wide, unit // 2)
    return call(
        shares_kernel,
        (1,),
        [whole(expand.shape), whole(contract.shape)],
        [whole(half)] * 2 + [whole((2,) + half)],
        [shaped(half, BF16)] * 2 + [shaped((2,) + half, BF16)],
        (expand, contract),
        after=after,
    )


def output_kernel(core, stream, one, two, bias, out, *, wide):
    half = out.shape[1] // 2
    total = stream[...] + one[...] + two[...] + bias[...]
    if wide % LANES:
        out[...] = total
        return
    for place in range(half // wide):
        at = place * wide
        own, other = total[:, at : at + wide], total[:, half + at : half + at + wide]
        out[:, 2 * at : 2 * at + wide] = jnp.where(core[0] == 0, own, other)
        out[:, 2 * at + wide : 2 * at + 2 * wide] = jnp.where(core[0] == 0, other, own)


def output_rows(core, stream, one, two, bias, wide, after=()):
    tile = row_tile(stream.shape)
    return call(
        partial(output_kernel, wide=wide),
        (stream.shape[0] // TILE,),
        [tile] * 3 + [whole(bias.shape)],
        [tile],
        [shaped(stream.shape, F32)],
        (stream, one, two, bias),
        scalars=(core,),
        after=after,
    )[0]


def finish_feed_kernel(blocks, expand, contract):
    expand[...] = blocks[0].astype(F32)
    contract[...] = blocks[1].astype(F32).T


def finish_feed(blocks):
    _, wide, unit = blocks.shape
    return call(
        finish_feed_kernel,
        (1,),
        [whole(blocks.shape)],
        [whole((wide, unit)), whole((unit, wide))],
        [shaped((wide, unit), F32), shaped((unit, wide), F32)],
        (blocks,),
    )


def finish_attention_kernel(blocks, attention, merge_out):
    attention[...] = blocks[:3].astype(F32)
    merge_out[...] = blocks[3].astype(F32).T


def finish_attention(blocks):
    _, wide, columns = blocks.shape
    return call(
        finish_attention_kernel,
        (1,),
        [whole(blocks.shape)],
        [whole((3, wide, columns)), whole((columns, wide))],
        [shaped((3, wide, columns), F32), shaped((columns, wide), F32)],
        (blocks,),
    )


def group_rows(band, group, values):
    return jnp.where(band == group, values, jnp.zeros_like(values))


def embed_kernel(present, pix, band, sin_own, cos_own, sin_came, cos_came, bias, gain, shift, lo_own, lo_came, hi_own, hi_came, stream, normed, turned, acc):
    tile = pl.program_id(0)
    half = acc.shape[1] // 2
    width = pix.shape[1]
    acc[...] = beside((sin_own, cos_own, sin_came, cos_came))
    for group in range(GROUPS):

        @pl.when(present[tile * GROUPS + group] > 0)
        def _():
            rows = group_rows(band[...], group, pix[...])
            at = pl.ds((group % 2) * width, width)
            own, came = (lo_own, lo_came) if group < 2 else (hi_own, hi_came)
            acc[:, :half] += dot(rows, merged(own[:, :, at]), NT)
            acc[:, half:] += dot(rows, merged(came[:, :, at]), NT)

    total = acc[...]
    for group in range(GROUPS):
        total = total + jnp.where(band[...] == group, bias[group : group + 1, :], 0.0)
    stream[...] = total
    rows = (normalize(total)[0] * gain[...] + shift[...]).astype(BF16)
    normed[...] = rows
    turned[...] = rows.T


def embed(present, pixels, band, table, bias, gain, shift, patches, after=()):
    rows, model = pixels.shape[0], gain.shape[1]
    args = (pixels, band) + table + (bias, gain, shift) + patches
    specs = [row_tile(a.shape) for a in args[:6]] + [whole(a.shape) for a in args[6:]]
    return call(
        embed_kernel,
        (rows // TILE,),
        specs,
        [row_tile((rows, model))] * 2 + [turned_tile((rows, model))],
        [shaped((rows, model), F32), shaped((rows, model), BF16), shaped((model, rows), BF16)],
        args,
        scratch=[pltpu.VMEM((TILE, model), F32)],
        flops=4 * rows * pixels.shape[1] * model,
        scalars=(present,),
        after=after,
    )


def project_kernel(x, bias, *refs):
    half = x.shape[1] // 2
    count = (len(refs) - 3) // 2
    weights, outs = refs[: 2 * count], refs[2 * count :]
    for mat, out in enumerate(outs):
        total = dot(x[:, :half], qkv_joined(weights[:count], mat)) + dot(x[:, half:], qkv_joined(weights[count:], mat))
        if mat != 1:
            total = total + bias[mat // 2 : mat // 2 + 1, :]
        out[...] = total.astype(BF16)


def project(x, own, came, bias, after=()):
    rows, model = x.shape
    width = bias.shape[1]
    weights = tuple(own) + tuple(came)
    return call(
        project_kernel,
        (rows // TILE,),
        [row_tile(x.shape), whole(bias.shape)] + [whole(w.shape) for w in weights],
        [row_tile((rows, width))] * 3,
        [shaped((rows, width), BF16)] * 3,
        (x, bias) + weights,
        flops=6 * rows * model * width,
        after=after,
    )


def head_mask(shape, head):
    lane = lax.broadcasted_iota(jnp.int32, shape, 1)
    return (lane < HEAD_DIM) if head == 0 else (lane >= HEAD_DIM)


def only_head(values, head):
    return jnp.where(head_mask(values.shape, head), values, jnp.zeros_like(values))


def attend_kernel(q_ref, k_ref, v_ref, seg_col_ref, seg_row_ref, out_ref, log_ref, bias_ref, *, base):
    pair = base + pl.program_id(0)
    rows = q_ref.shape[0]

    @pl.when(pl.program_id(0) == 0)
    def _():
        bias_ref[...] = jnp.where(seg_col_ref[...] == seg_row_ref[...], 0.0, -1e30).astype(F32)
        log_ref[...] = jnp.zeros_like(log_ref)

    keys = k_ref[...]
    value_of = [only_head(v_ref[...], head) for head in range(2)]
    for start in range(0, rows, TILE):
        at = pl.ds(start, TILE)
        query = q_ref[at, :] * jnp.asarray(HEAD_DIM ** (-0.5), BF16)
        lane = lax.broadcasted_iota(jnp.int32, (TILE, LANES), 1)
        logs = log_ref[at, :]
        total = jnp.zeros((TILE, LANES), F32)
        for head in range(2):
            scores = dot(only_head(query, head), keys, NT) + bias_ref[at, :]
            top = jnp.max(scores, axis=1, keepdims=True)
            shifted = jnp.exp(scores - top)
            mass = jnp.sum(shifted, axis=1, keepdims=True)
            total = total + dot(shifted.astype(BF16), value_of[head]) * (1.0 / mass)
            logs = jnp.where(lane == 2 * pair + head, top + jnp.log(mass), logs)
        out_ref[at, :] = total.astype(BF16)
        log_ref[at, :] = logs


def attend(query, key, value, seg, base, skip, pairs, after=()):
    rows = query.shape[0]
    width = pairs * LANES
    block = pl.BlockSpec((rows, LANES), lambda i: (0, skip + i))
    return call(
        partial(attend_kernel, base=base + skip),
        (pairs,),
        [block, block, block, whole((rows, 1)), whole((1, rows))],
        [pl.BlockSpec((rows, LANES), lambda i: (0, i)), whole((rows, LANES))],
        [shaped((rows, width), BF16), shaped((rows, LANES), F32)],
        (query, key, value) + seg,
        scratch=[pltpu.VMEM((rows, rows), F32)],
        flops=16 * rows * rows * width,
        exps=rows * rows * width // HEAD_DIM,
        after=after,
    )


def attend_back_kernel(
    q_ref, k_ref, v_ref, g_ref, seg_col_ref, seg_row_ref, log_ref, delta_ref, dq_ref, dk_ref, dv_ref, sum_ref, bias_ref, acc_ref, *, base
):
    pair = base + pl.program_id(0)
    rows = q_ref.shape[0]

    @pl.when(pl.program_id(0) == 0)
    def _():
        bias_ref[...] = jnp.where(seg_col_ref[...] == seg_row_ref[...], 0.0, -1e30).astype(F32)

    query = q_ref[...] * jnp.asarray(HEAD_DIM ** (-0.5), BF16)
    grads = g_ref[...]
    query_of = [only_head(query, head) for head in range(2)]
    grads_of = [only_head(grads, head) for head in range(2)]
    acc_ref[...] = jnp.zeros_like(acc_ref)
    value_sum = jnp.zeros((1, LANES), F32)
    for start in range(0, rows, TILE):
        at = pl.ds(start, TILE)
        keys = k_ref[at, :]
        values = v_ref[at, :]
        grad_key = jnp.zeros((TILE, LANES), F32)
        grad_value = jnp.zeros((TILE, LANES), F32)
        for head in range(2):
            key_h = only_head(keys, head)
            log_row = log_ref[pl.ds(2 * pair + head, 1), :]
            delta_row = delta_ref[pl.ds(2 * pair + head, 1), :]
            scores = dot(key_h, query, NT) + bias_ref[at, :]
            probs = jnp.exp(scores - log_row)
            grad_value = grad_value + dot(probs.astype(BF16), grads_of[head])
            grad_probs = dot(only_head(values, head), grads, NT)
            grad_scores = (probs * (grad_probs - delta_row)).astype(BF16)
            grad_key = grad_key + dot(grad_scores, query_of[head])
            acc_ref[...] += dot(key_h, grad_scores, TN)
        grad_value = grad_value.astype(BF16)
        dk_ref[at, :] = grad_key.astype(BF16)
        dv_ref[at, :] = grad_value
        value_sum = value_sum + jnp.sum(grad_value.astype(F32), axis=0, keepdims=True)
    grad_query = (acc_ref[...].T * HEAD_DIM ** (-0.5)).astype(BF16)
    dq_ref[...] = grad_query
    sum_ref[0:1, :] = jnp.sum(grad_query.astype(F32), axis=0, keepdims=True)
    sum_ref[1:2, :] = value_sum


def attend_back(query, key, value, grads, seg, log_rows, delta_rows, base, pairs, after=()):
    rows = query.shape[0]
    width = pairs * LANES
    taken = pl.BlockSpec((rows, LANES), lambda i: (0, base + i))
    given = pl.BlockSpec((rows, LANES), lambda i: (0, i))
    return call(
        partial(attend_back_kernel, base=base),
        (pairs,),
        [given] * 3 + [taken, whole((rows, 1)), whole((1, rows)), whole(log_rows.shape), whole(delta_rows.shape)],
        [given] * 3 + [pl.BlockSpec((2, LANES), lambda i: (0, i))],
        [shaped((rows, width), BF16)] * 3 + [shaped((2, width), F32)],
        (query, key, value, grads) + seg + (log_rows, delta_rows),
        scratch=[pltpu.VMEM((rows, rows), F32), pltpu.VMEM((LANES, rows), F32)],
        flops=40 * rows * rows * width,
        exps=rows * rows * width // HEAD_DIM,
        after=after,
    )


def merge_kernel(*refs, count):
    attended = beside(refs[:count])
    stream, bias, gain, shift, own_low, own_high, came_low, came_high, stream_one, normed, turned = refs[count:]
    half = stream.shape[1] // 2
    stream_one[:, :half] = stream[:, :half] + dot(attended, joined((own_low, own_high), 0, 1), NT)
    stream_one[:, half:] = stream[:, half:] + dot(attended, joined((came_low, came_high), 0, 1), NT)
    total = stream_one[...] + bias[...]
    stream_one[...] = total
    rows = (normalize(total)[0] * gain[...] + shift[...]).astype(BF16)
    normed[...] = rows
    turned[...] = rows.T


def first_two(array):
    return pl.BlockSpec(array.shape[:2] + (2,) + array.shape[3:], lambda *_: (0,) * array.ndim)


def merge(attended, stream, bias, gain, shift, weights, after=()):
    rows, model = stream.shape
    return call(
        partial(merge_kernel, count=len(attended)),
        (rows // TILE,),
        [row_tile(a.shape) for a in attended]
        + [row_tile(stream.shape)]
        + [whole((1, model))] * 3
        + [first_two(a) for a in weights],
        [row_tile((rows, model))] * 2 + [turned_tile((rows, model))],
        [shaped((rows, model), F32), shaped((rows, model), BF16), shaped((model, rows), BF16)],
        tuple(attended) + (stream, bias, gain, shift) + weights,
        flops=2 * rows * model * model,
        after=after,
    )


def gelu_parts(hidden):
    t = 1.0 / (1.0 + (0.3275911 * math.sqrt(0.5)) * jnp.abs(hidden))
    bell = jnp.exp(-0.5 * hidden * hidden)
    poly = t * (
        0.5 * 0.254829592
        + t * (-0.5 * 0.284496736 + t * (0.5 * 1.421413741 + t * (-0.5 * 1.453152027 + t * (0.5 * 1.061405429))))
    )
    tail = poly * bell
    below = jnp.where(hidden >= 0, 1.0 - tail, tail)
    return hidden * below, below + (hidden * (1.0 / math.sqrt(2.0 * math.pi))) * bell


def feed_kernel(
    x_ref, xt_ref, g_ref, gt_ref, e_own, e_other, c_own, c_other, b_ref, y_ref, d_ref, *grads
):
    e_keep, e_send, c_keep, c_send, db_ref, a_ref, h_ref = grads
    step = pl.program_id(0)
    rows, model = x_ref.shape
    half = model // 2

    @pl.when(step == 0)
    def _():
        y_ref[...] = jnp.zeros_like(y_ref)
        d_ref[...] = jnp.zeros_like(d_ref)

    expand = (merged(e_own[...]), merged(e_other[...]))
    contract = (merged(c_own[...]), merged(c_other[...]))
    sums = jnp.zeros((1, h_ref.shape[1]), F32)
    for start in range(0, rows, TILE):
        at = pl.ds(start, TILE)
        hidden = dot(x_ref[at, :half], expand[0]) + dot(x_ref[at, half:], expand[1]) + b_ref[0]
        grad_active = dot(g_ref[at, :half], contract[0]) + dot(g_ref[at, half:], contract[1])
        active, slope = gelu_parts(hidden)
        active = active.astype(BF16)
        grad_hidden = (grad_active * slope).astype(BF16)
        a_ref[at, :] = active
        h_ref[at, :] = grad_hidden
        sums = sums + jnp.sum(grad_hidden.astype(F32), axis=0, keepdims=True)
        for side in range(2):
            cols = pl.ds(side * half, half)
            y_ref[at, cols] += dot(active, contract[side], NT)
            d_ref[at, cols] += dot(grad_hidden, expand[side], NT)
    db_ref[0] = sums
    for side, (e_ref, c_ref) in enumerate(((e_keep, c_keep), (e_send, c_send))):
        cols = pl.ds(side * half, half)
        shape = e_ref.shape[:1] + e_ref.shape[2:]
        e_ref[:, 0] = dot(xt_ref[cols, :], h_ref[...]).astype(BF16).reshape(shape)
        c_ref[:, 0] = dot(gt_ref[cols, :], a_ref[...]).astype(BF16).reshape(shape)


def feed(core, rows_two, turned_two, top, turned_top, weights, bias, which, filled=(), after=()):
    rows, model = rows_two.shape
    steps, _, part = bias.shape
    pairs, wide = weights[0].shape[0], weights[0].shape[-2]
    if len(weights) == 1:
        weights = weights * 4
        block = (pairs, 1, 1, 1, wide, part)
        place = lambda side, mat: lambda i, core: (0, core[0] if side == 0 else 1 - core[0], i, mat, 0, 0)
        specs = [pl.BlockSpec(block, place(side, mat)) for mat in range(2) for side in range(2)]
    else:
        specs = [pl.BlockSpec((pairs, 1, wide, part), lambda i, core: (0, i, 0, 0))] * 4
    grad = pl.BlockSpec((pairs, 1, wide, part), lambda i, core: (0, i, 0, which))
    unit = pl.BlockSpec((1, 1, part), lambda i, core: (i, 0, 0))
    return call(
        lambda core, *refs: feed_kernel(*refs),
        (steps,),
        [whole((rows, model)), whole((model, rows))] * 2 + specs + [unit],
        [whole((rows, model))] * 2 + [grad] * 4 + [unit],
        [shaped((rows, model), F32)] * 2
        + [shaped((pairs, steps, wide, 2 * part), BF16)] * 4
        + [shaped((steps, 1, part), F32)],
        (rows_two, turned_two, top, turned_top) + tuple(weights) + (bias,),
        scratch=[pltpu.VMEM((rows, part), BF16)] * 2,
        flops=12 * rows * model * part * steps,
        exps=rows * part * steps,
        scalars=(core,),
        after=after,
        filled=[(2 + i, array) for i, array in enumerate(filled)],
    )


def merge_back_kernel(*refs, count):
    attended = beside(refs[:count])
    d_one, d_two, top, stream_one, gain, own_low, own_high, came_low, came_high, heads = refs[count : count + 10]
    grad_stream, turned, grad_attended, delta, sums = refs[count + 10 :]
    half = top.shape[1] // 2
    grad_two = d_one[...] + d_two[...]
    normed, scale = normalize(stream_one[...])
    cotangent = top[...].astype(F32)
    total = cotangent + normalize_back(grad_two * gain[...], normed, scale)
    grad_stream[...] = total
    low = total.astype(BF16)
    turned[...] = low.T
    grads = dot(low[:, :half], joined((own_low, own_high), 0, 1)) + dot(low[:, half:], joined((came_low, came_high), 0, 1))
    grads = grads.astype(BF16)
    grad_attended[...] = grads
    both = grads.astype(F32) * attended.astype(F32)
    high = both.astype(BF16)
    delta[...] = dot(heads[...], high, NT) + dot(heads[...], (both - high.astype(F32)).astype(BF16), NT)

    @pl.when(pl.program_id(0) == 0)
    def _():
        sums[...] = jnp.zeros_like(sums)

    for row, part in enumerate((grad_two * normed, grad_two, total, cotangent)):
        sums[row : row + 1, :] += jnp.sum(part, axis=0, keepdims=True)


def merge_back(attended, d_one, d_two, top, stream_one, gain, weights, heads, after=()):
    rows, model = stream_one.shape
    tile = row_tile((rows, model))
    return call(
        partial(merge_back_kernel, count=len(attended)),
        (rows // TILE,),
        [row_tile(a.shape) for a in attended]
        + [tile] * 4
        + [whole((1, model))]
        + [first_two(a) for a in weights]
        + [whole(heads.shape)],
        [tile, turned_tile((rows, model)), tile]
        + [pl.BlockSpec((heads.shape[0], TILE), lambda i: (0, i)), whole((8, model))],
        [
            shaped((rows, model), F32),
            shaped((model, rows), BF16),
            shaped((rows, model), BF16),
            shaped((heads.shape[0], rows), F32),
            shaped((8, model), F32),
        ],
        tuple(attended) + (d_one, d_two, top, stream_one, gain) + weights + (heads,),
        flops=2 * rows * model * model,
        after=after,
    )


def attention_grads_kernel(*refs, count):
    xt, bt = refs[:2]
    inputs = [beside(refs[2 + i * count : 2 + (i + 1) * count]) for i in range(3)]
    inputs.append(beside(refs[2 + 3 * count : -4]))
    outs = refs[-4:]
    half = xt.shape[0] // 2
    blocks, steps, _, wide, columns = outs[0].shape
    for place, right in enumerate(inputs):
        left = bt if place == 3 else xt
        for side in range(2):
            ref = outs[2 * (place // 2) + side]
            grad = dot(left[pl.ds(side * half, half), :], right).astype(BF16)
            for step in range(steps):
                part = grad[:, step * columns : (step + 1) * columns]
                ref[:, step, place % 2] = part.reshape(blocks, wide, columns)


def attention_grads(xt, bt, query, key, value, attended, blocks, columns, after=()):
    model, rows = xt.shape
    count = len(query)
    width = sum(a.shape[1] for a in query)
    shape = (blocks, width // columns, 2, model // (2 * blocks), columns)
    args = (xt, bt) + tuple(query) + tuple(key) + tuple(value) + tuple(attended)
    return call(
        partial(attention_grads_kernel, count=count),
        (1,),
        [whole(a.shape) for a in args],
        [whole(shape)] * 4,
        [shaped(shape, BF16)] * 4,
        args,
        flops=8 * rows * model * width,
        after=after,
    )


def project_back_kernel(*refs, count):
    grads = [beside(refs[i * count : (i + 1) * count]) for i in range(3)]
    rest = refs[3 * count :]
    grad_stream, stream, band, gain = rest[:4]
    weights = rest[4:-4]
    grad_embed, turned, sums, acc = rest[-4:]
    half = stream.shape[1] // 2
    each = len(weights) // 2
    for side in range(2):
        held = weights[side * each : (side + 1) * each]
        acc[:, side * half : (side + 1) * half] = sum(
            dot(grad, qkv_joined(held, mat), NT) for mat, grad in enumerate(grads)
        )
    grad_one = acc[...]
    normed, scale = normalize(stream[...])
    total = grad_stream[...] + normalize_back(grad_one * gain[...], normed, scale)
    low = total.astype(BF16)
    grad_embed[...] = low
    turned[...] = low.T

    @pl.when(pl.program_id(0) == 0)
    def _():
        sums[...] = jnp.zeros_like(sums)

    parts = [group_rows(band[...], group, total) for group in range(GROUPS)] + [grad_one * normed, grad_one]
    for row, part in enumerate(parts):
        sums[row : row + 1, :] += jnp.sum(part, axis=0, keepdims=True)


def project_back(query, key, value, grad_stream, stream, band, gain, weights, after=()):
    rows, model = stream.shape
    tile = row_tile((rows, model))
    parts = tuple(query) + tuple(key) + tuple(value)
    return call(
        partial(project_back_kernel, count=len(query)),
        (rows // TILE,),
        [row_tile(a.shape) for a in parts]
        + [tile] * 2
        + [row_tile(band.shape), whole((1, model))]
        + [whole(a.shape) for a in weights],
        [tile, turned_tile((rows, model)), whole((8, model))],
        [shaped((rows, model), BF16), shaped((model, rows), BF16), shaped((8, model), F32)],
        parts + (grad_stream, stream, band, gain) + weights,
        scratch=[pltpu.VMEM((TILE, model), F32)],
        flops=6 * rows * model * model,
        after=after,
    )


def patch_grads_kernel(present, gt, pix, band, keep, send, acc, *, base):
    group = base + pl.program_id(0)
    half = gt.shape[0] // 2
    acc[...] = jnp.zeros_like(acc)
    for tile in range(pix.shape[0] // TILE):

        @pl.when(present[tile * GROUPS + group] > 0)
        def _():
            at = pl.ds(tile * TILE, TILE)
            acc[...] += dot(gt[:, at], group_rows(band[at, :], group, pix[at, :]))

    keep[...] = acc[:half, :].astype(BF16)
    send[...] = acc[half:, :].astype(BF16)


def patch_grads(present, turned, pixels, band, base, after=()):
    model, rows = turned.shape
    width = pixels.shape[1]
    count = GROUPS // 2
    given = pl.BlockSpec((model // 2, width), lambda i, present: (0, i))
    return call(
        partial(patch_grads_kernel, base=base),
        (count,),
        [whole(turned.shape), whole(pixels.shape), whole(band.shape)],
        [given] * 2,
        [shaped((model // 2, count * width), BF16)] * 2,
        (turned, pixels, band),
        scratch=[pltpu.VMEM((model, width), F32)],
        flops=2 * rows * width * model,
        scalars=(present,),
        after=after,
    )


def pixel_grads_kernel(present, grads, band, lo_own, lo_came, hi_own, hi_came, out):
    tile = pl.program_id(0)
    half = grads.shape[1] // 2
    width = out.shape[1]
    out[...] = jnp.zeros_like(out)
    for group in range(GROUPS):

        @pl.when(present[tile * GROUPS + group] > 0)
        def _():
            at = pl.ds((group % 2) * width, width)
            own, came = (lo_own, lo_came) if group < 2 else (hi_own, hi_came)
            spread = dot(grads[:, :half], merged(own[:, :, at])) + dot(grads[:, half:], merged(came[:, :, at]))
            out[...] = jnp.where(band[...] == group, spread, out[...])


def pixel_grads(present, grads, band, patches, width, after=()):
    rows, model = grads.shape
    return call(
        pixel_grads_kernel,
        (rows // TILE,),
        [row_tile(grads.shape), row_tile(band.shape)] + [whole(a.shape) for a in patches],
        [row_tile((rows, width))],
        [shaped((rows, width), F32)],
        (grads, band) + patches,
        flops=4 * rows * width * model,
        scalars=(present,),
        after=after,
    )[0]


def make_body(fsdp, tensor):
    pairs = fsdp // 2
    t_bits = list(range(tensor.bit_length() - 1))
    f_bits = list(range(1, fsdp.bit_length() - 1))
    up, down = f_bits, f_bits[::-1]

    def swap(array, axis, bit):
        size = fsdp if axis == "fsdp" else tensor
        return lax.ppermute(array, axis, [(i, i ^ (1 << bit)) for i in range(size)])

    def body(
        pixels,
        segment,
        band_group,
        scaled_position,
        patch_weight,
        patch_bias,
        norm_gains,
        vector_biases,
        attention_weight,
        query_value_bias,
        merge_weight,
        expand_weight,
        expand_bias,
        contract_weight,
        cotangent,
    ):
        index = {"fsdp": lax.axis_index("fsdp"), "tensor": lax.axis_index("tensor")}
        core = index["fsdp"] & 1
        rows, pix = pixels.shape
        model = cotangent.shape[1]
        thin = patch_bias.shape[1]
        wide = model // fsdp
        unit = expand_weight.shape[1]
        half_unit = unit // 2
        segment = lax.dynamic_slice_in_dim(segment, index["tensor"] * rows, rows)

        def wider(array, came, axis, bit):
            dim = 0 if axis == "tensor" else len(f_bits) - bit
            mine = ((index[axis] >> bit) & 1) == 1
            return jnp.where(
                mine, jnp.concatenate([came, array], axis=dim), jnp.concatenate([array, came], axis=dim)
            )

        def shifts(make):
            count = tensor
            return [
                lax.ppermute(make(d), "tensor", [(i, (i + d) % count) for i in range(count)]) for d in range(1, count)
            ]

        def in_order(array, came):
            parts = jnp.stack([array] + came)[::-1]
            return lax.dynamic_slice_in_dim(jnp.concatenate([parts, parts]), tensor - 1 - index["tensor"], tensor)

        def open_f(array):
            return array.reshape((1,) * len(f_bits) + array.shape)

        def close_f(array):
            return array.reshape((pairs,) + array.shape[len(f_bits) :])

        def other_core(array):
            return swap(array, "fsdp", 0)

        class Pair:
            def __init__(self, one, two):
                self.held = [open_f(one), open_f(two)]
                self.todo = list(zip(up, down))

            def send(self):
                self.bits = self.todo.pop(0)
                return [swap(a, "fsdp", bit) for a, bit in zip(self.held, self.bits)]

            def take(self, came):
                self.held = [wider(a, c, "fsdp", bit) for a, c, bit in zip(self.held, came, self.bits)]

            def drain(self):
                while self.todo:
                    self.take(self.send())

            def closed(self):
                return [close_f(a) for a in self.held]

        def half_sum(keep, came, at, bit):
            dim = len(f_bits) - bit
            take = lambda array: lax.dynamic_slice_in_dim(array, at, 1, axis=dim)
            return (take(keep).astype(F32) + take(came).astype(F32)).astype(keep.dtype)

        class Sum:
            def __init__(self, keep, send, bits):
                self.keep, self.todo = unfold(keep), list(bits)
                self.came = unfold(swap(send, "fsdp", 0))

            def step(self):
                bit = self.todo.pop(0)
                mine = (index["fsdp"] >> bit) & 1
                self.sent = half_sum(self.keep, self.came, 1 - mine, bit)
                self.keep = half_sum(self.keep, self.came, mine, bit)
                self.came = swap(self.sent, "fsdp", bit)
                return self.sent

            def total(self):
                while self.todo:
                    self.step()
                return last_sum(self.keep, self.came)

        def unfold(array):
            return array.reshape((2,) * len(f_bits) + array.shape[1:])

        def last_sum(keep, came):
            rest = keep.shape[len(f_bits) :]
            return (keep.astype(F32) + came.astype(F32)).astype(keep.dtype).reshape(rest)

        def over_tensor(blocks):
            return lax.psum_scatter(blocks, "tensor", scatter_dimension=0, tiled=False)

        def to_split(array):
            parts = array.reshape(array.shape[0], pairs, 2, wide)
            even, odd = (parts[:, :, i].reshape(array.shape[0], -1) for i in range(2))
            return jnp.where(core == 0, jnp.concatenate([even, odd], axis=1), jnp.concatenate([odd, even], axis=1))

        def from_split(array):
            parts = array.reshape(array.shape[0], 2, pairs, wide)
            mine, other = parts[:, 0], parts[:, 1]
            parts = jnp.where(core == 0, jnp.stack([mine, other], axis=2), jnp.stack([other, mine], axis=2))
            return parts.reshape(array.shape)

        tie = lambda array, *others: lax.optimization_barrier((array,) + others)[0]
        core_at = core[None].astype(jnp.int32)
        aligned = wide % LANES == 0

        sync = lax.optimization_barrier
        n_vec = GROUPS + 2 + 4
        cut = n_vec * thin
        columns = (GROUPS // 2) * pix
        rest_up, rest_down = up[1:], down[1:]

        small = jnp.concatenate(
            [patch_bias, norm_gains, vector_biases, query_value_bias, expand_bias.reshape(-1, thin)], axis=0
        )
        extra = small.shape[0]
        small = jnp.pad(small.T, ((0, 0), (0, LANES - extra)))
        patch = jnp.concatenate([patch_weight.reshape(-1, thin).T, small], axis=1)
        attention = jnp.concatenate([attention_weight, merge_weight.T[None]], axis=0)[None]
        t_first, t_rest = t_bits[:1], t_bits[1:]

        def over_t(array, came, bits):
            for i, bit in enumerate(bits):
                array = wider(array, came if i == 0 else swap(array, "tensor", bit), "tensor", bit)
            return array

        def start_t(bits, *arrays):
            return [swap(a, "tensor", bits[0]) for a in arrays]

        def go(*pairs):
            return [p.send() if p.todo else None for p in pairs]

        def done(came, *pairs):
            for c, p in zip(came, pairs):
                if c is not None:
                    p.take(c)

        def both_cores(pair):
            held = pair.closed()
            return held, [other_core(a) for a in held]

        band = band_group[:, None]
        present = jnp.any(band_group.reshape(-1, TILE, 1) == jnp.arange(GROUPS), axis=1).astype(jnp.int32).reshape(-1)
        came = shifts(lambda d: patch)
        e_one, c_one, feed_high = shares(expand_weight, contract_weight)
        e_one, c_one = e_one[None], c_one[None]
        seg = (segment[:, None], segment[None, :])
        came, patch, attention, cotangent, e_one, band, present, seg = sync(
            (came, patch, attention, cotangent, e_one, band, present, seg)
        )
        patch = in_order(patch, came).reshape(tensor * thin, -1)
        patch = Pair(patch[:, :columns], patch[:, columns:])
        came = go(patch)
        came_t = start_t(t_first, attention, e_one)
        if aligned:
            top, turned_top = split_columns(core_at, cotangent, wide)
        else:
            top = to_split(cotangent)
            turned_top = top.T
        came, came_t, top, c_one, scaled_position = sync((came, came_t, top, c_one, scaled_position))
        done(came, patch)
        attention, e_one = (over_t(w, c, t_first) for w, c in zip((attention, e_one), came_t))
        came = go(patch)
        came_t = start_t(t_rest, attention) + start_t(t_first, c_one)
        half_width = model // 2
        column = jnp.arange(model)
        place = column % half_width
        natural = (2 * (place // wide) + (core ^ (column // half_width))) * wide + place % wide
        rates = jnp.exp((natural % half_width).astype(F32) * (-math.log(10000.0) / half_width))
        angles = scaled_position.astype(F32)[:, None] * rates[None, :]
        quarter = model // 4
        table = tuple(
            f(angles[:, i * quarter : (i + 1) * quarter]) for i, f in enumerate((jnp.sin, jnp.cos, jnp.sin, jnp.cos))
        )
        came, came_t, table, e_one = sync((came, came_t, table, e_one))
        done(came, patch)
        patch.drain()
        attention = over_t(attention, came_t[0], t_rest)
        c_one = over_t(c_one, came_t[1], t_first)
        quarter, half_t = tensor // 4, tensor // 2
        outward = [
            attention[i * half_t : (i + 1) * half_t, 3].reshape(quarter, 2, wide, -1) for i in range(2)
        ]
        qkv = [attention[i * quarter : (i + 1) * quarter, :3] for i in range(4)]
        qkv_one = Pair(*qkv[:2])
        qkv_two = Pair(*(jnp.concatenate(two, axis=1) for two in zip(outward, qkv[2:])))
        patch = both_cores(patch)
        came, came_t = go(qkv_one), start_t(t_rest, e_one)
        patch, came, came_t, c_one, feed_high = sync((patch, came, came_t, c_one, feed_high))
        patches = (patch[0][0], patch[1][0], patch[0][1], patch[1][1])
        done(came, qkv_one)
        e_one = over_t(e_one, came_t[0], t_rest)
        came, came_t = go(qkv_one), start_t(t_rest, c_one)
        feed_high = lax.all_gather(feed_high, ("fsdp", "tensor"), axis=0, tiled=False)
        feed_high = feed_high.reshape(pairs, 2, tensor, 2, wide, half_unit)
        small = [held[0] for held in (patch[0][1:], patch[1][1:])]
        small = jnp.stack([held[:, :, columns : columns + extra] for held in small]).astype(F32)
        vectors = small.reshape(model, extra).T
        patch_bias_rows = vectors[:GROUPS]
        gains = [vectors[GROUPS + i : GROUPS + i + 1] for i in range(2)]
        biases = [vectors[GROUPS + 2 + i : GROUPS + 3 + i] for i in range(4)]
        by_hidden = small[:, :, :, n_vec:].reshape(2, pairs, tensor, thin, extra - n_vec)
        by_hidden = jnp.where(core == 0, by_hidden, by_hidden[::-1]).transpose(4, 2, 1, 0, 3)
        qv_rows = by_hidden[:2].reshape(2, model)
        unit_bias = by_hidden[2:].reshape(-1, tensor, fsdp, thin).transpose(1, 2, 0, 3).reshape(tensor, 2, 1, half_unit)

        stream_zero, input_one, turned_one = embed(
            present, pixels, band, table, patch_bias_rows, gains[0], biases[0], patches
        )
        came, came_t, input_one, turned_one = sync((came, came_t, input_one, turned_one))
        done(came, qkv_one)
        qkv_one.drain()
        c_one = over_t(c_one, came_t[0], t_rest)
        feed_one = Pair(e_one, c_one)
        one, came = both_cores(qkv_one), go(qkv_two)
        one, came, input_one, feed_one.held = sync((one, came, input_one, feed_one.held))
        done(came, qkv_two)
        came = go(qkv_two)
        heads_width = model // 2
        each = heads_width // LANES
        first = project(input_one, *one, qv_rows[:, :heads_width])
        attended, logs = [None] * 3, [None] * 3
        attended[0], logs[0] = attend(*first, seg, 0, 0, each // 2)
        came, attended[0] = sync((came, attended[0]))
        done(came, qkv_two)
        qkv_two.drain()
        two, came = both_cores(qkv_two), go(feed_one)
        attended[1], logs[1] = attend(*first, seg, 0, each // 2, each // 2, after=(attended[0],))
        two, came, attended[1], input_one = sync((two, came, attended[1], input_one))
        done(came, feed_one)
        came = go(feed_one)
        last = project(input_one, *two, qv_rows[:, heads_width:])
        attended[2], logs[2] = attend(*last, seg, each, 0, each)
        came, attended[2] = sync((came, attended[2]))
        done(came, feed_one)
        feed_one.drain()
        feed_one = both_cores(feed_one)
        outward = tuple(two[0] + two[1])
        stream_one, input_two, turned_two = merge(attended, stream_zero, biases[1], gains[1], biases[2], outward)
        feed_one, input_two = sync((feed_one, input_two))

        rows_two = (input_two, turned_two, top, turned_top)
        weights = tuple(a for pair in zip(*feed_one) for a in pair)
        y_low, d_low, *grads_low, units_low = feed(core_at, *rows_two, weights, unit_bias[:, 0], 0)
        y_high, d_high, *grads_high, units_high = feed(
            core_at, *rows_two, (feed_high,), unit_bias[:, 1], 1, filled=grads_low, after=(y_low,)
        )
        unit_grads = [units_low, units_high]

        heads = model // HEAD_DIM
        head_rows = (jnp.arange(heads)[:, None] == jnp.arange(model)[None, :] // HEAD_DIM).astype(BF16)
        expand_sum = Sum(grads_high[0], grads_high[1], down)
        contract_sum = Sum(grads_high[2], grads_high[3], up)

        def meet(sums, *arrays):
            waited = sync(([t.came for t in sums],) + arrays)
            for t, came in zip(sums, waited[0]):
                t.came = came
            return waited[1] if len(arrays) == 1 else waited[1:]

        def advance(*sums):
            return [t.step() if t.todo else t.came for t in sums]

        def drain(*sums):
            for t in sums:
                while t.todo:
                    t.step()

        grad_stream_one, turned_branch, grad_attended, delta, sums_two = merge_back(
            attended, d_low, d_high, top, stream_one, gains[1], outward, head_rows
        )
        grad_attended = meet((expand_sum, contract_sum), grad_attended)
        log_rows = sum(logs)[:, :heads].T
        back = lambda i, after: attend_back(
            *(first, last)[i], grad_attended, seg, log_rows, delta, i * each, each, after=after
        )

        def grads_of(part, which, after):
            return attention_grads(
                turned_one, turned_branch, *([p] for p in part[:3]), attended[2 * which : 2 + which], pairs, model // tensor, after=after
            )

        first_part = back(0, advance(expand_sum, contract_sum))
        left = meet((expand_sum, contract_sum), grads_of(first_part, 0, ()))
        waits = advance(expand_sum, contract_sum)
        left_qk, left_vm = Sum(left[0], left[1], down), Sum(left[2], left[3], up)
        second_part = back(1, waits)
        second_part = meet((expand_sum, contract_sum, left_qk, left_vm), second_part)
        drain(expand_sum, contract_sum)
        feed_blocks = jnp.stack([expand_sum.total(), contract_sum.total()], axis=1)
        feed_grads = over_tensor(feed_blocks)
        right = grads_of(second_part, 1, advance(left_qk, left_vm) + [feed_blocks])
        right = meet((left_qk, left_vm), right)
        waits = advance(left_qk, left_vm)
        right_qk, right_vm = Sum(right[0], right[1], down), Sum(right[2], right[3], up)
        parts = (first_part, second_part)
        grad_query, grad_key, grad_value = ([p[i] for p in parts] for i in range(3))
        grad_qv = jnp.concatenate([p[3] for p in parts], axis=1)
        grad_embed, turned_embed, sums_one = project_back(
            grad_query, grad_key, grad_value, grad_stream_one, stream_zero, band, gains[0], tuple(one[0] + two[0] + one[1] + two[1]), after=waits
        )
        grad_embed, turned_embed = meet((left_qk, left_vm, right_qk, right_vm), grad_embed, turned_embed)

        waits = advance(right_qk, right_vm)
        shape = (pairs, tensor, thin, columns)
        lo = patch_grads(present, turned_embed, pixels, band, 0, after=waits)
        hi = patch_grads(present, turned_embed, pixels, band, GROUPS // 2, after=lo[:1])
        lo, hi = meet((right_qk, right_vm), lo, hi)
        lo = Sum(*(a.reshape(shape) for a in lo), up)
        hi = Sum(*(a.reshape(shape) for a in hi), down)
        waits = advance(right_qk, right_vm)

        vector_grads = from_split(
            jnp.concatenate(
                [sums_one[:GROUPS], sums_one[GROUPS : GROUPS + 1], sums_two[0:1], sums_one[GROUPS + 1 : GROUPS + 2]]
                + [sums_two[2:3], sums_two[1:2], sums_two[3:4]],
                axis=0,
            )
        )
        vector_grads = vector_grads.reshape(n_vec, fsdp * tensor, thin).transpose(1, 0, 2).reshape(fsdp, tensor, cut)
        hidden_grads = jnp.concatenate(
            [
                grad_qv.reshape(2, tensor, fsdp, thin).transpose(2, 1, 0, 3).reshape(fsdp, tensor, 2 * thin),
                jnp.stack(unit_grads, axis=1).reshape(tensor, fsdp, unit // fsdp).transpose(1, 0, 2),
            ],
            axis=2,
        )
        small_grads = jnp.concatenate([vector_grads, hidden_grads], axis=2).reshape(fsdp * tensor, -1)
        halvings = [("fsdp", bit) for bit in range(len(f_bits) + 1)[::-1]] + [("tensor", bit) for bit in t_bits[::-1]]

        def small_halves(array, axis, bit):
            half = array.shape[0] // 2
            mine = (index[axis] >> bit) & 1
            return (
                lax.dynamic_slice_in_dim(array, mine * half, half),
                swap(lax.dynamic_slice_in_dim(array, (1 - mine) * half, half), axis, bit),
            )

        small_kept, small_came = small_halves(small_grads, *halvings[0])
        block_output = output_rows(
            core_at, stream_one, y_low, y_high, biases[3], wide, after=waits + [small_kept]
        )
        if not aligned:
            block_output = from_split(block_output)
        small_came, block_output = meet((right_qk, right_vm, lo, hi), small_came, block_output)
        waits = advance(lo, hi)
        drain(left_qk, left_vm, right_qk, right_vm)
        small_kept, small_came = small_halves(small_kept + small_came, *halvings[1])
        pixel_grad = pixel_grads(present, grad_embed, band, patches, pix, after=waits + [small_kept])
        grad_attention = over_tensor(
            jnp.concatenate(
                [
                    jnp.concatenate([left_qk.total(), left_vm.total()], axis=1),
                    jnp.concatenate([right_qk.total(), right_vm.total()], axis=1),
                ],
                axis=0,
            )
        )
        small_came, pixel_grad = meet((lo, hi), small_came, pixel_grad)
        advance(lo, hi)
        drain(lo, hi)
        small_kept, small_came = small_halves(small_kept + small_came, *halvings[2])
        expand_out, contract_out = finish_feed(feed_grads)
        small_came, expand_out, contract_out = meet((lo, hi), small_came, expand_out, contract_out)
        blocks = jnp.concatenate([lo.total(), hi.total()], axis=2)
        own = lambda d: lax.dynamic_index_in_dim(blocks, (index["tensor"] + d) % tensor, 0, keepdims=False)
        came = shifts(own)
        for axis, bit in halvings[3:]:
            small_kept, small_came = small_halves(small_kept + small_came, axis, bit)
        small_grads = small_kept + small_came
        grad_patch = sum([c.astype(F32) for c in came], own(0).astype(F32)).T.reshape(GROUPS, pix, thin)
        attention_out, merge_grad = finish_attention(grad_attention)
        small_grads = small_grads[0]
        mine = small_grads[:cut].reshape(n_vec, thin)
        return (
            block_output,
            pixel_grad,
            grad_patch,
            mine[:GROUPS],
            mine[GROUPS : GROUPS + 2],
            mine[GROUPS + 2 :],
            attention_out,
            small_grads[cut : cut + 2 * thin].reshape(2, thin),
            merge_grad,
            expand_out,
            small_grads[cut + 2 * thin :],
            contract_out,
        )

    return body


def solution(mesh):
    every = ("fsdp", "tensor")
    args = (
        P(every, None),
        P("fsdp"),
        P(every),
        P(every),
        P(None, None, every),
        P(None, every),
        P(None, every),
        P(None, every),
        P(None, "fsdp", "tensor"),
        P(None, ("tensor", "fsdp")),
        P("tensor", "fsdp"),
        P("fsdp", "tensor"),
        P(("tensor", "fsdp")),
        P("tensor", "fsdp"),
        P(every, None),
    )
    outs = (P(every, None), P(every, None)) + args[4:14]
    body = make_body(mesh.shape["fsdp"], mesh.shape["tensor"])
    return jax.shard_map(body, mesh=mesh, in_specs=args, out_specs=outs, check_vma=False)
```

```python
import math
from functools import partial

import jax
import jax.numpy as jnp
from jax import lax
from jax.experimental import pallas as pl
from jax.experimental.pallas import tpu as pltpu
from jax.sharding import PartitionSpec as P

HEAD_DIM = 64
GROUPS = 4
LANES = 128
TILE = 256
EPSILON = 1e-06
VMEM = 56 * 1024 * 1024
F32 = jnp.float32
BF16 = jnp.bfloat16
NN = (((1,), (0,)), ((), ()))
NT = (((1,), (1,)), ((), ()))
TN = (((0,), (0,)), ((), ()))
ANY = pl.BlockSpec(memory_space=pl.ANY)


def dot(left, right, dims=NN):
    return lax.dot_general(left, right, dims, preferred_element_type=F32)


def merged(block):
    return block.reshape(-1, block.shape[-1])


def joined(refs, *mats):
    blocks = [merged(ref[:, t, mat]) for ref in refs for t in range(ref.shape[1]) for mat in mats]
    return jnp.concatenate(blocks, axis=1)


def qkv_joined(refs, mat):
    blocks = [merged(ref[:, t, ref.shape[2] - 3 + mat]) for ref in refs for t in range(ref.shape[1])]
    return jnp.concatenate(blocks, axis=1)


def beside(refs):
    return jnp.concatenate([ref[...] for ref in refs], axis=1)


def normalize(values):
    row_mean = jnp.mean(values, axis=-1, keepdims=True)
    centred = values - row_mean
    inv_scale = lax.rsqrt(jnp.mean(centred * centred, axis=-1, keepdims=True) + EPSILON)
    return (centred * inv_scale, inv_scale)


def normalize_back(grad_normed, normed, inv_scale):
    return inv_scale * (
        grad_normed
        - jnp.mean(grad_normed, axis=-1, keepdims=True)
        - normed * jnp.mean(grad_normed * normed, axis=-1, keepdims=True)
    )


def whole(shape):
    return pl.BlockSpec(shape, lambda *_: (0,) * len(shape))


def row_tile(shape):
    return pl.BlockSpec((TILE,) + shape[1:], lambda i, *_: (i,) + (0,) * (len(shape) - 1))


def call(kernel, grid, in_specs, out_specs, out_shape, args, scratch=(), flops=0, exps=0, scalars=(), after=(), filled=()):
    count = len(args)
    after = tuple(after) + tuple(array for _, array in filled)
    first = len(scalars) + len(args) + len(after) - len(filled)

    def with_waits(*refs):
        head = refs[: len(scalars) + count]
        return kernel(*head, *refs[len(scalars) + count + len(after) :])

    moved = sum(a.size * a.dtype.itemsize for a in args) + sum(math.prod(s.shape) * s.dtype.itemsize for s in out_shape)
    return pl.pallas_call(
        with_waits,
        grid_spec=pltpu.PrefetchScalarGridSpec(
            num_scalar_prefetch=len(scalars),
            grid=grid,
            in_specs=list(in_specs) + [ANY] * len(after),
            out_specs=list(out_specs),
            scratch_shapes=list(scratch),
        ),
        out_shape=list(out_shape),
        input_output_aliases={first + i: out for i, (out, _) in enumerate(filled)},
        compiler_params=pltpu.CompilerParams(vmem_limit_bytes=VMEM),
        cost_estimate=pl.CostEstimate(flops=int(flops), bytes_accessed=int(moved), transcendentals=int(exps)),
    )(*scalars, *args, *after)


def shaped(shape, dtype):
    return jax.ShapeDtypeStruct(shape, dtype)


def split_kernel(core, array, out, *, wide):
    half = out.shape[1] // 2
    for place in range(half // wide):
        even = array[:, 2 * place * wide : (2 * place + 1) * wide]
        odd = array[:, (2 * place + 1) * wide : (2 * place + 2) * wide]
        at = place * wide
        out[:, at : at + wide] = jnp.where(core[0] == 0, even, odd)
        out[:, half + at : half + at + wide] = jnp.where(core[0] == 0, odd, even)


def turned_tile(shape):
    return pl.BlockSpec((shape[1], TILE), lambda i, *_: (0, i))


def split_columns(core, array, wide):
    tile = row_tile(array.shape)
    return call(
        partial(split_kernel, wide=wide),
        (array.shape[0] // TILE,),
        [tile],
        [tile],
        [shaped(array.shape, array.dtype)],
        (array,),
        scalars=(core,),
    )[0]


def shares_kernel(expand, contract, e_low, c_low, high):
    part = e_low.shape[1]
    e_low[...] = expand[:, :part]
    c_low[...] = contract[:part, :].T
    high[0] = expand[:, part:]
    high[1] = contract[part:, :].T


def shares(expand, contract, after=()):
    wide, unit = expand.shape
    half = (wide, unit // 2)
    return call(
        shares_kernel,
        (1,),
        [whole(expand.shape), whole(contract.shape)],
        [whole(half)] * 2 + [whole((2,) + half)],
        [shaped(half, BF16)] * 2 + [shaped((2,) + half, BF16)],
        (expand, contract),
        after=after,
    )


def output_kernel(core, *refs, wide):
    *parts, bias, out = refs
    half = out.shape[1] // 2
    total = sum(part[...].astype(F32) for part in parts) + bias[...]
    if wide % LANES:
        out[...] = total
        return
    for place in range(half // wide):
        at = place * wide
        own, other = total[:, at : at + wide], total[:, half + at : half + at + wide]
        out[:, 2 * at : 2 * at + wide] = jnp.where(core[0] == 0, own, other)
        out[:, 2 * at + wide : 2 * at + 2 * wide] = jnp.where(core[0] == 0, other, own)


def output_rows(core, parts, bias, wide, after=()):
    tile = row_tile(parts[0].shape)
    return call(
        partial(output_kernel, wide=wide),
        (parts[0].shape[0] // TILE,),
        [tile] * len(parts) + [whole(bias.shape)],
        [tile],
        [shaped(parts[0].shape, F32)],
        tuple(parts) + (bias,),
        scalars=(core,),
        after=after,
    )[0]


def finish_feed_kernel(low, high, expand, contract):
    part = low.shape[2]
    for at, ref in ((0, low), (part, high)):
        expand[:, at : at + part] = ref[0].astype(F32)
        contract[at : at + part, :] = ref[1].astype(F32).T


def finish_feed(low, high, after=()):
    _, wide, part = low.shape
    return call(
        finish_feed_kernel,
        (1,),
        [whole(low.shape)] * 2,
        [whole((wide, 2 * part)), whole((2 * part, wide))],
        [shaped((wide, 2 * part), F32), shaped((2 * part, wide), F32)],
        (low, high),
        after=after,
    )


def finish_attention_kernel(blocks, attention, merge_out):
    attention[...] = blocks[:3].astype(F32)
    merge_out[...] = blocks[3].astype(F32).T


def finish_attention(blocks):
    _, wide, columns = blocks.shape
    return call(
        finish_attention_kernel,
        (1,),
        [whole(blocks.shape)],
        [whole((3, wide, columns)), whole((columns, wide))],
        [shaped((3, wide, columns), F32), shaped((columns, wide), F32)],
        (blocks,),
    )


def marks_kernel(rows, columns):
    columns[...] = rows[...].T


def marks_of(*rows):
    count = rows[0].shape[0]
    rows = jnp.stack(rows + (jnp.zeros((count,), jnp.int32),) * (8 - len(rows))).astype(F32)
    columns = call(
        marks_kernel, (1,), [whole(rows.shape)], [whole((count, 8))], [shaped((count, 8), F32)], (rows,)
    )[0]
    return rows, columns


def group_rows(marks, group, values):
    return jnp.where(marks[:, 0:1] == jnp.asarray(group, F32), values, jnp.zeros_like(values))


def embed_kernel(present, pix, band, sin_own, cos_own, sin_came, cos_came, bias, gain, shift, lo_own, lo_came, hi_own, hi_came, stream, normed, acc):
    tile = pl.program_id(0)
    half = acc.shape[1] // 2
    width = pix.shape[1]
    acc[...] = beside((sin_own, cos_own, sin_came, cos_came))
    for group in range(GROUPS):

        @pl.when(present[tile * GROUPS + group] > 0)
        def _():
            rows = group_rows(band[...], group, pix[...])
            at = pl.ds((group % 2) * width, width)
            own, came = (lo_own, lo_came) if group < 2 else (hi_own, hi_came)
            acc[:, :half] += dot(rows, merged(own[:, :, at]), NT)
            acc[:, half:] += dot(rows, merged(came[:, :, at]), NT)

    total = acc[...]
    for group in range(GROUPS):
        total = total + jnp.where(band[:, 0:1] == float(group), bias[group : group + 1, :], 0.0)
    stream[...] = total
    normed[...] = (normalize(total)[0] * gain[...] + shift[...]).astype(BF16)


def embed(present, pixels, band, table, bias, gain, shift, patches, after=()):
    rows, model = pixels.shape[0], gain.shape[1]
    args = (pixels, band) + table + (bias, gain, shift) + patches
    specs = [row_tile(a.shape) for a in args[:6]] + [whole(a.shape) for a in args[6:]]
    return call(
        embed_kernel,
        (rows // TILE,),
        specs,
        [row_tile((rows, model))] * 2,
        [shaped((rows, model), F32), shaped((rows, model), BF16)],
        args,
        scratch=[pltpu.VMEM((TILE, model), F32)],
        flops=4 * rows * pixels.shape[1] * model,
        scalars=(present,),
        after=after,
    )


def project_kernel(x, bias, *refs):
    half = x.shape[1] // 2
    count = (len(refs) - 3) // 2
    weights, outs = refs[: 2 * count], refs[2 * count :]
    for mat, out in enumerate(outs):
        total = dot(x[:, :half], qkv_joined(weights[:count], mat)) + dot(x[:, half:], qkv_joined(weights[count:], mat))
        if mat != 1:
            total = total + bias[mat // 2 : mat // 2 + 1, :]
        out[...] = total.astype(BF16)


def project(x, own, came, bias, after=()):
    rows, model = x.shape
    width = bias.shape[1]
    weights = tuple(own) + tuple(came)
    return call(
        project_kernel,
        (rows // TILE,),
        [row_tile(x.shape), whole(bias.shape)] + [whole(w.shape) for w in weights],
        [row_tile((rows, width))] * 3,
        [shaped((rows, width), BF16)] * 3,
        (x, bias) + weights,
        flops=6 * rows * model * width,
        after=after,
    )


def head_mask(shape, head):
    lane = lax.broadcasted_iota(jnp.int32, shape, 1)
    return (lane < HEAD_DIM) if head == 0 else (lane >= HEAD_DIM)


def only_head(values, head):
    return jnp.where(head_mask(values.shape, head), values, jnp.zeros_like(values))


def attend_kernel(q_ref, k_ref, v_ref, seg_col_ref, seg_row_ref, out_ref, log_ref, bias_ref, *, base):
    pair = base + pl.program_id(0)
    rows = q_ref.shape[0]

    @pl.when(pl.program_id(0) == 0)
    def _():
        bias_ref[...] = jnp.where(seg_col_ref[:, 1:2] == seg_row_ref[1:2, :], 0.0, -1e30).astype(F32)
        log_ref[...] = jnp.zeros_like(log_ref)

    keys = k_ref[...]
    value_of = [only_head(v_ref[...], head) for head in range(2)]
    for start in range(0, rows, TILE):
        at = pl.ds(start, TILE)
        query = q_ref[at, :] * jnp.asarray(HEAD_DIM ** (-0.5), BF16)
        lane = lax.broadcasted_iota(jnp.int32, (TILE, LANES), 1)
        logs = log_ref[at, :]
        total = jnp.zeros((TILE, LANES), F32)
        for head in range(2):
            scores = dot(only_head(query, head), keys, NT) + bias_ref[at, :]
            top = jnp.max(scores, axis=1, keepdims=True)
            shifted = jnp.exp(scores - top)
            mass = jnp.sum(shifted, axis=1, keepdims=True)
            total = total + dot(shifted.astype(BF16), value_of[head]) * (1.0 / mass)
            logs = jnp.where(lane == 2 * pair + head, top + jnp.log(mass), logs)
        out_ref[at, :] = total.astype(BF16)
        log_ref[at, :] = logs


def attend(query, key, value, seg, base, skip, pairs, after=()):
    rows = query.shape[0]
    width = pairs * LANES
    block = pl.BlockSpec((rows, LANES), lambda i: (0, skip + i))
    return call(
        partial(attend_kernel, base=base + skip),
        (pairs,),
        [block, block, block, whole((rows, 8)), whole((8, rows))],
        [pl.BlockSpec((rows, LANES), lambda i: (0, i)), whole((rows, LANES))],
        [shaped((rows, width), BF16), shaped((rows, LANES), F32)],
        (query, key, value) + seg,
        scratch=[pltpu.VMEM((rows, rows), F32)],
        flops=16 * rows * rows * width,
        exps=rows * rows * width // HEAD_DIM,
        after=after,
    )


def attend_back_kernel(
    q_ref, k_ref, v_ref, g_ref, seg_col_ref, seg_row_ref, log_ref, delta_ref, dq_ref, dk_ref, dv_ref, sum_ref, bias_ref, acc_ref, *, base
):
    pair = base + pl.program_id(0)
    rows = q_ref.shape[0]

    @pl.when(pl.program_id(0) == 0)
    def _():
        bias_ref[...] = jnp.where(seg_col_ref[:, 1:2] == seg_row_ref[1:2, :], 0.0, -1e30).astype(F32)

    query = q_ref[...] * jnp.asarray(HEAD_DIM ** (-0.5), BF16)
    grads = g_ref[...]
    query_of = [only_head(query, head) for head in range(2)]
    grads_of = [only_head(grads, head) for head in range(2)]
    acc_ref[...] = jnp.zeros_like(acc_ref)
    value_sum = jnp.zeros((1, LANES), F32)
    for start in range(0, rows, TILE):
        at = pl.ds(start, TILE)
        keys = k_ref[at, :]
        values = v_ref[at, :]
        grad_key = jnp.zeros((TILE, LANES), F32)
        grad_value = jnp.zeros((TILE, LANES), F32)
        for head in range(2):
            key_h = only_head(keys, head)
            log_row = log_ref[pl.ds(2 * pair + head, 1), :]
            delta_row = delta_ref[pl.ds(2 * pair + head, 1), :]
            scores = dot(key_h, query, NT) + bias_ref[at, :]
            probs = jnp.exp(scores - log_row)
            grad_value = grad_value + dot(probs.astype(BF16), grads_of[head])
            grad_probs = dot(only_head(values, head), grads, NT)
            grad_scores = (probs * (grad_probs - delta_row)).astype(BF16)
            grad_key = grad_key + dot(grad_scores, query_of[head])
            acc_ref[...] += dot(key_h, grad_scores, TN)
        grad_value = grad_value.astype(BF16)
        dk_ref[at, :] = grad_key.astype(BF16)
        dv_ref[at, :] = grad_value
        value_sum = value_sum + jnp.sum(grad_value.astype(F32), axis=0, keepdims=True)
    grad_query = (acc_ref[...].T * HEAD_DIM ** (-0.5)).astype(BF16)
    dq_ref[...] = grad_query
    sum_ref[0:1, :] = jnp.sum(grad_query.astype(F32), axis=0, keepdims=True)
    sum_ref[1:2, :] = value_sum


def attend_back(query, key, value, grads, seg, log_rows, delta_rows, base, pairs, after=()):
    rows = query.shape[0]
    width = pairs * LANES
    taken = pl.BlockSpec((rows, LANES), lambda i: (0, base + i))
    given = pl.BlockSpec((rows, LANES), lambda i: (0, i))
    return call(
        partial(attend_back_kernel, base=base),
        (pairs,),
        [given] * 3 + [taken, whole((rows, 8)), whole((8, rows)), whole(log_rows.shape), whole(delta_rows.shape)],
        [given] * 3 + [pl.BlockSpec((2, LANES), lambda i: (0, i))],
        [shaped((rows, width), BF16)] * 3 + [shaped((2, width), F32)],
        (query, key, value, grads) + seg + (log_rows, delta_rows),
        scratch=[pltpu.VMEM((rows, rows), F32), pltpu.VMEM((LANES, rows), F32)],
        flops=40 * rows * rows * width,
        exps=rows * rows * width // HEAD_DIM,
        after=after,
    )


def merge_kernel(*refs, count):
    attended = beside(refs[:count])
    logs = sum(ref[...] for ref in refs[count : 2 * count])
    stream, bias, gain, shift, own_low, own_high, came_low, came_high = refs[2 * count : 2 * count + 8]
    stream_one, normed, log_rows = refs[2 * count + 8 :]
    log_rows[...] = logs.T
    half = stream.shape[1] // 2
    stream_one[:, :half] = stream[:, :half] + dot(attended, joined((own_low, own_high), 0, 1), NT)
    stream_one[:, half:] = stream[:, half:] + dot(attended, joined((came_low, came_high), 0, 1), NT)
    total = stream_one[...] + bias[...]
    stream_one[...] = total
    normed[...] = (normalize(total)[0] * gain[...] + shift[...]).astype(BF16)


def first_two(array):
    return pl.BlockSpec(array.shape[:2] + (2,) + array.shape[3:], lambda *_: (0,) * array.ndim)


def merge(attended, logs, stream, bias, gain, shift, weights, after=()):
    rows, model = stream.shape
    return call(
        partial(merge_kernel, count=len(attended)),
        (rows // TILE,),
        [row_tile(a.shape) for a in tuple(attended) + tuple(logs)]
        + [row_tile(stream.shape)]
        + [whole((1, model))] * 3
        + [first_two(a) for a in weights],
        [row_tile((rows, model))] * 2 + [turned_tile((rows, LANES))],
        [shaped((rows, model), F32), shaped((rows, model), BF16), shaped((LANES, rows), F32)],
        tuple(attended) + tuple(logs) + (stream, bias, gain, shift) + weights,
        flops=2 * rows * model * model,
        after=after,
    )


def gelu_parts(hidden):
    t = 1.0 / (1.0 + (0.3275911 * math.sqrt(0.5)) * jnp.abs(hidden))
    bell = jnp.exp(-0.5 * hidden * hidden)
    poly = t * (
        0.5 * 0.254829592
        + t * (-0.5 * 0.284496736 + t * (0.5 * 1.421413741 + t * (-0.5 * 1.453152027 + t * (0.5 * 1.061405429))))
    )
    tail = poly * bell
    below = jnp.where(hidden >= 0, 1.0 - tail, tail)
    return hidden * below, below + (hidden * (1.0 / math.sqrt(2.0 * math.pi))) * bell


def feed_kernel(x_ref, g_ref, e_own, e_other, c_own, c_other, b_ref, y_ref, d_ref, *refs):
    e_keep, e_send, c_keep, c_send, db_ref, a_ref, h_ref, y_sum, d_sum = refs
    step = pl.program_id(0)
    half = x_ref.shape[1] // 2

    @pl.when(step == 0)
    def _():
        y_sum[...] = jnp.zeros_like(y_sum)
        d_sum[...] = jnp.zeros_like(d_sum)

    expand = jnp.concatenate([merged(e_own[...]), merged(e_other[...])], axis=0)
    contract = jnp.concatenate([merged(c_own[...]), merged(c_other[...])], axis=0)
    hidden = dot(x_ref[...], expand) + b_ref[0]
    grad_active = dot(g_ref[...], contract)
    active, slope = gelu_parts(hidden)
    a_ref[...] = active.astype(BF16)
    grad_hidden = (grad_active * slope).astype(BF16)
    h_ref[...] = grad_hidden
    db_ref[0] = jnp.sum(grad_hidden.astype(F32), axis=0, keepdims=True)
    y_sum[...] += dot(a_ref[...], contract, NT)
    d_sum[...] += dot(h_ref[...], expand, NT)
    for side, (e_ref, c_ref) in enumerate(((e_keep, c_keep), (e_send, c_send))):
        cols = pl.ds(side * half, half)
        shape = e_ref.shape[:1] + e_ref.shape[2:]
        e_ref[:, 0] = dot(x_ref[:, cols], h_ref[...], TN).astype(BF16).reshape(shape)
        c_ref[:, 0] = dot(g_ref[:, cols], a_ref[...], TN).astype(BF16).reshape(shape)

    @pl.when(step == pl.num_programs(0) - 1)
    def _():
        y_ref[...] = y_sum[...].astype(BF16)
        d_ref[...] = d_sum[...].astype(BF16)


def feed(core, rows_two, top, weights, bias, base, steps, filled=(), after=()):
    rows, model = rows_two.shape
    blocks, _, part = bias.shape
    pairs, wide = weights[0].shape[0], weights[0].shape[-2]
    if len(weights) == 1:
        weights = weights * 4
        block = (pairs, 1, 1, 1, wide, part)
        place = lambda side, mat: lambda i, core: (0, core[0] if side == 0 else 1 - core[0], base + i, mat, 0, 0)
        specs = [pl.BlockSpec(block, place(side, mat)) for mat in range(2) for side in range(2)]
    else:
        specs = [pl.BlockSpec((pairs, 1, wide, part), lambda i, core: (0, base + i, 0, 0))] * 4
    grad = pl.BlockSpec((pairs, 1, wide, part), lambda i, core: (0, base + i, 0, 0))
    unit = pl.BlockSpec((1, 1, part), lambda i, core: (base + i, 0, 0))
    return call(
        lambda core, *refs: feed_kernel(*refs),
        (steps,),
        [whole((rows, model))] * 2 + specs + [unit],
        [whole((rows, model))] * 2 + [grad] * 4 + [unit],
        [shaped((rows, model), BF16)] * 2
        + [shaped((pairs, blocks, wide, part), BF16)] * 4
        + [shaped((blocks, 1, part), F32)],
        (rows_two, top) + tuple(weights) + (bias,),
        scratch=[pltpu.VMEM((rows, part), BF16)] * 2 + [pltpu.VMEM((rows, model), F32)] * 2,
        flops=12 * rows * model * part * steps,
        exps=rows * part * steps,
        scalars=(core,),
        after=after,
        filled=[(2 + i, array) for i, array in enumerate(filled)],
    )


def merge_back_kernel(*refs, count, parts):
    attended = beside(refs[:count])
    grad_two = sum(ref[...].astype(F32) for ref in refs[count : count + parts])
    refs = refs[count + parts :]
    top, stream_one, gain, own_low, own_high, came_low, came_high, heads = refs[:8]
    grad_stream, branch, grad_attended, delta, sums = refs[8:]
    half = top.shape[1] // 2
    normed, scale = normalize(stream_one[...])
    cotangent = top[...].astype(F32)
    total = cotangent + normalize_back(grad_two * gain[...], normed, scale)
    grad_stream[...] = total
    low = total.astype(BF16)
    branch[...] = low
    grads = dot(low[:, :half], joined((own_low, own_high), 0, 1)) + dot(low[:, half:], joined((came_low, came_high), 0, 1))
    grads = grads.astype(BF16)
    grad_attended[...] = grads
    both = grads.astype(F32) * attended.astype(F32)
    high = both.astype(BF16)
    delta[...] = dot(heads[...], high, NT) + dot(heads[...], (both - high.astype(F32)).astype(BF16), NT)

    @pl.when(pl.program_id(0) == 0)
    def _():
        sums[...] = jnp.zeros_like(sums)

    for row, part in enumerate((grad_two * normed, grad_two, total, cotangent)):
        sums[row : row + 1, :] += jnp.sum(part, axis=0, keepdims=True)


def merge_back(attended, grads, top, stream_one, gain, weights, heads, after=()):
    rows, model = stream_one.shape
    tile = row_tile((rows, model))
    return call(
        partial(merge_back_kernel, count=len(attended), parts=len(grads)),
        (rows // TILE,),
        [row_tile(a.shape) for a in attended]
        + [tile] * (len(grads) + 2)
        + [whole((1, model))]
        + [first_two(a) for a in weights]
        + [whole(heads.shape)],
        [tile] * 3
        + [pl.BlockSpec((heads.shape[0], TILE), lambda i: (0, i)), whole((8, model))],
        [
            shaped((rows, model), F32),
            shaped((rows, model), BF16),
            shaped((rows, model), BF16),
            shaped((heads.shape[0], rows), F32),
            shaped((8, model), F32),
        ],
        tuple(attended) + tuple(grads) + (top, stream_one, gain) + weights + (heads,),
        flops=2 * rows * model * model,
        after=after,
    )


def attention_grads_kernel(*refs, count):
    x, branch, xt, bt = refs[0], refs[1], refs[-2], refs[-1]
    xt[...] = x[...].T
    bt[...] = branch[...].T
    inputs = [beside(refs[2 + i * count : 2 + (i + 1) * count]) for i in range(3)]
    inputs.append(beside(refs[2 + 3 * count : -6]))
    outs = refs[-6:-2]
    half = xt.shape[0] // 2
    blocks, steps, _, wide, columns = outs[0].shape
    for place, right in enumerate(inputs):
        left = bt if place == 3 else xt
        for side in range(2):
            ref = outs[2 * (place // 2) + side]
            grad = dot(left[pl.ds(side * half, half), :], right).astype(BF16)
            for step in range(steps):
                part = grad[:, step * columns : (step + 1) * columns]
                ref[:, step, place % 2] = part.reshape(blocks, wide, columns)


def attention_grads(x, branch, query, key, value, attended, blocks, columns, after=()):
    rows, model = x.shape
    count = len(query)
    width = sum(a.shape[1] for a in query)
    shape = (blocks, width // columns, 2, model // (2 * blocks), columns)
    args = (x, branch) + tuple(query) + tuple(key) + tuple(value) + tuple(attended)
    return call(
        partial(attention_grads_kernel, count=count),
        (1,),
        [whole(a.shape) for a in args],
        [whole(shape)] * 4,
        [shaped(shape, BF16)] * 4,
        args,
        scratch=[pltpu.VMEM((model, rows), BF16)] * 2,
        flops=8 * rows * model * width,
        after=after,
    )


def project_back_kernel(*refs, count):
    grads = [beside(refs[i * count : (i + 1) * count]) for i in range(3)]
    rest = refs[3 * count :]
    grad_stream, stream, band, gain = rest[:4]
    weights = rest[4:-3]
    grad_embed, sums, acc = rest[-3:]
    half = stream.shape[1] // 2
    each = len(weights) // 2
    for side in range(2):
        held = weights[side * each : (side + 1) * each]
        acc[:, side * half : (side + 1) * half] = sum(
            dot(grad, qkv_joined(held, mat), NT) for mat, grad in enumerate(grads)
        )
    grad_one = acc[...]
    normed, scale = normalize(stream[...])
    total = grad_stream[...] + normalize_back(grad_one * gain[...], normed, scale)
    grad_embed[...] = total.astype(BF16)

    @pl.when(pl.program_id(0) == 0)
    def _():
        sums[...] = jnp.zeros_like(sums)

    parts = [group_rows(band[...], group, total) for group in range(GROUPS)] + [grad_one * normed, grad_one]
    for row, part in enumerate(parts):
        sums[row : row + 1, :] += jnp.sum(part, axis=0, keepdims=True)


def project_back(query, key, value, grad_stream, stream, band, gain, weights, after=()):
    rows, model = stream.shape
    tile = row_tile((rows, model))
    parts = tuple(query) + tuple(key) + tuple(value)
    return call(
        partial(project_back_kernel, count=len(query)),
        (rows // TILE,),
        [row_tile(a.shape) for a in parts]
        + [tile] * 2
        + [row_tile(band.shape), whole((1, model))]
        + [whole(a.shape) for a in weights],
        [tile, whole((8, model))],
        [shaped((rows, model), BF16), shaped((8, model), F32)],
        parts + (grad_stream, stream, band, gain) + weights,
        scratch=[pltpu.VMEM((TILE, model), F32)],
        flops=6 * rows * model * model,
        after=after,
    )


def patch_grads_kernel(present, grads, pix, band, lo_keep, lo_send, hi_keep, hi_send, acc):
    group = pl.program_id(0)
    half = grads.shape[1] // 2
    acc[...] = jnp.zeros_like(acc)
    for tile in range(pix.shape[0] // TILE):

        @pl.when(present[tile * GROUPS + group] > 0)
        def _():
            at = pl.ds(tile * TILE, TILE)
            acc[...] += dot(grads[at, :], group_rows(band[at, :], group, pix[at, :]), TN)

    for place, (keep, send) in enumerate(((lo_keep, lo_send), (hi_keep, hi_send))):

        @pl.when(group // 2 == place)
        def _():
            keep[...] = acc[:half, :].astype(BF16)
            send[...] = acc[half:, :].astype(BF16)


def patch_grads(present, grads, pixels, band, after=()):
    rows, model = grads.shape
    width = pixels.shape[1]
    count = GROUPS // 2
    low = pl.BlockSpec((model // 2, width), lambda i, present: (0, jnp.minimum(i, count - 1)))
    high = pl.BlockSpec((model // 2, width), lambda i, present: (0, jnp.maximum(i - count, 0)))
    return call(
        patch_grads_kernel,
        (GROUPS,),
        [whole(grads.shape), whole(pixels.shape), whole(band.shape)],
        [low, low, high, high],
        [shaped((model // 2, count * width), BF16)] * 4,
        (grads, pixels, band),
        scratch=[pltpu.VMEM((model, width), F32)],
        flops=4 * rows * width * model,
        scalars=(present,),
        after=after,
    )


def pixel_grads_kernel(present, grads, band, lo_own, lo_came, hi_own, hi_came, out):
    tile = pl.program_id(0)
    half = grads.shape[1] // 2
    width = out.shape[1]
    out[...] = jnp.zeros_like(out)
    for group in range(GROUPS):

        @pl.when(present[tile * GROUPS + group] > 0)
        def _():
            at = pl.ds((group % 2) * width, width)
            own, came = (lo_own, lo_came) if group < 2 else (hi_own, hi_came)
            spread = dot(grads[:, :half], merged(own[:, :, at])) + dot(grads[:, half:], merged(came[:, :, at]))
            out[...] = jnp.where(band[:, 0:1] == float(group), spread, out[...])


def pixel_grads(present, grads, band, patches, width, after=()):
    rows, model = grads.shape
    return call(
        pixel_grads_kernel,
        (rows // TILE,),
        [row_tile(grads.shape), row_tile(band.shape)] + [whole(a.shape) for a in patches],
        [row_tile((rows, width))],
        [shaped((rows, width), F32)],
        (grads, band) + patches,
        flops=4 * rows * width * model,
        scalars=(present,),
        after=after,
    )[0]


def make_body(fsdp, tensor):
    pairs = fsdp // 2
    t_bits = list(range(tensor.bit_length() - 1))
    f_bits = list(range(1, fsdp.bit_length() - 1))
    up, down = f_bits, f_bits[::-1]

    def swap(array, axis, bit):
        size = fsdp if axis == "fsdp" else tensor
        return lax.ppermute(array, axis, [(i, i ^ (1 << bit)) for i in range(size)])

    def body(
        pixels,
        segment,
        band_group,
        scaled_position,
        patch_weight,
        patch_bias,
        norm_gains,
        vector_biases,
        attention_weight,
        query_value_bias,
        merge_weight,
        expand_weight,
        expand_bias,
        contract_weight,
        cotangent,
    ):
        index = {"fsdp": lax.axis_index("fsdp"), "tensor": lax.axis_index("tensor")}
        core = index["fsdp"] & 1
        rows, pix = pixels.shape
        model = cotangent.shape[1]
        thin = patch_bias.shape[1]
        wide = model // fsdp
        unit = expand_weight.shape[1]
        half_unit = unit // 2
        segment = lax.dynamic_slice_in_dim(segment, index["tensor"] * rows, rows)

        def wider(array, came, axis, bit):
            dim = 0 if axis == "tensor" else len(f_bits) - bit
            mine = ((index[axis] >> bit) & 1) == 1
            return jnp.where(
                mine, jnp.concatenate([came, array], axis=dim), jnp.concatenate([array, came], axis=dim)
            )

        def shifts(make):
            count = tensor
            return [
                lax.ppermute(make(d), "tensor", [(i, (i + d) % count) for i in range(count)]) for d in range(1, count)
            ]

        def in_order(array, came):
            parts = jnp.stack([array] + came)[::-1]
            return lax.dynamic_slice_in_dim(jnp.concatenate([parts, parts]), tensor - 1 - index["tensor"], tensor)

        def open_f(array):
            return array.reshape((1,) * len(f_bits) + array.shape)

        def close_f(array):
            return array.reshape((pairs,) + array.shape[len(f_bits) :])

        def other_core(array):
            return swap(array, "fsdp", 0)

        class Pair:
            def __init__(self, one, two):
                self.held = [open_f(one), open_f(two)]
                self.todo = list(zip(up, down))

            def send(self):
                self.bits = self.todo.pop(0)
                return [swap(a, "fsdp", bit) for a, bit in zip(self.held, self.bits)]

            def take(self, came):
                self.held = [wider(a, c, "fsdp", bit) for a, c, bit in zip(self.held, came, self.bits)]

            def drain(self):
                while self.todo:
                    self.take(self.send())

            def closed(self):
                return [close_f(a) for a in self.held]

        def half_sum(keep, came, at, bit):
            dim = len(f_bits) - bit
            take = lambda array: lax.dynamic_slice_in_dim(array, at, 1, axis=dim)
            return (take(keep).astype(F32) + take(came).astype(F32)).astype(keep.dtype)

        class Sum:
            def __init__(self, keep, send, bits):
                self.keep, self.todo = unfold(keep), list(bits)
                self.came = unfold(swap(send, "fsdp", 0))

            def step(self):
                bit = self.todo.pop(0)
                mine = (index["fsdp"] >> bit) & 1
                self.sent = half_sum(self.keep, self.came, 1 - mine, bit)
                self.keep = half_sum(self.keep, self.came, mine, bit)
                self.came = swap(self.sent, "fsdp", bit)
                return self.sent

            def total(self):
                while self.todo:
                    self.step()
                return last_sum(self.keep, self.came)

        def unfold(array):
            return array.reshape((2,) * len(f_bits) + array.shape[1:])

        def last_sum(keep, came):
            rest = keep.shape[len(f_bits) :]
            return (keep.astype(F32) + came.astype(F32)).astype(keep.dtype).reshape(rest)

        def over_tensor(blocks):
            return lax.psum_scatter(blocks, "tensor", scatter_dimension=0, tiled=False)

        def to_split(array):
            parts = array.reshape(array.shape[0], pairs, 2, wide)
            even, odd = (parts[:, :, i].reshape(array.shape[0], -1) for i in range(2))
            return jnp.where(core == 0, jnp.concatenate([even, odd], axis=1), jnp.concatenate([odd, even], axis=1))

        def from_split(array):
            parts = array.reshape(array.shape[0], 2, pairs, wide)
            mine, other = parts[:, 0], parts[:, 1]
            parts = jnp.where(core == 0, jnp.stack([mine, other], axis=2), jnp.stack([other, mine], axis=2))
            return parts.reshape(array.shape)

        tie = lambda array, *others: lax.optimization_barrier((array,) + others)[0]
        core_at = core[None].astype(jnp.int32)
        aligned = wide % LANES == 0

        sync = lax.optimization_barrier
        n_vec = GROUPS + 2 + 4
        cut = n_vec * thin
        columns = (GROUPS // 2) * pix
        rest_up, rest_down = up[1:], down[1:]

        small = jnp.concatenate(
            [patch_bias, norm_gains, vector_biases, query_value_bias, expand_bias.reshape(-1, thin)], axis=0
        )
        extra = small.shape[0]
        small = jnp.pad(lax.optimization_barrier(small).T, ((0, 0), (0, LANES - extra)))
        patch = jnp.concatenate([patch_weight.reshape(-1, thin).T, small], axis=1)
        attention = jnp.concatenate([attention_weight, merge_weight.T[None]], axis=0)[None]
        t_first, t_rest = t_bits[:1], t_bits[1:]

        def over_t(array, came, bits):
            for i, bit in enumerate(bits):
                array = wider(array, came if i == 0 else swap(array, "tensor", bit), "tensor", bit)
            return array

        def start_t(bits, *arrays):
            return [swap(a, "tensor", bits[0]) for a in arrays]

        def go(*pairs):
            return [p.send() if p.todo else None for p in pairs]

        def done(came, *pairs):
            for c, p in zip(came, pairs):
                if c is not None:
                    p.take(c)

        def both_cores(pair):
            held = pair.closed()
            return held, [other_core(a) for a in held]

        present = jnp.any(band_group.reshape(-1, TILE, 1) == jnp.arange(GROUPS), axis=1).astype(jnp.int32).reshape(-1)
        came = shifts(lambda d: patch)
        e_one, c_one, feed_high = shares(expand_weight, contract_weight)
        e_one, c_one = e_one[None], c_one[None]
        mark_rows, band = marks_of(band_group, segment)
        seg = (band, mark_rows)
        came, patch, attention, cotangent, e_one, band, present, seg = sync(
            (came, patch, attention, cotangent, e_one, band, present, seg)
        )
        patch = in_order(patch, came).reshape(tensor * thin, -1)
        patch = Pair(patch[:, :columns], patch[:, columns:])
        came = go(patch)
        came_t = start_t(t_first, attention)
        if aligned:
            top = split_columns(core_at, cotangent, wide)
        else:
            top = to_split(cotangent)
        came, came_t, top, e_one, c_one, scaled_position = sync((came, came_t, top, e_one, c_one, scaled_position))
        done(came, patch)
        attention = over_t(attention, came_t[0], t_first)
        came = go(patch)
        came_t = start_t(t_rest, attention) + start_t(t_first, e_one, c_one)
        half_width = model // 2
        column = jnp.arange(model)
        place = column % half_width
        natural = (2 * (place // wide) + (core ^ (column // half_width))) * wide + place % wide
        rates = jnp.exp((natural % half_width).astype(F32) * (-math.log(10000.0) / half_width))
        angles = scaled_position.astype(F32)[:, None] * rates[None, :]
        quarter = model // 4
        table = tuple(
            f(angles[:, i * quarter : (i + 1) * quarter]) for i, f in enumerate((jnp.sin, jnp.cos, jnp.sin, jnp.cos))
        )
        hidden = jnp.arange(model)
        owner, block = hidden // thin % fsdp, hidden // (thin * fsdp)
        source = ((((owner & 1) ^ core) * pairs + owner // 2) * tensor + block) * thin + hidden % thin
        to_hidden = (hidden[:, None] == source[None, :]).astype(BF16)
        came, came_t, table, to_hidden = sync((came, came_t, table, to_hidden))
        done(came, patch)
        patch.drain()
        attention = over_t(attention, came_t[0], t_rest)
        e_one, c_one = (over_t(w, c, t_first) for w, c in zip((e_one, c_one), came_t[1:]))
        quarter, half_t = tensor // 4, tensor // 2
        outward = [
            attention[i * half_t : (i + 1) * half_t, 3].reshape(quarter, 2, wide, -1) for i in range(2)
        ]
        qkv = [attention[i * quarter : (i + 1) * quarter, :3] for i in range(4)]
        qkv_one = Pair(*qkv[:2])
        qkv_two = Pair(*(jnp.concatenate(two, axis=1) for two in zip(outward, qkv[2:])))
        patch = both_cores(patch)
        came, came_t = go(qkv_one), start_t(t_rest, e_one)
        patch, came, came_t, c_one, band = sync((patch, came, came_t, c_one, band))
        patches = (patch[0][0], patch[1][0], patch[0][1], patch[1][1])
        done(came, qkv_one)
        e_one = over_t(e_one, came_t[0], t_rest)
        came, came_t = go(qkv_one), start_t(t_rest, c_one)
        small = [held[0] for held in (patch[0][1:], patch[1][1:])]
        small = jnp.stack([held[:, :, columns : columns + extra] for held in small]).astype(F32)
        vectors = small.reshape(model, extra).T
        patch_bias_rows = vectors[:GROUPS]
        gains = [vectors[GROUPS + i : GROUPS + i + 1] for i in range(2)]
        biases = [vectors[GROUPS + 2 + i : GROUPS + 3 + i] for i in range(4)]
        by_hidden = dot(vectors[n_vec:].astype(BF16), to_hidden)
        qv_rows = by_hidden[:2]

        stream_zero, input_one = embed(
            present, pixels, band, table, patch_bias_rows, gains[0], biases[0], patches
        )
        came, came_t, input_one, qkv_two.held = sync((came, came_t, input_one, qkv_two.held))
        done(came, qkv_one)
        qkv_one.drain()
        c_one = over_t(c_one, came_t[0], t_rest)
        feed_one = Pair(e_one, c_one)
        one, came = both_cores(qkv_one), go(qkv_two)
        one, came, input_one, feed_one.held = sync((one, came, input_one, feed_one.held))
        done(came, qkv_two)
        came = go(qkv_two)
        heads_width = model // 2
        each = heads_width // LANES
        first = project(input_one, *one, qv_rows[:, :heads_width])
        attended, logs = [None] * 3, [None] * 3
        attended[0], logs[0] = attend(*first, seg, 0, 0, each // 2)
        came, attended[0], feed_high = sync((came, attended[0], feed_high))
        feed_high = lax.all_gather(feed_high, ("fsdp", "tensor"), axis=0, tiled=False)
        feed_high = feed_high.reshape(pairs, 2, tensor, 2, wide, half_unit)
        done(came, qkv_two)
        qkv_two.drain()
        two, came = both_cores(qkv_two), go(feed_one)
        attended[1], logs[1] = attend(*first, seg, 0, each // 2, each // 2, after=(attended[0],))
        two, came, attended[1], input_one = sync((two, came, attended[1], input_one))
        done(came, feed_one)
        came = go(feed_one)
        last = project(input_one, *two, qv_rows[:, heads_width:])
        attended[2], logs[2] = attend(*last, seg, each, 0, each)
        came, attended[2] = sync((came, attended[2]))
        done(came, feed_one)
        feed_one.drain()
        feed_one = both_cores(feed_one)
        outward = tuple(two[0] + two[1])
        stream_one, input_two, log_rows = merge(
            attended, logs, stream_zero, biases[1], gains[1], biases[2], outward
        )
        feed_one, input_two, by_hidden = sync((feed_one, input_two, by_hidden))
        unit_bias = by_hidden[2:].reshape(-1, tensor, fsdp, thin).transpose(1, 2, 0, 3).reshape(tensor, 2, 1, half_unit)

        rows_two = (input_two, top)
        def meet(sums, *arrays):
            waited = sync(([t.came for t in sums],) + arrays)
            for t, came in zip(sums, waited[0]):
                t.came = came
            return waited[1] if len(arrays) == 1 else waited[1:]

        def advance(*sums):
            return [t.step() if t.todo else t.came for t in sums]

        def drain(*sums):
            for t in sums:
                while t.todo:
                    t.step()

        weights = tuple(a for pair in zip(*feed_one) for a in pair)
        y_low, d_low, *grads_low, units_low = feed(core_at, *rows_two, weights, unit_bias[:, 0], 0, tensor)
        low = [Sum(grads_low[0], grads_low[1], down), Sum(grads_low[2], grads_low[3], up)]
        share = max(1, tensor // 4)
        y_mid, d_mid, *grads_mid, units_mid = feed(
            core_at, *rows_two, (feed_high,), unit_bias[:, 1], 0, share, after=(y_low,)
        )
        y_mid = meet(low, y_mid)
        y_high, d_high, *grads_high, units_high = feed(
            core_at,
            *rows_two,
            (feed_high,),
            unit_bias[:, 1],
            share,
            tensor - share,
            filled=grads_mid + [units_mid],
            after=[y_mid] + advance(*low),
        )
        y_high, *grads_high = meet(low, y_high, *grads_high)
        high = [Sum(grads_high[0], grads_high[1], down), Sum(grads_high[2], grads_high[3], up)]
        unit_grads = [units_low, units_high]
        outs = [y_low, y_mid, y_high]

        heads = model // HEAD_DIM
        head_rows = (jnp.arange(heads)[:, None] == jnp.arange(model)[None, :] // HEAD_DIM).astype(BF16)
        grad_stream_one, grad_branch, grad_attended, delta, sums_two = merge_back(
            attended, [d_low, d_mid, d_high], top, stream_one, gains[1], outward, head_rows, after=advance(*low)
        )
        grad_attended = meet(low + high, grad_attended)
        back = lambda i, after: attend_back(
            *(first, last)[i], grad_attended, seg, log_rows, delta, i * each, each, after=after
        )

        def grads_of(part, which, after):
            return attention_grads(
                input_one, grad_branch, *([p] for p in part[:3]), attended[2 * which : 2 + which], pairs, model // tensor, after=after
            )

        first_part = back(0, advance(*high))
        drain(*low)
        low_blocks = jnp.stack([t.total() for t in low], axis=1)
        feed_grads_low = over_tensor(low_blocks)
        left = meet(high, grads_of(first_part, 0, (low_blocks,)))
        waits = advance(*high)
        left_qk, left_vm = Sum(left[0], left[1], down), Sum(left[2], left[3], up)
        second_part = back(1, waits)
        second_part = meet(high + [left_qk, left_vm], second_part)
        drain(*high)
        feed_blocks = jnp.stack([t.total() for t in high], axis=1)
        feed_grads_high = over_tensor(feed_blocks)
        right = grads_of(second_part, 1, advance(left_qk, left_vm) + [feed_blocks])
        right = meet((left_qk, left_vm), right)
        waits = advance(left_qk, left_vm)
        right_qk, right_vm = Sum(right[0], right[1], down), Sum(right[2], right[3], up)
        parts = (first_part, second_part)
        grad_query, grad_key, grad_value = ([p[i] for p in parts] for i in range(3))
        grad_qv = jnp.concatenate([p[3] for p in parts], axis=1)
        grad_embed, sums_one = project_back(
            grad_query, grad_key, grad_value, grad_stream_one, stream_zero, band, gains[0], tuple(one[0] + two[0] + one[1] + two[1]), after=waits
        )
        grad_embed = meet((left_qk, left_vm, right_qk, right_vm), grad_embed)

        waits = advance(right_qk, right_vm)
        shape = (pairs, tensor, thin, columns)
        patch_kept = meet((right_qk, right_vm), patch_grads(present, grad_embed, pixels, band, after=waits))
        lo = Sum(*(a.reshape(shape) for a in patch_kept[:2]), up)
        hi = Sum(*(a.reshape(shape) for a in patch_kept[2:]), down)

        vector_grads = from_split(
            jnp.concatenate(
                [sums_one[:GROUPS], sums_one[GROUPS : GROUPS + 1], sums_two[0:1], sums_one[GROUPS + 1 : GROUPS + 2]]
                + [sums_two[2:3], sums_two[1:2], sums_two[3:4]],
                axis=0,
            )
        )
        vector_grads = vector_grads.reshape(n_vec, fsdp * tensor, thin).transpose(1, 0, 2).reshape(fsdp, tensor, cut)
        hidden_grads = jnp.concatenate(
            [
                grad_qv.reshape(2, tensor, fsdp, thin).transpose(2, 1, 0, 3).reshape(fsdp, tensor, 2 * thin),
                jnp.stack(unit_grads, axis=1).reshape(tensor, fsdp, unit // fsdp).transpose(1, 0, 2),
            ],
            axis=2,
        )
        small_grads = jnp.concatenate([vector_grads, hidden_grads], axis=2).reshape(fsdp * tensor, -1)
        small_grads = small_grads.reshape((2,) * (len(f_bits) + 1 + len(t_bits)) + (-1,))

        def small_halves(array, axis, bit):
            dim = (len(f_bits) - bit) if axis == "fsdp" else len(f_bits) + len(t_bits) - bit
            mine = (index[axis] >> bit) & 1
            take = lambda at: lax.dynamic_slice_in_dim(array, at, 1, axis=dim)
            return take(mine), swap(take(1 - mine), axis, bit)

        def small_steps(kept, came, axis, bits):
            for bit in bits:
                kept, came = small_halves(kept + came, axis, bit)
            return kept, came

        small_kept, small_came = small_halves(small_grads, "fsdp", 0)
        waits = advance(right_qk, right_vm)
        small_came = meet((lo, hi), small_came)
        waits += advance(lo, hi)
        small_kept, small_came = small_steps(small_kept, small_came, "tensor", t_bits)
        block_output = output_rows(core_at, [stream_one] + outs, biases[3], wide, after=waits)
        if not aligned:
            block_output = from_split(block_output)
        pixel_grad = pixel_grads(present, grad_embed, band, patches, pix, after=[block_output])
        small_came, pixel_grad = meet((lo, hi, left_qk, left_vm, right_qk, right_vm), small_came, pixel_grad)
        advance(lo, hi)
        small_kept, small_came = small_steps(small_kept, small_came, "fsdp", f_bits)
        drain(lo, hi, left_qk, left_vm, right_qk, right_vm)
        grad_attention = over_tensor(
            jnp.concatenate(
                [
                    jnp.concatenate([left_qk.total(), left_vm.total()], axis=1),
                    jnp.concatenate([right_qk.total(), right_vm.total()], axis=1),
                ],
                axis=0,
            )
        )
        small_came = meet((lo, hi), small_came)
        blocks = jnp.concatenate([lo.total(), hi.total()], axis=2)
        expand_out, contract_out = finish_feed(feed_grads_low, feed_grads_high, after=[blocks])
        own = lambda d: lax.dynamic_index_in_dim(blocks, (index["tensor"] + d) % tensor, 0, keepdims=False)
        came = shifts(own)
        small_grads = (small_kept + small_came).reshape(1, -1)
        grad_patch = sum([c.astype(F32) for c in came], own(0).astype(F32)).T.reshape(GROUPS, pix, thin)
        attention_out, merge_grad = finish_attention(grad_attention)
        small_grads = small_grads[0]
        mine = small_grads[:cut].reshape(n_vec, thin)
        return (
            block_output,
            pixel_grad,
            grad_patch,
            mine[:GROUPS],
            mine[GROUPS : GROUPS + 2],
            mine[GROUPS + 2 :],
            attention_out,
            small_grads[cut : cut + 2 * thin].reshape(2, thin),
            merge_grad,
            expand_out,
            small_grads[cut + 2 * thin :],
            contract_out,
        )

    return body


def solution(mesh):
    every = ("fsdp", "tensor")
    args = (
        P(every, None),
        P("fsdp"),
        P(every),
        P(every),
        P(None, None, every),
        P(None, every),
        P(None, every),
        P(None, every),
        P(None, "fsdp", "tensor"),
        P(None, ("tensor", "fsdp")),
        P("tensor", "fsdp"),
        P("fsdp", "tensor"),
        P(("tensor", "fsdp")),
        P("tensor", "fsdp"),
        P(every, None),
    )
    outs = (P(every, None), P(every, None)) + args[4:14]
    body = make_body(mesh.shape["fsdp"], mesh.shape["tensor"])
    return jax.shard_map(body, mesh=mesh, in_specs=args, out_specs=outs, check_vma=False)
```

```python
import math
from functools import partial

import jax
import jax.numpy as jnp
from jax import lax
from jax.experimental import pallas as pl
from jax.experimental.pallas import tpu as pltpu
from jax.sharding import PartitionSpec as P

HEAD_DIM = 64
GROUPS = 4
LANES = 128
TILE = 256
LONG = 512
EPSILON = 1e-06
VMEM = 56 * 1024 * 1024
F32 = jnp.float32
BF16 = jnp.bfloat16
NN = (((1,), (0,)), ((), ()))
NT = (((1,), (1,)), ((), ()))
TN = (((0,), (0,)), ((), ()))
ANY = pl.BlockSpec(memory_space=pl.ANY)


def dot(left, right, dims=NN):
    return lax.dot_general(left, right, dims, preferred_element_type=F32)


def merged(block):
    return block.reshape(-1, block.shape[-1])


def joined(refs, *mats):
    blocks = [merged(ref[:, t, mat]) for ref in refs for t in range(ref.shape[1]) for mat in mats]
    return jnp.concatenate(blocks, axis=1)


def qkv_joined(refs, mat):
    blocks = [merged(ref[:, t, ref.shape[2] - 3 + mat]) for ref in refs for t in range(ref.shape[1])]
    return jnp.concatenate(blocks, axis=1)


def beside(refs):
    return jnp.concatenate([ref[...] for ref in refs], axis=1)


def normalize(values):
    row_mean = jnp.mean(values, axis=-1, keepdims=True)
    centred = values - row_mean
    inv_scale = lax.rsqrt(jnp.mean(centred * centred, axis=-1, keepdims=True) + EPSILON)
    return (centred * inv_scale, inv_scale)


def normalize_back(grad_normed, normed, inv_scale):
    return inv_scale * (
        grad_normed
        - jnp.mean(grad_normed, axis=-1, keepdims=True)
        - normed * jnp.mean(grad_normed * normed, axis=-1, keepdims=True)
    )


def whole(shape):
    return pl.BlockSpec(shape, lambda *_: (0,) * len(shape))


def row_tile(shape, tile=TILE):
    return pl.BlockSpec((tile,) + shape[1:], lambda i, *_: (i,) + (0,) * (len(shape) - 1))


def call(kernel, grid, in_specs, out_specs, out_shape, args, scratch=(), flops=0, exps=0, scalars=(), after=(), filled=()):
    count = len(args)
    after = tuple(after) + tuple(array for _, array in filled)
    first = len(scalars) + len(args) + len(after) - len(filled)

    def with_waits(*refs):
        head = refs[: len(scalars) + count]
        return kernel(*head, *refs[len(scalars) + count + len(after) :])

    moved = sum(a.size * a.dtype.itemsize for a in args) + sum(math.prod(s.shape) * s.dtype.itemsize for s in out_shape)
    return pl.pallas_call(
        with_waits,
        grid_spec=pltpu.PrefetchScalarGridSpec(
            num_scalar_prefetch=len(scalars),
            grid=grid,
            in_specs=list(in_specs) + [ANY] * len(after),
            out_specs=list(out_specs),
            scratch_shapes=list(scratch),
        ),
        out_shape=list(out_shape),
        input_output_aliases={first + i: out for i, (out, _) in enumerate(filled)},
        compiler_params=pltpu.CompilerParams(vmem_limit_bytes=VMEM),
        cost_estimate=pl.CostEstimate(flops=int(flops), bytes_accessed=int(moved), transcendentals=int(exps)),
    )(*scalars, *args, *after)


def shaped(shape, dtype):
    return jax.ShapeDtypeStruct(shape, dtype)


def split_kernel(core, array, out, *, wide):
    half = out.shape[1] // 2
    for place in range(half // wide):
        even = array[:, 2 * place * wide : (2 * place + 1) * wide]
        odd = array[:, (2 * place + 1) * wide : (2 * place + 2) * wide]
        at = place * wide
        out[:, at : at + wide] = jnp.where(core[0] == 0, even, odd)
        out[:, half + at : half + at + wide] = jnp.where(core[0] == 0, odd, even)


def turned_tile(shape, tile=TILE):
    return pl.BlockSpec((shape[1], tile), lambda i, *_: (0, i))


def split_columns(core, array, wide):
    tile = row_tile(array.shape, LONG)
    return call(
        partial(split_kernel, wide=wide),
        (array.shape[0] // LONG,),
        [tile],
        [tile],
        [shaped(array.shape, array.dtype)],
        (array,),
        scalars=(core,),
    )[0]


def shares_kernel(expand, contract, e_low, c_low, high):
    part = e_low.shape[1]
    e_low[...] = expand[:, :part]
    c_low[...] = contract[:part, :].T
    high[0] = expand[:, part:]
    high[1] = contract[part:, :].T


def shares(expand, contract, after=()):
    wide, unit = expand.shape
    half = (wide, unit // 2)
    return call(
        shares_kernel,
        (1,),
        [whole(expand.shape), whole(contract.shape)],
        [whole(half)] * 2 + [whole((2,) + half)],
        [shaped(half, BF16)] * 2 + [shaped((2,) + half, BF16)],
        (expand, contract),
        after=after,
    )


def output_kernel(core, *refs, wide):
    *parts, bias, out = refs
    half = out.shape[1] // 2
    total = sum(part[...].astype(F32) for part in parts) + bias[...]
    if wide % LANES:
        out[...] = total
        return
    for place in range(half // wide):
        at = place * wide
        own, other = total[:, at : at + wide], total[:, half + at : half + at + wide]
        out[:, 2 * at : 2 * at + wide] = jnp.where(core[0] == 0, own, other)
        out[:, 2 * at + wide : 2 * at + 2 * wide] = jnp.where(core[0] == 0, other, own)


def output_rows(core, parts, bias, wide, after=()):
    tile = row_tile(parts[0].shape, LONG)
    return call(
        partial(output_kernel, wide=wide),
        (parts[0].shape[0] // LONG,),
        [tile] * len(parts) + [whole(bias.shape)],
        [tile],
        [shaped(parts[0].shape, F32)],
        tuple(parts) + (bias,),
        scalars=(core,),
        after=after,
    )[0]


def finish_feed_kernel(low, high, expand, contract):
    part = low.shape[2]
    for at, ref in ((0, low), (part, high)):
        expand[:, at : at + part] = ref[0].astype(F32)
        contract[at : at + part, :] = ref[1].astype(F32).T


def finish_feed(low, high, after=()):
    _, wide, part = low.shape
    return call(
        finish_feed_kernel,
        (1,),
        [whole(low.shape)] * 2,
        [whole((wide, 2 * part)), whole((2 * part, wide))],
        [shaped((wide, 2 * part), F32), shaped((2 * part, wide), F32)],
        (low, high),
        after=after,
    )


def finish_attention_kernel(blocks, attention, merge_out):
    attention[...] = blocks[:3].astype(F32)
    merge_out[...] = blocks[3].astype(F32).T


def finish_attention(blocks):
    _, wide, columns = blocks.shape
    return call(
        finish_attention_kernel,
        (1,),
        [whole(blocks.shape)],
        [whole((3, wide, columns)), whole((columns, wide))],
        [shaped((3, wide, columns), F32), shaped((columns, wide), F32)],
        (blocks,),
    )


def marks_kernel(rows, columns):
    columns[...] = rows[...].T


def marks_of(*rows):
    count = rows[0].shape[0]
    rows = jnp.stack(rows + (jnp.zeros((count,), jnp.int32),) * (8 - len(rows))).astype(F32)
    columns = call(
        marks_kernel, (1,), [whole(rows.shape)], [whole((count, 8))], [shaped((count, 8), F32)], (rows,)
    )[0]
    return rows, columns


def group_rows(marks, group, values):
    return jnp.where(marks[:, 0:1] == jnp.asarray(group, F32), values, jnp.zeros_like(values))


def embed_kernel(present, pix, band, sin_own, cos_own, sin_came, cos_came, bias, gain, shift, lo_own, lo_came, hi_own, hi_came, stream, normed, acc):
    tile = pl.program_id(0)
    half = acc.shape[1] // 2
    width = pix.shape[1]
    acc[...] = beside((sin_own, cos_own, sin_came, cos_came))
    for group in range(GROUPS):

        @pl.when(present[tile * GROUPS + group] > 0)
        def _():
            rows = group_rows(band[...], group, pix[...])
            at = pl.ds((group % 2) * width, width)
            own, came = (lo_own, lo_came) if group < 2 else (hi_own, hi_came)
            acc[:, :half] += dot(rows, merged(own[:, :, at]), NT)
            acc[:, half:] += dot(rows, merged(came[:, :, at]), NT)

    total = acc[...]
    for group in range(GROUPS):
        total = total + jnp.where(band[:, 0:1] == float(group), bias[group : group + 1, :], 0.0)
    stream[...] = total
    normed[...] = (normalize(total)[0] * gain[...] + shift[...]).astype(BF16)


def embed(present, pixels, band, table, bias, gain, shift, patches, after=()):
    rows, model = pixels.shape[0], gain.shape[1]
    args = (pixels, band) + table + (bias, gain, shift) + patches
    specs = [row_tile(a.shape) for a in args[:6]] + [whole(a.shape) for a in args[6:]]
    return call(
        embed_kernel,
        (rows // TILE,),
        specs,
        [row_tile((rows, model))] * 2,
        [shaped((rows, model), F32), shaped((rows, model), BF16)],
        args,
        scratch=[pltpu.VMEM((TILE, model), F32)],
        flops=4 * rows * pixels.shape[1] * model,
        scalars=(present,),
        after=after,
    )


def project_kernel(x, bias, *refs):
    half = x.shape[1] // 2
    count = (len(refs) - 3) // 2
    weights, outs = refs[: 2 * count], refs[2 * count :]
    for mat, out in enumerate(outs):
        total = dot(x[:, :half], qkv_joined(weights[:count], mat)) + dot(x[:, half:], qkv_joined(weights[count:], mat))
        if mat != 1:
            total = total + bias[mat // 2 : mat // 2 + 1, :]
        out[...] = total.astype(BF16)


def project(x, own, came, bias, after=()):
    rows, model = x.shape
    width = bias.shape[1]
    weights = tuple(own) + tuple(came)
    return call(
        project_kernel,
        (rows // LONG,),
        [row_tile(x.shape, LONG), whole(bias.shape)] + [whole(w.shape) for w in weights],
        [row_tile((rows, width), LONG)] * 3,
        [shaped((rows, width), BF16)] * 3,
        (x, bias) + weights,
        flops=6 * rows * model * width,
        after=after,
    )


def head_mask(shape, head):
    lane = lax.broadcasted_iota(jnp.int32, shape, 1)
    return (lane < HEAD_DIM) if head == 0 else (lane >= HEAD_DIM)


def only_head(values, head):
    return jnp.where(head_mask(values.shape, head), values, jnp.zeros_like(values))


def attend_kernel(q_ref, k_ref, v_ref, seg_col_ref, seg_row_ref, out_ref, log_ref, bias_ref, *, base):
    pair = base + pl.program_id(0)
    rows = q_ref.shape[0]

    @pl.when(pl.program_id(0) == 0)
    def _():
        bias_ref[...] = jnp.where(seg_col_ref[:, 1:2] == seg_row_ref[1:2, :], 0.0, -1e30).astype(F32)
        log_ref[...] = jnp.zeros_like(log_ref)

    keys = k_ref[...]
    value_of = [only_head(v_ref[...], head) for head in range(2)]
    for start in range(0, rows, TILE):
        at = pl.ds(start, TILE)
        query = q_ref[at, :] * jnp.asarray(HEAD_DIM ** (-0.5), BF16)
        lane = lax.broadcasted_iota(jnp.int32, (TILE, LANES), 1)
        logs = log_ref[at, :]
        total = jnp.zeros((TILE, LANES), F32)
        for head in range(2):
            scores = dot(only_head(query, head), keys, NT) + bias_ref[at, :]
            top = jnp.max(scores, axis=1, keepdims=True)
            shifted = jnp.exp(scores - top)
            mass = jnp.sum(shifted, axis=1, keepdims=True)
            total = total + dot(shifted.astype(BF16), value_of[head]) * (1.0 / mass)
            logs = jnp.where(lane == 2 * pair + head, top + jnp.log(mass), logs)
        out_ref[at, :] = total.astype(BF16)
        log_ref[at, :] = logs


def attend(query, key, value, seg, base, skip, pairs, after=()):
    rows = query.shape[0]
    width = pairs * LANES
    block = pl.BlockSpec((rows, LANES), lambda i: (0, skip + i))
    return call(
        partial(attend_kernel, base=base + skip),
        (pairs,),
        [block, block, block, whole((rows, 8)), whole((8, rows))],
        [pl.BlockSpec((rows, LANES), lambda i: (0, i)), whole((rows, LANES))],
        [shaped((rows, width), BF16), shaped((rows, LANES), F32)],
        (query, key, value) + seg,
        scratch=[pltpu.VMEM((rows, rows), F32)],
        flops=16 * rows * rows * width,
        exps=rows * rows * width // HEAD_DIM,
        after=after,
    )


def attend_back_kernel(
    q_ref, k_ref, v_ref, g_ref, seg_col_ref, seg_row_ref, log_ref, delta_ref, dq_ref, dk_ref, dv_ref, sum_ref, bias_ref, acc_ref, *, base
):
    pair = base + pl.program_id(0)
    rows = q_ref.shape[0]

    @pl.when(pl.program_id(0) == 0)
    def _():
        bias_ref[...] = jnp.where(seg_col_ref[:, 1:2] == seg_row_ref[1:2, :], 0.0, -1e30).astype(F32)

    query = q_ref[...] * jnp.asarray(HEAD_DIM ** (-0.5), BF16)
    grads = g_ref[...]
    query_of = [only_head(query, head) for head in range(2)]
    grads_of = [only_head(grads, head) for head in range(2)]
    acc_ref[...] = jnp.zeros_like(acc_ref)
    value_sum = jnp.zeros((1, LANES), F32)
    for start in range(0, rows, TILE):
        at = pl.ds(start, TILE)
        keys = k_ref[at, :]
        values = v_ref[at, :]
        grad_key = jnp.zeros((TILE, LANES), F32)
        grad_value = jnp.zeros((TILE, LANES), F32)
        for head in range(2):
            key_h = only_head(keys, head)
            log_row = log_ref[pl.ds(2 * pair + head, 1), :]
            delta_row = delta_ref[pl.ds(2 * pair + head, 1), :]
            scores = dot(key_h, query, NT) + bias_ref[at, :]
            probs = jnp.exp(scores - log_row)
            grad_value = grad_value + dot(probs.astype(BF16), grads_of[head])
            grad_probs = dot(only_head(values, head), grads, NT)
            grad_scores = (probs * (grad_probs - delta_row)).astype(BF16)
            grad_key = grad_key + dot(grad_scores, query_of[head])
            acc_ref[...] += dot(key_h, grad_scores, TN)
        grad_value = grad_value.astype(BF16)
        dk_ref[at, :] = grad_key.astype(BF16)
        dv_ref[at, :] = grad_value
        value_sum = value_sum + jnp.sum(grad_value.astype(F32), axis=0, keepdims=True)
    grad_query = (acc_ref[...].T * HEAD_DIM ** (-0.5)).astype(BF16)
    dq_ref[...] = grad_query
    sum_ref[0:1, :] = jnp.sum(grad_query.astype(F32), axis=0, keepdims=True)
    sum_ref[1:2, :] = value_sum


def attend_back(query, key, value, grads, seg, log_rows, delta_rows, base, pairs, after=()):
    rows = query.shape[0]
    width = pairs * LANES
    taken = pl.BlockSpec((rows, LANES), lambda i: (0, base + i))
    given = pl.BlockSpec((rows, LANES), lambda i: (0, i))
    return call(
        partial(attend_back_kernel, base=base),
        (pairs,),
        [given] * 3 + [taken, whole((rows, 8)), whole((8, rows)), whole(log_rows.shape), whole(delta_rows.shape)],
        [given] * 3 + [pl.BlockSpec((2, LANES), lambda i: (0, i))],
        [shaped((rows, width), BF16)] * 3 + [shaped((2, width), F32)],
        (query, key, value, grads) + seg + (log_rows, delta_rows),
        scratch=[pltpu.VMEM((rows, rows), F32), pltpu.VMEM((LANES, rows), F32)],
        flops=40 * rows * rows * width,
        exps=rows * rows * width // HEAD_DIM,
        after=after,
    )


def merge_kernel(*refs, count):
    attended = beside(refs[:count])
    logs = sum(ref[...] for ref in refs[count : 2 * count])
    stream, bias, gain, shift, own_low, own_high, came_low, came_high = refs[2 * count : 2 * count + 8]
    stream_one, normed, log_rows = refs[2 * count + 8 :]
    log_rows[...] = logs.T
    half = stream.shape[1] // 2
    stream_one[:, :half] = stream[:, :half] + dot(attended, joined((own_low, own_high), 0, 1), NT)
    stream_one[:, half:] = stream[:, half:] + dot(attended, joined((came_low, came_high), 0, 1), NT)
    total = stream_one[...] + bias[...]
    stream_one[...] = total
    normed[...] = (normalize(total)[0] * gain[...] + shift[...]).astype(BF16)


def first_two(array):
    return pl.BlockSpec(array.shape[:2] + (2,) + array.shape[3:], lambda *_: (0,) * array.ndim)


def merge(attended, logs, stream, bias, gain, shift, weights, after=()):
    rows, model = stream.shape
    return call(
        partial(merge_kernel, count=len(attended)),
        (rows // LONG,),
        [row_tile(a.shape, LONG) for a in tuple(attended) + tuple(logs)]
        + [row_tile(stream.shape, LONG)]
        + [whole((1, model))] * 3
        + [first_two(a) for a in weights],
        [row_tile((rows, model), LONG)] * 2 + [turned_tile((rows, LANES), LONG)],
        [shaped((rows, model), F32), shaped((rows, model), BF16), shaped((LANES, rows), F32)],
        tuple(attended) + tuple(logs) + (stream, bias, gain, shift) + weights,
        flops=2 * rows * model * model,
        after=after,
    )


def gelu_parts(hidden):
    t = 1.0 / (1.0 + (0.3275911 * math.sqrt(0.5)) * jnp.abs(hidden))
    bell = jnp.exp(-0.5 * hidden * hidden)
    poly = t * (
        0.5 * 0.254829592
        + t * (-0.5 * 0.284496736 + t * (0.5 * 1.421413741 + t * (-0.5 * 1.453152027 + t * (0.5 * 1.061405429))))
    )
    tail = poly * bell
    below = jnp.where(hidden >= 0, 1.0 - tail, tail)
    return hidden * below, below + (hidden * (1.0 / math.sqrt(2.0 * math.pi))) * bell


def feed_kernel(x_ref, g_ref, e_own, e_other, c_own, c_other, b_ref, y_ref, d_ref, *refs):
    e_keep, e_send, c_keep, c_send, db_ref, a_ref, h_ref, y_sum, d_sum = refs
    step = pl.program_id(0)
    half = x_ref.shape[1] // 2

    @pl.when(step == 0)
    def _():
        y_sum[...] = jnp.zeros_like(y_sum)
        d_sum[...] = jnp.zeros_like(d_sum)

    expand = jnp.concatenate([merged(e_own[...]), merged(e_other[...])], axis=0)
    contract = jnp.concatenate([merged(c_own[...]), merged(c_other[...])], axis=0)
    hidden = dot(x_ref[...], expand) + b_ref[0]
    grad_active = dot(g_ref[...], contract)
    active, slope = gelu_parts(hidden)
    a_ref[...] = active.astype(BF16)
    grad_hidden = (grad_active * slope).astype(BF16)
    h_ref[...] = grad_hidden
    db_ref[0] = jnp.sum(grad_hidden.astype(F32), axis=0, keepdims=True)
    y_sum[...] += dot(a_ref[...], contract, NT)
    d_sum[...] += dot(h_ref[...], expand, NT)
    for side, (e_ref, c_ref) in enumerate(((e_keep, c_keep), (e_send, c_send))):
        cols = pl.ds(side * half, half)
        shape = e_ref.shape[:1] + e_ref.shape[2:]
        e_ref[:, 0] = dot(x_ref[:, cols], h_ref[...], TN).astype(BF16).reshape(shape)
        c_ref[:, 0] = dot(g_ref[:, cols], a_ref[...], TN).astype(BF16).reshape(shape)

    @pl.when(step == pl.num_programs(0) - 1)
    def _():
        y_ref[...] = y_sum[...].astype(BF16)
        d_ref[...] = d_sum[...].astype(BF16)


def feed(core, rows_two, top, weights, bias, base, steps, filled=(), after=()):
    rows, model = rows_two.shape
    blocks, _, part = bias.shape
    pairs, wide = weights[0].shape[0], weights[0].shape[-2]
    if len(weights) == 1:
        weights = weights * 4
        block = (pairs, 1, 1, 1, wide, part)
        place = lambda side, mat: lambda i, core: (0, core[0] if side == 0 else 1 - core[0], base + i, mat, 0, 0)
        specs = [pl.BlockSpec(block, place(side, mat)) for mat in range(2) for side in range(2)]
    else:
        specs = [pl.BlockSpec((pairs, 1, wide, part), lambda i, core: (0, base + i, 0, 0))] * 4
    grad = pl.BlockSpec((pairs, 1, wide, part), lambda i, core: (0, base + i, 0, 0))
    unit = pl.BlockSpec((1, 1, part), lambda i, core: (base + i, 0, 0))
    return call(
        lambda core, *refs: feed_kernel(*refs),
        (steps,),
        [whole((rows, model))] * 2 + specs + [unit],
        [whole((rows, model))] * 2 + [grad] * 4 + [unit],
        [shaped((rows, model), BF16)] * 2
        + [shaped((pairs, blocks, wide, part), BF16)] * 4
        + [shaped((blocks, 1, part), F32)],
        (rows_two, top) + tuple(weights) + (bias,),
        scratch=[pltpu.VMEM((rows, part), BF16)] * 2 + [pltpu.VMEM((rows, model), F32)] * 2,
        flops=12 * rows * model * part * steps,
        exps=rows * part * steps,
        scalars=(core,),
        after=after,
        filled=[(2 + i, array) for i, array in enumerate(filled)],
    )


def merge_back_kernel(*refs, count, parts):
    attended = beside(refs[:count])
    grad_two = sum(ref[...].astype(F32) for ref in refs[count : count + parts])
    refs = refs[count + parts :]
    top, stream_one, gain, own_low, own_high, came_low, came_high, heads = refs[:8]
    grad_stream, branch, grad_attended, delta, sums = refs[8:]
    half = top.shape[1] // 2
    normed, scale = normalize(stream_one[...])
    cotangent = top[...].astype(F32)
    total = cotangent + normalize_back(grad_two * gain[...], normed, scale)
    grad_stream[...] = total
    low = total.astype(BF16)
    branch[...] = low
    grads = dot(low[:, :half], joined((own_low, own_high), 0, 1)) + dot(low[:, half:], joined((came_low, came_high), 0, 1))
    grads = grads.astype(BF16)
    grad_attended[...] = grads
    both = grads.astype(F32) * attended.astype(F32)
    high = both.astype(BF16)
    delta[...] = dot(heads[...], high, NT) + dot(heads[...], (both - high.astype(F32)).astype(BF16), NT)

    @pl.when(pl.program_id(0) == 0)
    def _():
        sums[...] = jnp.zeros_like(sums)

    for row, part in enumerate((grad_two * normed, grad_two, total, cotangent)):
        sums[row : row + 1, :] += jnp.sum(part, axis=0, keepdims=True)


def merge_back(attended, grads, top, stream_one, gain, weights, heads, after=()):
    rows, model = stream_one.shape
    tile = row_tile((rows, model), LONG)
    return call(
        partial(merge_back_kernel, count=len(attended), parts=len(grads)),
        (rows // LONG,),
        [row_tile(a.shape, LONG) for a in attended]
        + [tile] * (len(grads) + 2)
        + [whole((1, model))]
        + [first_two(a) for a in weights]
        + [whole(heads.shape)],
        [tile] * 3
        + [pl.BlockSpec((heads.shape[0], LONG), lambda i: (0, i)), whole((8, model))],
        [
            shaped((rows, model), F32),
            shaped((rows, model), BF16),
            shaped((rows, model), BF16),
            shaped((heads.shape[0], rows), F32),
            shaped((8, model), F32),
        ],
        tuple(attended) + tuple(grads) + (top, stream_one, gain) + weights + (heads,),
        flops=2 * rows * model * model,
        after=after,
    )


def attention_grads_kernel(*refs, count):
    x, branch, xt, bt = refs[0], refs[1], refs[-2], refs[-1]
    xt[...] = x[...].T
    bt[...] = branch[...].T
    inputs = [beside(refs[2 + i * count : 2 + (i + 1) * count]) for i in range(3)]
    inputs.append(beside(refs[2 + 3 * count : -6]))
    outs = refs[-6:-2]
    half = xt.shape[0] // 2
    blocks, steps, _, wide, columns = outs[0].shape
    for place, right in enumerate(inputs):
        left = bt if place == 3 else xt
        for side in range(2):
            ref = outs[2 * (place // 2) + side]
            grad = dot(left[pl.ds(side * half, half), :], right).astype(BF16)
            for step in range(steps):
                part = grad[:, step * columns : (step + 1) * columns]
                ref[:, step, place % 2] = part.reshape(blocks, wide, columns)


def attention_grads(x, branch, query, key, value, attended, blocks, columns, after=()):
    rows, model = x.shape
    count = len(query)
    width = sum(a.shape[1] for a in query)
    shape = (blocks, width // columns, 2, model // (2 * blocks), columns)
    args = (x, branch) + tuple(query) + tuple(key) + tuple(value) + tuple(attended)
    return call(
        partial(attention_grads_kernel, count=count),
        (1,),
        [whole(a.shape) for a in args],
        [whole(shape)] * 4,
        [shaped(shape, BF16)] * 4,
        args,
        scratch=[pltpu.VMEM((model, rows), BF16)] * 2,
        flops=8 * rows * model * width,
        after=after,
    )


def project_back_kernel(*refs, count):
    grads = [beside(refs[i * count : (i + 1) * count]) for i in range(3)]
    rest = refs[3 * count :]
    grad_stream, stream, band, gain = rest[:4]
    weights = rest[4:-3]
    grad_embed, sums, acc = rest[-3:]
    half = stream.shape[1] // 2
    each = len(weights) // 2
    for side in range(2):
        held = weights[side * each : (side + 1) * each]
        acc[:, side * half : (side + 1) * half] = sum(
            dot(grad, qkv_joined(held, mat), NT) for mat, grad in enumerate(grads)
        )
    grad_one = acc[...]
    normed, scale = normalize(stream[...])
    total = grad_stream[...] + normalize_back(grad_one * gain[...], normed, scale)
    grad_embed[...] = total.astype(BF16)

    @pl.when(pl.program_id(0) == 0)
    def _():
        sums[...] = jnp.zeros_like(sums)

    parts = [group_rows(band[...], group, total) for group in range(GROUPS)] + [grad_one * normed, grad_one]
    for row, part in enumerate(parts):
        sums[row : row + 1, :] += jnp.sum(part, axis=0, keepdims=True)


def project_back(query, key, value, grad_stream, stream, band, gain, weights, after=()):
    rows, model = stream.shape
    tile = row_tile((rows, model))
    parts = tuple(query) + tuple(key) + tuple(value)
    return call(
        partial(project_back_kernel, count=len(query)),
        (rows // TILE,),
        [row_tile(a.shape) for a in parts]
        + [tile] * 2
        + [row_tile(band.shape), whole((1, model))]
        + [whole(a.shape) for a in weights],
        [tile, whole((8, model))],
        [shaped((rows, model), BF16), shaped((8, model), F32)],
        parts + (grad_stream, stream, band, gain) + weights,
        scratch=[pltpu.VMEM((TILE, model), F32)],
        flops=6 * rows * model * model,
        after=after,
    )


def patch_grads_kernel(present, grads, pix, band, lo_keep, lo_send, hi_keep, hi_send, acc):
    group = pl.program_id(0)
    half = grads.shape[1] // 2
    acc[...] = jnp.zeros_like(acc)
    for tile in range(pix.shape[0] // TILE):

        @pl.when(present[tile * GROUPS + group] > 0)
        def _():
            at = pl.ds(tile * TILE, TILE)
            acc[...] += dot(grads[at, :], group_rows(band[at, :], group, pix[at, :]), TN)

    for place, (keep, send) in enumerate(((lo_keep, lo_send), (hi_keep, hi_send))):

        @pl.when(group // 2 == place)
        def _():
            keep[...] = acc[:half, :].astype(BF16)
            send[...] = acc[half:, :].astype(BF16)


def patch_grads(present, grads, pixels, band, after=()):
    rows, model = grads.shape
    width = pixels.shape[1]
    count = GROUPS // 2
    low = pl.BlockSpec((model // 2, width), lambda i, present: (0, jnp.minimum(i, count - 1)))
    high = pl.BlockSpec((model // 2, width), lambda i, present: (0, jnp.maximum(i - count, 0)))
    return call(
        patch_grads_kernel,
        (GROUPS,),
        [whole(grads.shape), whole(pixels.shape), whole(band.shape)],
        [low, low, high, high],
        [shaped((model // 2, count * width), BF16)] * 4,
        (grads, pixels, band),
        scratch=[pltpu.VMEM((model, width), F32)],
        flops=4 * rows * width * model,
        scalars=(present,),
        after=after,
    )


def pixel_grads_kernel(present, grads, band, lo_own, lo_came, hi_own, hi_came, out):
    tile = pl.program_id(0)
    half = grads.shape[1] // 2
    width = out.shape[1]
    out[...] = jnp.zeros_like(out)
    for group in range(GROUPS):

        @pl.when(present[tile * GROUPS + group] > 0)
        def _():
            at = pl.ds((group % 2) * width, width)
            own, came = (lo_own, lo_came) if group < 2 else (hi_own, hi_came)
            spread = dot(grads[:, :half], merged(own[:, :, at])) + dot(grads[:, half:], merged(came[:, :, at]))
            out[...] = jnp.where(band[:, 0:1] == float(group), spread, out[...])


def pixel_grads(present, grads, band, patches, width, after=()):
    rows, model = grads.shape
    return call(
        pixel_grads_kernel,
        (rows // TILE,),
        [row_tile(grads.shape), row_tile(band.shape)] + [whole(a.shape) for a in patches],
        [row_tile((rows, width))],
        [shaped((rows, width), F32)],
        (grads, band) + patches,
        flops=4 * rows * width * model,
        scalars=(present,),
        after=after,
    )[0]


def make_body(fsdp, tensor):
    pairs = fsdp // 2
    t_bits = list(range(tensor.bit_length() - 1))
    f_bits = list(range(1, fsdp.bit_length() - 1))
    up, down = f_bits, f_bits[::-1]

    def swap(array, axis, bit):
        size = fsdp if axis == "fsdp" else tensor
        return lax.ppermute(array, axis, [(i, i ^ (1 << bit)) for i in range(size)])

    def body(
        pixels,
        segment,
        band_group,
        scaled_position,
        patch_weight,
        patch_bias,
        norm_gains,
        vector_biases,
        attention_weight,
        query_value_bias,
        merge_weight,
        expand_weight,
        expand_bias,
        contract_weight,
        cotangent,
    ):
        index = {"fsdp": lax.axis_index("fsdp"), "tensor": lax.axis_index("tensor")}
        core = index["fsdp"] & 1
        rows, pix = pixels.shape
        model = cotangent.shape[1]
        thin = patch_bias.shape[1]
        wide = model // fsdp
        unit = expand_weight.shape[1]
        half_unit = unit // 2
        segment = lax.dynamic_slice_in_dim(segment, index["tensor"] * rows, rows)

        def wider(array, came, axis, bit):
            dim = 0 if axis == "tensor" else len(f_bits) - bit
            mine = ((index[axis] >> bit) & 1) == 1
            return jnp.where(
                mine, jnp.concatenate([came, array], axis=dim), jnp.concatenate([array, came], axis=dim)
            )

        def shifts(make):
            count = tensor
            return [
                lax.ppermute(make(d), "tensor", [(i, (i + d) % count) for i in range(count)]) for d in range(1, count)
            ]

        def in_order(array, came):
            parts = jnp.stack([array] + came)[::-1]
            return lax.dynamic_slice_in_dim(jnp.concatenate([parts, parts]), tensor - 1 - index["tensor"], tensor)

        def open_f(array):
            return array.reshape((1,) * len(f_bits) + array.shape)

        def close_f(array):
            return array.reshape((pairs,) + array.shape[len(f_bits) :])

        def other_core(array):
            return swap(array, "fsdp", 0)

        class Pair:
            def __init__(self, one, two):
                self.held = [open_f(one), open_f(two)]
                self.todo = list(zip(up, down))

            def send(self):
                self.bits = self.todo.pop(0)
                return [swap(a, "fsdp", bit) for a, bit in zip(self.held, self.bits)]

            def take(self, came):
                self.held = [wider(a, c, "fsdp", bit) for a, c, bit in zip(self.held, came, self.bits)]

            def drain(self):
                while self.todo:
                    self.take(self.send())

            def closed(self):
                return [close_f(a) for a in self.held]

        def half_sum(keep, came, at, bit):
            dim = len(f_bits) - bit
            take = lambda array: lax.dynamic_slice_in_dim(array, at, 1, axis=dim)
            return (take(keep).astype(F32) + take(came).astype(F32)).astype(keep.dtype)

        class Sum:
            def __init__(self, keep, send, bits):
                self.keep, self.todo = unfold(keep), list(bits)
                self.came = unfold(swap(send, "fsdp", 0))

            def step(self):
                bit = self.todo.pop(0)
                mine = (index["fsdp"] >> bit) & 1
                self.sent = half_sum(self.keep, self.came, 1 - mine, bit)
                self.keep = half_sum(self.keep, self.came, mine, bit)
                self.came = swap(self.sent, "fsdp", bit)
                return self.sent

            def total(self):
                while self.todo:
                    self.step()
                return last_sum(self.keep, self.came)

        def unfold(array):
            return array.reshape((2,) * len(f_bits) + array.shape[1:])

        def last_sum(keep, came):
            rest = keep.shape[len(f_bits) :]
            return (keep.astype(F32) + came.astype(F32)).astype(keep.dtype).reshape(rest)

        def over_tensor(blocks):
            return lax.psum_scatter(blocks, "tensor", scatter_dimension=0, tiled=False)

        def to_split(array):
            parts = array.reshape(array.shape[0], pairs, 2, wide)
            even, odd = (parts[:, :, i].reshape(array.shape[0], -1) for i in range(2))
            return jnp.where(core == 0, jnp.concatenate([even, odd], axis=1), jnp.concatenate([odd, even], axis=1))

        def from_split(array):
            parts = array.reshape(array.shape[0], 2, pairs, wide)
            mine, other = parts[:, 0], parts[:, 1]
            parts = jnp.where(core == 0, jnp.stack([mine, other], axis=2), jnp.stack([other, mine], axis=2))
            return parts.reshape(array.shape)

        core_at = core[None].astype(jnp.int32)
        aligned = wide % LANES == 0

        sync = lax.optimization_barrier
        n_vec = GROUPS + 2 + 4
        cut = n_vec * thin
        columns = (GROUPS // 2) * pix
        rest_up, rest_down = up[1:], down[1:]

        small = jnp.concatenate(
            [patch_bias, norm_gains, vector_biases, query_value_bias, expand_bias.reshape(-1, thin)], axis=0
        )
        extra = small.shape[0]
        small = jnp.pad(lax.optimization_barrier(small).T, ((0, 0), (0, LANES - extra)))
        patch = jnp.concatenate([patch_weight.reshape(-1, thin).T, small], axis=1)
        attention = jnp.concatenate([attention_weight, merge_weight.T[None]], axis=0)[None]
        t_first, t_rest = t_bits[:1], t_bits[1:]

        def over_t(array, came, bits):
            for i, bit in enumerate(bits):
                array = wider(array, came if i == 0 else swap(array, "tensor", bit), "tensor", bit)
            return array

        def start_t(bits, *arrays):
            return [swap(a, "tensor", bits[0]) for a in arrays]

        def go(*pairs):
            return [p.send() if p.todo else None for p in pairs]

        def done(came, *pairs):
            for c, p in zip(came, pairs):
                if c is not None:
                    p.take(c)

        def both_cores(pair):
            held = pair.closed()
            return held, [other_core(a) for a in held]

        present = jnp.any(band_group.reshape(-1, TILE, 1) == jnp.arange(GROUPS), axis=1).astype(jnp.int32).reshape(-1)
        came = shifts(lambda d: patch)
        e_one, c_one, feed_high = shares(expand_weight, contract_weight)
        e_one, c_one = e_one[None], c_one[None]
        mark_rows, band = marks_of(band_group, segment)
        seg = (band, mark_rows)
        came, patch, attention, cotangent, e_one, band, present, seg = sync(
            (came, patch, attention, cotangent, e_one, band, present, seg)
        )
        patch = in_order(patch, came).reshape(tensor * thin, -1)
        patch = Pair(patch[:, :columns], patch[:, columns:])
        came = go(patch)
        came_t = start_t(t_first, attention)
        if aligned:
            top = split_columns(core_at, cotangent, wide)
        else:
            top = to_split(cotangent)
        came, came_t, top, e_one, c_one, scaled_position = sync((came, came_t, top, e_one, c_one, scaled_position))
        done(came, patch)
        attention = over_t(attention, came_t[0], t_first)
        came = go(patch)
        came_t = start_t(t_rest, attention) + start_t(t_first, e_one, c_one)
        half_width = model // 2
        column = jnp.arange(model)
        place = column % half_width
        natural = (2 * (place // wide) + (core ^ (column // half_width))) * wide + place % wide
        rates = jnp.exp((natural % half_width).astype(F32) * (-math.log(10000.0) / half_width))
        angles = scaled_position.astype(F32)[:, None] * rates[None, :]
        quarter = model // 4
        table = tuple(
            f(angles[:, i * quarter : (i + 1) * quarter]) for i, f in enumerate((jnp.sin, jnp.cos, jnp.sin, jnp.cos))
        )
        hidden = jnp.arange(model)
        owner, block = hidden // thin % fsdp, hidden // (thin * fsdp)
        source = ((((owner & 1) ^ core) * pairs + owner // 2) * tensor + block) * thin + hidden % thin
        to_hidden = (hidden[:, None] == source[None, :]).astype(BF16)
        came, came_t, table, to_hidden = sync((came, came_t, table, to_hidden))
        done(came, patch)
        patch.drain()
        attention = over_t(attention, came_t[0], t_rest)
        e_one, c_one = (over_t(w, c, t_first) for w, c in zip((e_one, c_one), came_t[1:]))
        quarter, half_t = tensor // 4, tensor // 2
        outward = [
            attention[i * half_t : (i + 1) * half_t, 3].reshape(quarter, 2, wide, -1) for i in range(2)
        ]
        qkv = [attention[i * quarter : (i + 1) * quarter, :3] for i in range(4)]
        qkv_one = Pair(*qkv[:2])
        qkv_two = Pair(*(jnp.concatenate(two, axis=1) for two in zip(outward, qkv[2:])))
        patch = both_cores(patch)
        came = go(qkv_one)
        patch, came, e_one, c_one, band = sync((patch, came, e_one, c_one, band))
        patches = (patch[0][0], patch[1][0], patch[0][1], patch[1][1])
        done(came, qkv_one)
        came, came_t = go(qkv_one), start_t(t_rest, e_one)
        small = [held[0] for held in (patch[0][1:], patch[1][1:])]
        small = jnp.stack([held[:, :, columns : columns + extra] for held in small]).astype(F32)
        vectors = small.reshape(model, extra).T
        patch_bias_rows = vectors[:GROUPS]
        gains = [vectors[GROUPS + i : GROUPS + i + 1] for i in range(2)]
        biases = [vectors[GROUPS + 2 + i : GROUPS + 3 + i] for i in range(4)]
        by_hidden = dot(vectors[n_vec:].astype(BF16), to_hidden)
        qv_rows = by_hidden[:2]

        stream_zero, input_one = embed(
            present, pixels, band, table, patch_bias_rows, gains[0], biases[0], patches
        )
        came, came_t, input_one, qkv_two.held = sync((came, came_t, input_one, qkv_two.held))
        done(came, qkv_one)
        qkv_one.drain()
        e_one = over_t(e_one, came_t[0], t_rest)
        one, came = both_cores(qkv_one), go(qkv_two)
        one, came, input_one, c_one = sync((one, came, input_one, c_one))
        done(came, qkv_two)
        came, came_t = go(qkv_two), start_t(t_rest, c_one)
        heads_width = model // 2
        each = heads_width // LANES
        first = project(input_one, *one, qv_rows[:, :heads_width])
        attended, logs = [None] * 3, [None] * 3
        attended[0], logs[0] = attend(*first, seg, 0, 0, each // 2)
        came, came_t, attended[0], feed_high = sync((came, came_t, attended[0], feed_high))
        feed_one = Pair(e_one, over_t(c_one, came_t[0], t_rest))
        feed_high = lax.all_gather(feed_high, ("fsdp", "tensor"), axis=0, tiled=False)
        feed_high = feed_high.reshape(pairs, 2, tensor, 2, wide, half_unit)
        done(came, qkv_two)
        qkv_two.drain()
        two, came = both_cores(qkv_two), go(feed_one)
        attended[1], logs[1] = attend(*first, seg, 0, each // 2, each // 2, after=(attended[0],))
        two, came, attended[1], input_one = sync((two, came, attended[1], input_one))
        done(came, feed_one)
        came = go(feed_one)
        last = project(input_one, *two, qv_rows[:, heads_width:])
        attended[2], logs[2] = attend(*last, seg, each, 0, each)
        came, attended[2] = sync((came, attended[2]))
        done(came, feed_one)
        feed_one.drain()
        feed_one = both_cores(feed_one)
        outward = tuple(two[0] + two[1])
        stream_one, input_two, log_rows = merge(
            attended, logs, stream_zero, biases[1], gains[1], biases[2], outward
        )
        feed_one, input_two, by_hidden = sync((feed_one, input_two, by_hidden))
        unit_bias = by_hidden[2:].reshape(-1, tensor, fsdp, thin).transpose(1, 2, 0, 3).reshape(tensor, 2, 1, half_unit)

        rows_two = (input_two, top)
        def meet(sums, *arrays):
            waited = sync(([t.came for t in sums],) + arrays)
            for t, came in zip(sums, waited[0]):
                t.came = came
            return waited[1] if len(arrays) == 1 else waited[1:]

        def advance(*sums):
            return [t.step() if t.todo else t.came for t in sums]

        def drain(*sums):
            for t in sums:
                while t.todo:
                    t.step()

        weights = tuple(a for pair in zip(*feed_one) for a in pair)
        y_low, d_low, *grads_low, units_low = feed(core_at, *rows_two, weights, unit_bias[:, 0], 0, tensor)
        low = [Sum(grads_low[0], grads_low[1], down), Sum(grads_low[2], grads_low[3], up)]
        share = max(1, tensor // 4)
        y_mid, d_mid, *grads_mid, units_mid = feed(
            core_at, *rows_two, (feed_high,), unit_bias[:, 1], 0, share, after=(y_low,)
        )
        y_mid = meet(low, y_mid)
        y_high, d_high, *grads_high, units_high = feed(
            core_at,
            *rows_two,
            (feed_high,),
            unit_bias[:, 1],
            share,
            tensor - share,
            filled=grads_mid + [units_mid],
            after=[y_mid] + advance(*low),
        )
        y_high, *grads_high = meet(low, y_high, *grads_high)
        high = [Sum(grads_high[0], grads_high[1], down), Sum(grads_high[2], grads_high[3], up)]
        unit_grads = [units_low, units_high]
        outs = [y_low, y_mid, y_high]

        heads = model // HEAD_DIM
        head_rows = (jnp.arange(heads)[:, None] == jnp.arange(model)[None, :] // HEAD_DIM).astype(BF16)
        grad_stream_one, grad_branch, grad_attended, delta, sums_two = merge_back(
            attended, [d_low, d_mid, d_high], top, stream_one, gains[1], outward, head_rows, after=advance(*low)
        )
        grad_attended = meet(low + high, grad_attended)
        back = lambda i, after: attend_back(
            *(first, last)[i], grad_attended, seg, log_rows, delta, i * each, each, after=after
        )

        def grads_of(part, which, after):
            return attention_grads(
                input_one, grad_branch, *([p] for p in part[:3]), attended[2 * which : 2 + which], pairs, model // tensor, after=after
            )

        first_part = back(0, advance(*high))
        drain(*low)
        low_blocks = jnp.stack([t.total() for t in low], axis=1)
        feed_grads_low = over_tensor(low_blocks)
        left = meet(high, grads_of(first_part, 0, (low_blocks,)))
        waits = advance(*high)
        left_qk, left_vm = Sum(left[0], left[1], down), Sum(left[2], left[3], up)
        second_part = back(1, waits)
        second_part = meet(high + [left_qk, left_vm], second_part)
        drain(*high)
        feed_blocks = jnp.stack([t.total() for t in high], axis=1)
        feed_grads_high = over_tensor(feed_blocks)
        right = grads_of(second_part, 1, advance(left_qk, left_vm) + [feed_blocks])
        right = meet((left_qk, left_vm), right)
        waits = advance(left_qk, left_vm)
        right_qk, right_vm = Sum(right[0], right[1], down), Sum(right[2], right[3], up)
        parts = (first_part, second_part)
        grad_query, grad_key, grad_value = ([p[i] for p in parts] for i in range(3))
        grad_qv = jnp.concatenate([p[3] for p in parts], axis=1)
        grad_embed, sums_one = project_back(
            grad_query, grad_key, grad_value, grad_stream_one, stream_zero, band, gains[0], tuple(one[0] + two[0] + one[1] + two[1]), after=waits
        )
        grad_embed = meet((left_qk, left_vm, right_qk, right_vm), grad_embed)

        waits = advance(right_qk, right_vm)
        shape = (pairs, tensor, thin, columns)
        patch_kept = meet((right_qk, right_vm), patch_grads(present, grad_embed, pixels, band, after=waits))
        lo = Sum(*(a.reshape(shape) for a in patch_kept[:2]), up)
        hi = Sum(*(a.reshape(shape) for a in patch_kept[2:]), down)

        vector_grads = from_split(
            jnp.concatenate(
                [sums_one[:GROUPS], sums_one[GROUPS : GROUPS + 1], sums_two[0:1], sums_one[GROUPS + 1 : GROUPS + 2]]
                + [sums_two[2:3], sums_two[1:2], sums_two[3:4]],
                axis=0,
            )
        )
        vector_grads = vector_grads.reshape(n_vec, fsdp * tensor, thin).transpose(1, 0, 2).reshape(fsdp, tensor, cut)
        hidden_grads = jnp.concatenate(
            [
                grad_qv.reshape(2, tensor, fsdp, thin).transpose(2, 1, 0, 3).reshape(fsdp, tensor, 2 * thin),
                jnp.stack(unit_grads, axis=1).reshape(tensor, fsdp, unit // fsdp).transpose(1, 0, 2),
            ],
            axis=2,
        )
        small_grads = jnp.concatenate([vector_grads, hidden_grads], axis=2).reshape(fsdp * tensor, -1)
        small_grads = small_grads.reshape((2,) * (len(f_bits) + 1 + len(t_bits)) + (-1,))

        def small_halves(array, axis, bit):
            dim = (len(f_bits) - bit) if axis == "fsdp" else len(f_bits) + len(t_bits) - bit
            mine = (index[axis] >> bit) & 1
            take = lambda at: lax.dynamic_slice_in_dim(array, at, 1, axis=dim)
            return take(mine), swap(take(1 - mine), axis, bit)

        def small_steps(kept, came, axis, bits):
            for bit in bits:
                kept, came = small_halves(kept + came, axis, bit)
            return kept, came

        small_kept, small_came = small_halves(small_grads, "fsdp", 0)
        waits = advance(right_qk, right_vm)
        small_came = meet((lo, hi), small_came)
        waits += advance(lo, hi)
        small_kept, small_came = small_steps(small_kept, small_came, "tensor", t_bits)
        block_output = output_rows(core_at, [stream_one] + outs, biases[3], wide, after=waits)
        if not aligned:
            block_output = from_split(block_output)
        pixel_grad = pixel_grads(present, grad_embed, band, patches, pix, after=[block_output])
        small_came, pixel_grad = meet((lo, hi, left_qk, left_vm, right_qk, right_vm), small_came, pixel_grad)
        advance(lo, hi)
        small_kept, small_came = small_steps(small_kept, small_came, "fsdp", f_bits)
        drain(lo, hi, left_qk, left_vm, right_qk, right_vm)
        grad_attention = over_tensor(
            jnp.concatenate(
                [
                    jnp.concatenate([left_qk.total(), left_vm.total()], axis=1),
                    jnp.concatenate([right_qk.total(), right_vm.total()], axis=1),
                ],
                axis=0,
            )
        )
        small_came = meet((lo, hi), small_came)
        blocks = jnp.concatenate([lo.total(), hi.total()], axis=2)
        expand_out, contract_out = finish_feed(feed_grads_low, feed_grads_high, after=[blocks])
        own = lambda d: lax.dynamic_index_in_dim(blocks, (index["tensor"] + d) % tensor, 0, keepdims=False)
        came = shifts(own)
        small_grads = (small_kept + small_came).reshape(1, -1)
        grad_patch = sum([c.astype(F32) for c in came], own(0).astype(F32)).T.reshape(GROUPS, pix, thin)
        attention_out, merge_grad = finish_attention(grad_attention)
        small_grads = small_grads[0]
        mine = small_grads[:cut].reshape(n_vec, thin)
        return (
            block_output,
            pixel_grad,
            grad_patch,
            mine[:GROUPS],
            mine[GROUPS : GROUPS + 2],
            mine[GROUPS + 2 :],
            attention_out,
            small_grads[cut : cut + 2 * thin].reshape(2, thin),
            merge_grad,
            expand_out,
            small_grads[cut + 2 * thin :],
            contract_out,
        )

    return body


def solution(mesh):
    every = ("fsdp", "tensor")
    args = (
        P(every, None),
        P("fsdp"),
        P(every),
        P(every),
        P(None, None, every),
        P(None, every),
        P(None, every),
        P(None, every),
        P(None, "fsdp", "tensor"),
        P(None, ("tensor", "fsdp")),
        P("tensor", "fsdp"),
        P("fsdp", "tensor"),
        P(("tensor", "fsdp")),
        P("tensor", "fsdp"),
        P(every, None),
    )
    outs = (P(every, None), P(every, None)) + args[4:14]
    body = make_body(mesh.shape["fsdp"], mesh.shape["tensor"])
    return jax.shard_map(body, mesh=mesh, in_specs=args, out_specs=outs, check_vma=False)
```
